32 devices in a mesh: parts: 2 (over y), blk: 4 (over z), op: 4 (over x, core).
Axes of the slice: x: 2, y: 2, z: 4, core: 2. Of those that a mesh axis runs over, the one named last changes fastest.
Arguments:
- psi: bfloat16 [16, 8, 128, 128], P(('parts', 'blk')), parts along dimension 0, may hold values from -6 to 6
- left_ops: bfloat16 [32, 8, 128, 128], P(('parts', 'op'), 'blk'), parts along dimension 0, may hold values from -0.5 to 0.5
- right_ops: bfloat16 [32, 8, 128, 128], P(('parts', 'op'), 'blk'), parts along dimension 0, may hold values from -0.1875 to 0.1875
- term_blocks: int32 [32, 8], P(('parts', 'op')), parts along dimension 0, may hold values from 0 to 1, as said below
- left_sizes: int32 [16], P('parts'), parts along dimension 0, may hold values from 1 to 128
- right_sizes: int32 [16], P('parts'), parts along dimension 0, may hold values from 1 to 128
Outputs:
- sigma: bfloat16 [16, 8, 128, 128], P(('parts', 'blk'), 'op'), parts along dimension 0
The draws below stay inside these ranges and needn't reach their ends.
There are 2 independent parts, one for each index of `parts`. The reference program is written for one: setup_inputs(seed, part) draws one part's arguments, and reference() takes and returns one part's arrays. A program takes and returns all parts, laid end to end along the dimension named above; each array names one. Nothing has to cross between parts.
Inputs may be any that keep to these rules, and one draw needn't show every extreme that they name: `term_blocks`: terms come in consecutive groups of 4; within every group, exactly 2 terms act on each left sector.
All inputs are finite; a program needn't handle non-finite values.
Results may differ from the reference program's by a relative error of at most 0.0095.
Values may be sent and summed in bfloat16 or wider, within the bound.
No kernel may reach another device: no remote copies, remote signals or barrier semaphores. Data moves between devices by JAX's collectives and lax.ppermute only.
A program may use at most 128 MiB of HBM per device.

```python
import jax
import jax.numpy as jnp
from jax import lax

TILE = 128
TERM_DEV = 4
ACT_DEV = 2
SL = 8
SR = 8
NT = 16


def draw_term_blocks(key, part):
    key = jax.random.fold_in(key, 5)
    groups = NT // TERM_DEV
    scores = jax.random.randint(key, (groups, TERM_DEV, SL), 0, 65536, dtype=jnp.int32)
    scores = scores * TERM_DEV + jnp.arange(TERM_DEV, dtype=jnp.int32)[None, :, None]
    ranks = jnp.argsort(jnp.argsort(scores, axis=1), axis=1)
    chosen = (ranks < ACT_DEV).astype(jnp.int32)
    return chosen.reshape(NT, SL)


def place_ends(drawn, stream_key, smallest, high):
    longest = drawn.shape.index(max(drawn.shape))
    spots = []
    for shift in (0, 1):
        where = [jax.random.randint(jax.random.fold_in(stream_key, axis), (), 0, length) for axis, length in enumerate(drawn.shape)]
        where[longest] = (where[longest] + shift) % drawn.shape[longest]
        spots.append(tuple(where))
    return drawn.at[spots[0]].set(smallest).at[spots[1]].set(high)


def block_levels(own_key, dims, shards, low, top_value):
    def one(position, shards_of):
        heights = jax.random.uniform(jax.random.fold_in(jax.random.fold_in(own_key, 6), position), (shards_of,), jnp.float32, low / len(shards), top_value / len(shards))
        return jnp.repeat(jnp.exp(heights), dims[position] // shards_of).reshape((-1,) + (1,) * (len(dims) - position - 1))

    gain = one(*shards[0])
    for cut in shards[1:]:
        gain = gain * one(*cut)
    return gain


def noise(key, shape, scale, reach, shards=(), held_as=jnp.bfloat16):
    entries = jax.random.normal(key, shape, jnp.float32) * scale
    if len(shards) > 0:
        entries = block_levels(key, shape, shards, -0.22, 0.18) * entries
    return jnp.clip(entries, min=-reach, max=reach).astype(held_as)


def setup_inputs(seed: int = 0, part: int = 0) -> dict:
    key_list = jax.random.split(jax.random.key(seed), 7)
    own_keys = jax.random.split(jax.random.fold_in(key_list[6], part), 7)
    return {
        "psi": noise(own_keys[0], (SL, SR, TILE, TILE), 1.0, 6.0, ((0, 4),)),
        "left_ops": noise(own_keys[1], (NT, SL, TILE, TILE), TILE ** -0.5, 0.5, ((0, 4), (1, 4))),
        "right_ops": noise(own_keys[2], (NT, SR, TILE, TILE), (TILE * NT // 2) ** -0.5, 0.1875, ((0, 4), (1, 4))),
        "term_blocks": draw_term_blocks(jax.random.fold_in(jax.random.fold_in(key_list[6], part), 71), part),
        "left_sizes": place_ends(jax.random.randint(own_keys[4], (SL,), 1, TILE + 1), jax.random.fold_in(own_keys[4], 1), 1, TILE).astype(jnp.int32),
        "right_sizes": place_ends(jax.random.randint(own_keys[5], (SR,), 1, TILE + 1), jax.random.fold_in(own_keys[5], 1), 1, TILE).astype(jnp.int32),
    }


def reference(psi, left_ops, right_ops, term_blocks, left_sizes, right_sizes):
    positions = jnp.arange(TILE, dtype=jnp.int32)
    left_keep = positions[None, :] < left_sizes[:, None]
    right_keep = positions[None, :] < right_sizes[:, None]
    keep_mask = (left_keep[:, None, :, None] & right_keep[None, :, None, :]).astype(jnp.bfloat16)
    masked = psi * keep_mask
    scaled = left_ops * term_blocks.astype(jnp.bfloat16)[:, :, None, None]
    group_count = NT // TERM_DEV
    scaled_groups = scaled.reshape(group_count, TERM_DEV, SL, TILE, TILE)
    right_groups = right_ops.reshape(group_count, TERM_DEV, SR, TILE, TILE)

    def one_term(inner, operators):
        left_term, right_term = operators
        applied = jnp.einsum("aik,abkj->abij", left_term.astype(jnp.float32), masked.astype(jnp.float32)).astype(jnp.bfloat16)
        update = jnp.einsum("abij,blj->bail", applied.astype(jnp.float32), right_term.astype(jnp.float32))
        return inner + update, None

    def one_group(total, operators):
        start_inner = jnp.zeros((SR, SL, TILE, TILE), jnp.float32)
        inner, unused = lax.scan(one_term, start_inner, operators)
        rounded = inner.astype(jnp.bfloat16).astype(jnp.float32)
        return total + rounded, None

    start_total = jnp.zeros((SR, SL, TILE, TILE), jnp.float32)
    total, unused = lax.scan(one_group, start_total, (scaled_groups, right_groups))
    out_keep = (right_keep[:, None, None, :] & left_keep[None, :, :, None]).astype(jnp.float32)
    return (total * out_keep).astype(jnp.bfloat16)
```

```python
import functools

import jax
import jax.numpy as jnp
from jax import lax
from jax.experimental import pallas as pl
from jax.experimental.pallas import tpu as pltpu
from jax.sharding import PartitionSpec as P

ANY = pl.BlockSpec(memory_space=pl.ANY)
SMEM = pl.BlockSpec(memory_space=pltpu.SMEM)
VMEM = pl.BlockSpec(memory_space=pltpu.VMEM)


def acting_terms(blocks_ref, sector):
    count = blocks_ref.shape[0]
    first = jnp.int32(0)
    second = jnp.int32(0)
    for term in reversed(range(count)):
        acts = blocks_ref[term, sector] > 0
        second = jnp.where(acts, first, second)
        first = jnp.where(acts, term, first)
    return first, second


def pack_kernel(steps, blocks_ref, psi_ref, left_ref, *rest):
    left_out, psi_out, sem = rest[0], rest[1 : 1 + len(steps)], rest[-1]
    here = lax.axis_index("blk")
    sectors = psi_ref.shape[0]
    copies = []
    for local in range(sectors):
        for slot, term in enumerate(acting_terms(blocks_ref, here * sectors + local)):
            copies.append(
                pltpu.make_async_copy(
                    left_ref.at[term, local], left_out.at[local, slot], sem.at[len(copies)]
                )
            )
    for step, out in zip(steps, psi_out):
        there = jnp.bitwise_xor(here, step)
        copies.append(
            pltpu.make_async_copy(
                psi_ref.at[:, pl.ds(there * sectors, sectors)], out, sem.at[len(copies)]
            )
        )
    for copy in copies:
        copy.start()
    for copy in copies:
        copy.wait()


def apply_kernel(nz, blocks_ref, lsize_ref, rsize_ref, *rest):
    lefts, psis, (right_hbm,) = rest[:nz], rest[nz : 2 * nz], rest[2 * nz : 2 * nz + 1]
    outs = rest[2 * nz + 1 : 3 * nz + 1]
    left_all, psi_all, right, sem, right_sem = rest[3 * nz + 1 :]
    here = lax.axis_index("blk")
    mine = lax.axis_index("op")
    sectors = lefts[0].shape[0]
    tile = right.shape[-1]
    right_copy = pltpu.make_async_copy(right_hbm, right, right_sem)
    right_copy.start()
    copies = []
    for step in range(nz):
        there = jnp.bitwise_xor(here, step)
        copies.append(pltpu.make_async_copy(lefts[step], left_all.at[there], sem.at[len(copies)]))
        column = here * sectors if step == 0 else 0
        for b in range(sectors):
            copies.append(
                pltpu.make_async_copy(
                    psis[step].at[:, column + b],
                    psi_all.at[there, :, :, pl.ds(b * tile, tile)],
                    sem.at[len(copies)],
                )
            )
    for copy in copies:
        copy.start()
    right_copy.wait()
    for copy in copies:
        copy.wait()
    rows = lax.broadcasted_iota(jnp.int32, (tile, sectors * tile), 0)
    lanes = lax.broadcasted_iota(jnp.int32, (tile, sectors * tile), 1)
    width = jnp.zeros_like(lanes)
    for b in range(sectors):
        inside = (lanes >= b * tile) & (lanes < b * tile + rsize_ref[here * sectors + b])
        width = width | inside.astype(jnp.int32)
    for step in range(nz):
        there = jnp.bitwise_xor(mine, step)
        for local in range(sectors):
            sector = there * sectors + local
            keep = (width > 0) & (rows < lsize_ref[sector])
            block = psi_all[there, local].astype(jnp.float32)
            block = jnp.where(keep, block, 0.0).astype(jnp.bfloat16)
            ops = left_all[there, local].reshape(2 * tile, tile)
            applied = jnp.dot(ops, block, preferred_element_type=jnp.float32).astype(jnp.bfloat16)
            first, second = acting_terms(blocks_ref, sector)
            for b in range(sectors):
                cut = slice(b * tile, (b + 1) * tile)
                both = jnp.concatenate([applied[:tile, cut], applied[tile:, cut]], axis=1)
                pair = jnp.concatenate([right[first, b], right[second, b]], axis=1)
                total = lax.dot_general(
                    both, pair, (((1,), (1,)), ((), ())), preferred_element_type=jnp.float32
                )
                outs[step][b, local] = total.astype(jnp.bfloat16)


def sum_kernel(lsize_ref, rsize_ref, *rest):
    parts, out_ref = rest[:-1], rest[-1]
    here = lax.axis_index("blk")
    mine = lax.axis_index("op")
    sectors, tile = out_ref.shape[0], out_ref.shape[-1]
    rows = lax.broadcasted_iota(jnp.int32, (tile, tile), 0)
    lanes = lax.broadcasted_iota(jnp.int32, (tile, tile), 1)
    for b in range(sectors):
        for a in range(out_ref.shape[1]):
            total = parts[0][b, a].astype(jnp.float32)
            for part in parts[1:]:
                total = total + part[b, a].astype(jnp.float32)
            keep = (rows < lsize_ref[mine * sectors + a]) & (lanes < rsize_ref[here * sectors + b])
            out_ref[b, a] = jnp.where(keep, total, 0.0).astype(jnp.bfloat16)


def shards(nz, psi, left_ops, right_ops, term_blocks, left_sizes, right_sizes):
    sectors, tile = psi.shape[0], psi.shape[-1]
    steps = tuple(range(1, nz))
    block = functools.partial(jax.ShapeDtypeStruct, dtype=jnp.bfloat16)
    packed = pl.pallas_call(
        functools.partial(pack_kernel, steps),
        out_shape=[block((sectors, 2, tile, tile))] + [block((sectors, sectors, tile, tile))] * len(steps),
        in_specs=[SMEM, ANY, ANY],
        out_specs=[ANY] * nz,
        scratch_shapes=[pltpu.SemaphoreType.DMA((2 * sectors + len(steps),))],
        name="pack",
    )(term_blocks, psi, left_ops)
    left_own, psi_sent = packed[0], packed[1:]
    lefts, psis = [left_own], [psi]
    for step, sent in zip(steps, psi_sent):
        pairs = [(z, z ^ step) for z in range(nz)]
        psis.append(lax.ppermute(sent, "blk", pairs))
        lefts.append(lax.ppermute(left_own, "blk", pairs))
    parts = pl.pallas_call(
        functools.partial(apply_kernel, nz),
        out_shape=[block((sectors, sectors, tile, tile))] * nz,
        in_specs=[SMEM] * 3 + [ANY] * (2 * nz + 1),
        out_specs=[VMEM] * nz,
        scratch_shapes=[
            pltpu.VMEM((nz, sectors, 2, tile, tile), jnp.bfloat16),
            pltpu.VMEM((nz, sectors, tile, sectors * tile), jnp.bfloat16),
            pltpu.VMEM(right_ops.shape, jnp.bfloat16),
            pltpu.SemaphoreType.DMA((nz * (1 + sectors),)),
            pltpu.SemaphoreType.DMA(()),
        ],
        compiler_params=pltpu.CompilerParams(vmem_limit_bytes=32 * 1024 * 1024),
        name="apply",
    )(term_blocks, left_sizes, right_sizes, *lefts, *psis, right_ops)
    arrived = [parts[0]]
    for step in steps:
        arrived.append(lax.ppermute(parts[step], "op", [(o, o ^ step) for o in range(nz)]))
    return pl.pallas_call(
        sum_kernel,
        out_shape=block((sectors, sectors, tile, tile)),
        in_specs=[SMEM] * 2 + [VMEM] * nz,
        out_specs=VMEM,
        compiler_params=pltpu.CompilerParams(vmem_limit_bytes=32 * 1024 * 1024),
        name="sum",
    )(left_sizes, right_sizes, *arrived)


def wide_shards(psi, left_ops, right_ops, term_blocks, left_sizes, right_sizes):
    sectors_here = psi.shape[0]
    tile_size = psi.shape[2]
    left_first = lax.axis_index("blk") * sectors_here
    positions = lax.broadcasted_iota(jnp.int32, (tile_size,), 0)
    left_local = lax.dynamic_slice_in_dim(left_sizes, left_first, sectors_here)
    left_keep = positions[None, :] < left_local[:, None]
    right_keep = positions[None, :] < right_sizes[:, None]
    keep_mask = (left_keep[:, None, :, None] & right_keep[None, :, None, :]).astype(jnp.bfloat16)
    masked = psi * keep_mask
    acting_count = left_ops.shape[0] // 2
    order = jnp.argsort(1 - term_blocks, axis=0, stable=True)[:acting_count]
    ids_local = lax.dynamic_slice_in_dim(order, left_first, sectors_here, 1)
    sector_index = lax.broadcasted_iota(jnp.int32, (acting_count, sectors_here), 1)
    picked = left_ops[ids_local, sector_index]
    applied = jnp.einsum(
        "kaim,abmj->kabij", picked, masked, preferred_element_type=jnp.float32
    ).astype(jnp.bfloat16)
    arrived = lax.all_to_all(applied, "blk", split_axis=2, concat_axis=1, tiled=True)
    right_picked = right_ops[order]
    partial_value = jnp.einsum(
        "kabij,kablj->bail", arrived, right_picked, preferred_element_type=jnp.float32
    )
    summed = lax.psum_scatter(
        partial_value.astype(jnp.bfloat16), "op", scatter_dimension=1, tiled=True
    ).astype(jnp.float32)
    row_count = summed.shape[1]
    op_first = lax.axis_index("op") * row_count
    left_share = lax.dynamic_slice_in_dim(left_sizes, op_first, row_count)
    right_local = lax.dynamic_slice_in_dim(right_sizes, left_first, sectors_here)
    rows_keep = positions[None, :] < left_share[:, None]
    cols_keep = positions[None, :] < right_local[:, None]
    out_keep = (cols_keep[:, None, None, :] & rows_keep[None, :, :, None]).astype(jnp.float32)
    return (summed * out_keep).astype(jnp.bfloat16)


def solution(mesh):
    in_specs = (
        P(("parts", "blk"), None, None, None),
        P(("parts", "op"), "blk", None, None),
        P(("parts", "op"), "blk", None, None),
        P(("parts", "op"), None),
        P("parts"),
        P("parts"),
    )
    out_specs = P(("parts", "blk"), "op", None, None)
    nz, no = mesh.shape["blk"], mesh.shape["op"]
    body = functools.partial(shards, nz) if nz == no == 4 else wide_shards
    return jax.shard_map(body, mesh=mesh, in_specs=in_specs, out_specs=out_specs, check_vma=False)
```

```python
import functools

import jax
import jax.numpy as jnp
from jax import lax
from jax.experimental import pallas as pl
from jax.experimental.pallas import tpu as pltpu
from jax.sharding import PartitionSpec as P

ANY = pl.BlockSpec(memory_space=pl.ANY)
SMEM = pl.BlockSpec(memory_space=pltpu.SMEM)
VMEM = pl.BlockSpec(memory_space=pltpu.VMEM)
PARAMS = pltpu.CompilerParams(vmem_limit_bytes=32 * 1024 * 1024)
ID_ROWS = 16
PSI_STEP = (0, 2, 1, 3)


def acting_terms(blocks_ref, sector):
    first = jnp.int32(0)
    second = jnp.int32(0)
    for term in reversed(range(blocks_ref.shape[0])):
        acts = blocks_ref[term, sector] > 0
        second = jnp.where(acts, first, second)
        first = jnp.where(acts, term, first)
    return first, second


def pack_kernel(blocks_ref, psi_ref, left_ref, left_out, psi_out, sem):
    here = lax.axis_index("blk")
    mine = lax.axis_index("op")
    sectors, tile = psi_ref.shape[0], psi_ref.shape[-1]
    distance = jnp.int32(0)
    for index, step in enumerate(PSI_STEP):
        distance = jnp.where(mine == index, step, distance)
    there = jnp.bitwise_xor(here, distance)
    copies = [
        pltpu.make_async_copy(psi_ref.at[:, pl.ds(there * sectors, sectors)], psi_out, sem.at[0])
    ]
    row = lax.broadcasted_iota(jnp.int32, (ID_ROWS, tile), 0)
    ids = jnp.zeros((ID_ROWS, tile), jnp.float32)
    for local in range(sectors):
        for slot, term in enumerate(acting_terms(blocks_ref, here * sectors + local)):
            place = 2 * local + slot
            copies.append(
                pltpu.make_async_copy(
                    left_ref.at[term, local],
                    left_out.at[pl.ds(place * tile, tile)],
                    sem.at[len(copies)],
                )
            )
            ids = jnp.where(row == place, term.astype(jnp.float32), ids)
    for copy in copies:
        copy.start()
    left_out[pl.ds(2 * sectors * tile, ID_ROWS)] = ids.astype(jnp.bfloat16)
    for copy in copies:
        copy.wait()


def apply_kernel(n, lsize_ref, rsize_ref, psi_ref, *rest):
    lefts, rights, out_ref = rest[:n], rest[n : 2 * n], rest[2 * n]
    right_all, sem = rest[2 * n + 1 :]
    here = lax.axis_index("blk")
    mine = lax.axis_index("op")
    sectors, tile = out_ref.shape[0], out_ref.shape[-1]
    terms = right_all.shape[1]
    copies = [
        pltpu.make_async_copy(rights[r], right_all.at[jnp.bitwise_xor(here, r)], sem.at[r])
        for r in range(n)
    ]
    for copy in copies:
        copy.start()
    rows = lax.broadcasted_iota(jnp.int32, (tile, tile), 0)
    lanes = lax.broadcasted_iota(jnp.int32, (tile, tile), 1)
    applied = []
    for a in range(sectors):
        height = lsize_ref[mine * sectors + a]
        cut = []
        for b in range(sectors):
            keep = (rows < height) & (lanes < rsize_ref[here * sectors + b])
            cut.append(jnp.where(keep, psi_ref[a, b].astype(jnp.float32), 0.0).astype(jnp.bfloat16))
        block = jnp.concatenate(cut, axis=1)
        applied.append([])
        for s in range(n):
            ops = lefts[s][pl.ds(2 * a * tile, 2 * tile)]
            both = jnp.dot(ops, block, preferred_element_type=jnp.float32).astype(jnp.bfloat16)
            applied[a] += [both[:tile], both[tile:]]
    for copy in copies:
        copy.wait()
    ids = [lefts[s][pl.ds(2 * sectors * tile, ID_ROWS)].astype(jnp.float32) for s in range(n)]
    for a in range(sectors):
        height = lsize_ref[mine * sectors + a]
        for b in range(sectors):
            picked = []
            for s in range(n):
                for slot in range(2):
                    place = 2 * a + slot
                    term = jnp.broadcast_to(ids[s][place : place + 1], (tile, tile))
                    block = right_all[s, 0, b].astype(jnp.float32)
                    for t in range(1, terms):
                        block = jnp.where(term == t, right_all[s, t, b].astype(jnp.float32), block)
                    picked.append(block.astype(jnp.bfloat16))
            column = [x[:, b * tile : (b + 1) * tile] for x in applied[a]]
            total = lax.dot_general(
                jnp.concatenate(column, axis=1),
                jnp.concatenate(picked, axis=1),
                (((1,), (1,)), ((), ())),
                preferred_element_type=jnp.float32,
            )
            keep = (rows < height) & (lanes < rsize_ref[here * sectors + b])
            out_ref[b, a] = jnp.where(keep, total, 0.0).astype(jnp.bfloat16)


def shards(n, psi, left_ops, right_ops, term_blocks, left_sizes, right_sizes):
    sectors, tile = psi.shape[0], psi.shape[-1]
    block = functools.partial(jax.ShapeDtypeStruct, dtype=jnp.bfloat16)

    def over_op(array, step):
        return lax.ppermute(array, "op", [(o, o ^ step) for o in range(n)])

    def over_both(array, target):
        pairs = []
        for z in range(n):
            for o in range(n):
                to_z, to_o = target(z, o)
                pairs.append((z * n + o, to_z * n + to_o))
        return lax.ppermute(array, ("blk", "op"), pairs)

    left_sent, psi_sent = pl.pallas_call(
        pack_kernel,
        out_shape=[block((2 * sectors * tile + ID_ROWS, tile)), block((sectors, sectors, tile, tile))],
        in_specs=[SMEM, ANY, ANY],
        out_specs=[VMEM, VMEM],
        scratch_shapes=[pltpu.SemaphoreType.DMA((2 * sectors + 1,))],
        compiler_params=PARAMS,
        name="pack",
    )(term_blocks, psi, left_ops)
    across = over_op(right_ops, 2)
    rights = [right_ops, over_op(right_ops, 1), across, over_op(across, 1)]
    lefts = [over_both(left_sent, lambda z, o: (z ^ o ^ s, z)) for s in range(n)]
    psi_here = over_both(psi_sent, lambda z, o: (z ^ PSI_STEP[o], z))
    return pl.pallas_call(
        functools.partial(apply_kernel, n),
        out_shape=block((sectors, sectors, tile, tile)),
        in_specs=[SMEM] * 2 + [VMEM] * (1 + n) + [ANY] * n,
        out_specs=VMEM,
        scratch_shapes=[
            pltpu.VMEM((n,) + right_ops.shape, jnp.bfloat16),
            pltpu.SemaphoreType.DMA((n,)),
        ],
        compiler_params=PARAMS,
        name="apply",
    )(left_sizes, right_sizes, psi_here, *lefts, *rights)


def wide_shards(psi, left_ops, right_ops, term_blocks, left_sizes, right_sizes):
    sectors_here = psi.shape[0]
    tile_size = psi.shape[2]
    left_first = lax.axis_index("blk") * sectors_here
    positions = lax.broadcasted_iota(jnp.int32, (tile_size,), 0)
    left_local = lax.dynamic_slice_in_dim(left_sizes, left_first, sectors_here)
    left_keep = positions[None, :] < left_local[:, None]
    right_keep = positions[None, :] < right_sizes[:, None]
    keep_mask = (left_keep[:, None, :, None] & right_keep[None, :, None, :]).astype(jnp.bfloat16)
    masked = psi * keep_mask
    acting_count = left_ops.shape[0] // 2
    order = jnp.argsort(1 - term_blocks, axis=0, stable=True)[:acting_count]
    ids_local = lax.dynamic_slice_in_dim(order, left_first, sectors_here, 1)
    sector_index = lax.broadcasted_iota(jnp.int32, (acting_count, sectors_here), 1)
    picked = left_ops[ids_local, sector_index]
    applied = jnp.einsum(
        "kaim,abmj->kabij", picked, masked, preferred_element_type=jnp.float32
    ).astype(jnp.bfloat16)
    arrived = lax.all_to_all(applied, "blk", split_axis=2, concat_axis=1, tiled=True)
    right_picked = right_ops[order]
    partial_value = jnp.einsum(
        "kabij,kablj->bail", arrived, right_picked, preferred_element_type=jnp.float32
    )
    summed = lax.psum_scatter(
        partial_value.astype(jnp.bfloat16), "op", scatter_dimension=1, tiled=True
    ).astype(jnp.float32)
    row_count = summed.shape[1]
    op_first = lax.axis_index("op") * row_count
    left_share = lax.dynamic_slice_in_dim(left_sizes, op_first, row_count)
    right_local = lax.dynamic_slice_in_dim(right_sizes, left_first, sectors_here)
    rows_keep = positions[None, :] < left_share[:, None]
    cols_keep = positions[None, :] < right_local[:, None]
    out_keep = (cols_keep[:, None, None, :] & rows_keep[None, :, :, None]).astype(jnp.float32)
    return (summed * out_keep).astype(jnp.bfloat16)


def solution(mesh):
    in_specs = (
        P(("parts", "blk"), None, None, None),
        P(("parts", "op"), "blk", None, None),
        P(("parts", "op"), "blk", None, None),
        P(("parts", "op"), None),
        P("parts"),
        P("parts"),
    )
    out_specs = P(("parts", "blk"), "op", None, None)
    nz, no = mesh.shape["blk"], mesh.shape["op"]
    body = functools.partial(shards, nz) if nz == no == 4 else wide_shards
    return jax.shard_map(body, mesh=mesh, in_specs=in_specs, out_specs=out_specs, check_vma=False)
```

```python
import functools

import jax
import jax.numpy as jnp
from jax import lax
from jax.experimental import pallas as pl
from jax.experimental.pallas import tpu as pltpu
from jax.sharding import PartitionSpec as P

ANY = pl.BlockSpec(memory_space=pl.ANY)
SMEM = pl.BlockSpec(memory_space=pltpu.SMEM)
VMEM = pl.BlockSpec(memory_space=pltpu.VMEM)
PARAMS = pltpu.CompilerParams(vmem_limit_bytes=32 * 1024 * 1024)
ID_ROWS = 16


def acting_terms(blocks_ref, sector):
    first = jnp.int32(0)
    second = jnp.int32(0)
    for term in reversed(range(blocks_ref.shape[0])):
        acts = blocks_ref[term, sector] > 0
        second = jnp.where(acts, first, second)
        first = jnp.where(acts, term, first)
    return first, second


def place():
    op = lax.axis_index("op")
    return lax.axis_index("blk"), lax.shift_right_logical(op, 1), jnp.bitwise_and(op, 1)


def pack_kernel(blocks_ref, psi_ref, left_ref, *rest):
    outs, sem = list(enumerate(rest[:-1])), rest[-1]
    z, _, c = place()
    sectors, tile = psi_ref.shape[0], psi_ref.shape[-1]
    row = lax.broadcasted_iota(jnp.int32, (ID_ROWS, tile), 0)
    ids = jnp.zeros((ID_ROWS, tile), jnp.float32)
    sources = []
    for local in range(sectors):
        for slot, term in enumerate(acting_terms(blocks_ref, z * sectors + local)):
            ids = jnp.where(row == len(sources), term.astype(jnp.float32), ids)
            sources.append(left_ref.at[term, local])
    copies = []
    for step, out in outs:
        there = jnp.bitwise_xor(z, jnp.bitwise_xor(c, step))
        column = there * sectors + c
        blocks = sources + [psi_ref.at[local, column] for local in range(sectors)]
        for spot, source in enumerate(blocks):
            copies.append(
                pltpu.make_async_copy(source, out.at[pl.ds(spot * tile, tile)], sem.at[len(copies)])
            )
    for copy in copies:
        copy.start()
    for _, out in outs:
        out[pl.ds(3 * sectors * tile, ID_ROWS)] = ids.astype(jnp.bfloat16)
    for copy in copies:
        copy.wait()


def apply_kernel(stays, lsize_ref, rsize_ref, *rest):
    messages, rights, out_ref = rest[:4], rest[4:6], rest[6]
    z, x, c = place()
    sectors, tile = out_ref.shape[0], out_ref.shape[-1]
    terms = rights[0].shape[0]
    half = lax.shift_right_logical(z, 1)
    odd = jnp.bitwise_and(z, 1)
    rows = lax.broadcasted_iota(jnp.int32, (tile, tile), 0)
    lanes = lax.broadcasted_iota(jnp.int32, (tile, tile), 1)

    def run(far, own_first):
        owner = 2 * ((1 - half) if far else half) + c
        pair = messages[2:] if far else messages[:2]
        order = rights if own_first else rights[::-1]
        columns = (c, 1 - c) if own_first else (1 - c, c)
        ids = [ref[pl.ds(3 * sectors * tile, ID_ROWS)].astype(jnp.float32) for ref in pair]
        for a in range(sectors):
            height = lsize_ref[owner * sectors + a]
            cut = []
            for ref, b in zip(pair, columns):
                keep = (rows < height) & (lanes < rsize_ref[z * sectors + b])
                block = ref[pl.ds((2 * sectors + a) * tile, tile)].astype(jnp.float32)
                cut.append(jnp.where(keep, block, 0.0).astype(jnp.bfloat16))
            wide = jnp.concatenate(cut, axis=1)
            applied = []
            for ref in pair:
                ops = ref[pl.ds(2 * a * tile, 2 * tile)]
                both = jnp.dot(ops, wide, preferred_element_type=jnp.float32).astype(jnp.bfloat16)
                applied += [both[:tile], both[tile:]]
            for side, b in enumerate(columns):
                picked = []
                for s in range(2):
                    for slot in range(2):
                        spot = 2 * a + slot
                        term = jnp.broadcast_to(ids[s][spot : spot + 1], (tile, tile))
                        block = order[s][0, b].astype(jnp.float32)
                        for t in range(1, terms):
                            block = jnp.where(term == t, order[s][t, b].astype(jnp.float32), block)
                        picked.append(block.astype(jnp.bfloat16))
                column = [part[:, side * tile : (side + 1) * tile] for part in applied]
                total = lax.dot_general(
                    jnp.concatenate(column, axis=1),
                    jnp.concatenate(picked, axis=1),
                    (((1,), (1,)), ((), ())),
                    preferred_element_type=jnp.float32,
                )
                out_ref[b, a] = total.astype(out_ref.dtype)

    for far in (False, True):
        for own_first in (False, True):
            wanted = ((half == x) != far) == stays

            @pl.when(wanted & (odd == (0 if own_first else 1)))
            def _(far=far, own_first=own_first):
                run(far, own_first)


def sum_kernel(lsize_ref, rsize_ref, kept_ref, arrived_ref, out_ref):
    z, _, _ = place()
    op = lax.axis_index("op")
    sectors, tile = out_ref.shape[0], out_ref.shape[-1]
    rows = lax.broadcasted_iota(jnp.int32, (tile, tile), 0)
    lanes = lax.broadcasted_iota(jnp.int32, (tile, tile), 1)
    for b in range(sectors):
        for a in range(sectors):
            total = kept_ref[b, a] + arrived_ref[b, a].astype(jnp.float32)
            keep = (rows < lsize_ref[op * sectors + a]) & (lanes < rsize_ref[z * sectors + b])
            out_ref[b, a] = jnp.where(keep, total, 0.0).astype(jnp.bfloat16)


def shards(psi, left_ops, right_ops, term_blocks, left_sizes, right_sizes):
    n = 4
    sectors, tile = psi.shape[0], psi.shape[-1]
    block = functools.partial(jax.ShapeDtypeStruct, dtype=jnp.bfloat16)

    def over_op(array, step):
        return lax.ppermute(array, "op", [(o, o ^ step) for o in range(n)])

    def over_z(array, distance):
        pairs = []
        for z in range(n):
            for o in range(n):
                pairs.append((z * n + o, (z ^ distance(o & 1)) * n + (o & 2) + (z & 1)))
        return lax.ppermute(array, ("blk", "op"), pairs)

    sent = pl.pallas_call(
        pack_kernel,
        out_shape=[block((3 * sectors * tile + ID_ROWS, tile))] * n,
        in_specs=[SMEM, ANY, ANY],
        out_specs=[VMEM] * n,
        scratch_shapes=[pltpu.SemaphoreType.DMA((3 * sectors * n,))],
        compiler_params=pltpu.CompilerParams(vmem_limit_bytes=60 * 1024 * 1024),
        name="pack",
    )(term_blocks, psi, left_ops)
    messages = [None] * n
    for s in (2, 3, 0, 1):
        messages[s] = over_z(sent[s], lambda c: s ^ c)
    held, _ = lax.optimization_barrier((right_ops, sent[0]))
    rights = [right_ops, over_op(held, 1)]

    def apply(stays, dtype):
        return pl.pallas_call(
            functools.partial(apply_kernel, stays),
            out_shape=jax.ShapeDtypeStruct((sectors, sectors, tile, tile), dtype),
            in_specs=[SMEM] * 2 + [VMEM] * 6,
            out_specs=VMEM,
            compiler_params=PARAMS,
            name="apply_kept" if stays else "apply_sent",
        )(left_sizes, right_sizes, *messages, *rights)

    arrived = over_op(apply(False, jnp.bfloat16), 2)
    kept = apply(True, jnp.float32)
    return pl.pallas_call(
        sum_kernel,
        out_shape=block((sectors, sectors, tile, tile)),
        in_specs=[SMEM] * 2 + [VMEM] * 2,
        out_specs=VMEM,
        compiler_params=PARAMS,
        name="sum",
    )(left_sizes, right_sizes, kept, arrived)


def wide_shards(psi, left_ops, right_ops, term_blocks, left_sizes, right_sizes):
    sectors_here = psi.shape[0]
    tile_size = psi.shape[2]
    left_first = lax.axis_index("blk") * sectors_here
    positions = lax.broadcasted_iota(jnp.int32, (tile_size,), 0)
    left_local = lax.dynamic_slice_in_dim(left_sizes, left_first, sectors_here)
    left_keep = positions[None, :] < left_local[:, None]
    right_keep = positions[None, :] < right_sizes[:, None]
    keep_mask = (left_keep[:, None, :, None] & right_keep[None, :, None, :]).astype(jnp.bfloat16)
    masked = psi * keep_mask
    acting_count = left_ops.shape[0] // 2
    order = jnp.argsort(1 - term_blocks, axis=0, stable=True)[:acting_count]
    ids_local = lax.dynamic_slice_in_dim(order, left_first, sectors_here, 1)
    sector_index = lax.broadcasted_iota(jnp.int32, (acting_count, sectors_here), 1)
    picked = left_ops[ids_local, sector_index]
    applied = jnp.einsum(
        "kaim,abmj->kabij", picked, masked, preferred_element_type=jnp.float32
    ).astype(jnp.bfloat16)
    arrived = lax.all_to_all(applied, "blk", split_axis=2, concat_axis=1, tiled=True)
    right_picked = right_ops[order]
    partial_value = jnp.einsum(
        "kabij,kablj->bail", arrived, right_picked, preferred_element_type=jnp.float32
    )
    summed = lax.psum_scatter(
        partial_value.astype(jnp.bfloat16), "op", scatter_dimension=1, tiled=True
    ).astype(jnp.float32)
    row_count = summed.shape[1]
    op_first = lax.axis_index("op") * row_count
    left_share = lax.dynamic_slice_in_dim(left_sizes, op_first, row_count)
    right_local = lax.dynamic_slice_in_dim(right_sizes, left_first, sectors_here)
    rows_keep = positions[None, :] < left_share[:, None]
    cols_keep = positions[None, :] < right_local[:, None]
    out_keep = (cols_keep[:, None, None, :] & rows_keep[None, :, :, None]).astype(jnp.float32)
    return (summed * out_keep).astype(jnp.bfloat16)


def solution(mesh):
    in_specs = (
        P(("parts", "blk"), None, None, None),
        P(("parts", "op"), "blk", None, None),
        P(("parts", "op"), "blk", None, None),
        P(("parts", "op"), None),
        P("parts"),
        P("parts"),
    )
    out_specs = P(("parts", "blk"), "op", None, None)
    nz, no = mesh.shape["blk"], mesh.shape["op"]
    body = shards if nz == no == 4 else wide_shards
    return jax.shard_map(body, mesh=mesh, in_specs=in_specs, out_specs=out_specs, check_vma=False)
```

```python
import functools

import jax
import jax.numpy as jnp
from jax import lax
from jax.experimental import pallas as pl
from jax.experimental.pallas import tpu as pltpu
from jax.sharding import PartitionSpec as P

ANY = pl.BlockSpec(memory_space=pl.ANY)
SMEM = pl.BlockSpec(memory_space=pltpu.SMEM)
VMEM = pl.BlockSpec(memory_space=pltpu.VMEM)
PARAMS = pltpu.CompilerParams(vmem_limit_bytes=32 * 1024 * 1024)
ID_ROWS = 16


def acting_terms(blocks_ref, sector):
    first = jnp.int32(0)
    second = jnp.int32(0)
    for term in reversed(range(blocks_ref.shape[0])):
        acts = blocks_ref[term, sector] > 0
        second = jnp.where(acts, first, second)
        first = jnp.where(acts, term, first)
    return first, second


def place():
    op = lax.axis_index("op")
    return lax.axis_index("blk"), lax.shift_right_logical(op, 1), jnp.bitwise_and(op, 1)


def pack_kernel(blocks_ref, psi_ref, left_ref, left_out, own_out, first_out, second_out, sem):
    z, _, c = place()
    sectors, tile = psi_ref.shape[0], psi_ref.shape[-1]
    home = c == jnp.bitwise_and(z, 1)
    row = lax.broadcasted_iota(jnp.int32, (ID_ROWS, tile), 0)
    ids = jnp.zeros((ID_ROWS, tile), jnp.float32)
    copies = []
    for local in range(sectors):
        for term in acting_terms(blocks_ref, z * sectors + local):
            spot = len(copies)
            ids = jnp.where(row == spot, term.astype(jnp.float32), ids)
            copies.append(
                pltpu.make_async_copy(
                    left_ref.at[term, local], left_out.at[pl.ds(spot * tile, tile)], sem.at[spot]
                )
            )
    for distance, out in ((jnp.where(home, 2, 3), first_out), (1, second_out), (0, own_out)):
        columns = pl.ds(jnp.bitwise_xor(z, distance) * sectors, sectors)
        copies.append(pltpu.make_async_copy(psi_ref.at[:, columns], out, sem.at[len(copies)]))
    for copy in copies:
        copy.start()
    left_out[pl.ds(2 * sectors * tile, ID_ROWS)] = ids.astype(jnp.bfloat16)
    for copy in copies:
        copy.wait()


def partial_sums(z, distance, sizes, pair, psi_ref, rights, store):
    lsize_ref, rsize_ref = sizes
    sectors, tile = psi_ref.shape[0], psi_ref.shape[-1]
    rows = lax.broadcasted_iota(jnp.int32, (tile, tile), 0)
    lanes = lax.broadcasted_iota(jnp.int32, (tile, tile), 1)
    owner = jnp.bitwise_xor(z, distance)
    ids = [ref[pl.ds(2 * sectors * tile, ID_ROWS)].astype(jnp.float32) for ref in pair]
    for a in range(sectors):
        height = lsize_ref[owner * sectors + a]
        keeps = [(rows < height) & (lanes < rsize_ref[z * sectors + b]) for b in range(sectors)]
        cut = [
            jnp.where(keep, psi_ref[a, b].astype(jnp.float32), 0.0).astype(jnp.bfloat16)
            for b, keep in enumerate(keeps)
        ]
        wide = jnp.concatenate(cut, axis=1)
        applied = []
        for ref in pair:
            ops = ref[pl.ds(2 * a * tile, 2 * tile)]
            both = jnp.dot(ops, wide, preferred_element_type=jnp.float32).astype(jnp.bfloat16)
            applied += [both[:tile], both[tile:]]
        for b, keep in enumerate(keeps):
            picked = []
            for right_ref, id_rows in zip(rights, ids):
                for spot in (2 * a, 2 * a + 1):
                    term = jnp.broadcast_to(id_rows[spot : spot + 1], (tile, tile))
                    block = right_ref[0, b].astype(jnp.float32)
                    for t in range(1, right_ref.shape[0]):
                        block = jnp.where(term == t, right_ref[t, b].astype(jnp.float32), block)
                    picked.append(block.astype(jnp.bfloat16))
            column = [part[:, b * tile : (b + 1) * tile] for part in applied]
            total = lax.dot_general(
                jnp.concatenate(column, axis=1),
                jnp.concatenate(picked, axis=1),
                (((1,), (1,)), ((), ())),
                preferred_element_type=jnp.float32,
            )
            store(b, a, jnp.where(keep, total, 0.0))


def near_kernel(lsize_ref, rsize_ref, *rest):
    own, swapped, direct_a, direct_b, psi_own, psi_second = rest[:6]
    rights, out_ref = rest[6:8], rest[8]
    z, _, c = place()
    home = c == jnp.bitwise_and(z, 1)

    def store(b, a, total):
        out_ref[b, a] = total

    @pl.when(home)
    def _():
        partial_sums(z, 0, (lsize_ref, rsize_ref), (own, swapped), psi_own, rights, store)

    @pl.when(jnp.logical_not(home))
    def _():
        partial_sums(z, 1, (lsize_ref, rsize_ref), (direct_b, direct_a), psi_second, rights, store)


def far_kernel(lsize_ref, rsize_ref, *rest):
    direct_a, direct_b, passed_a, passed_b, psi_first = rest[:5]
    rights, near_ref, sent_ref, out_ref = rest[5:7], rest[7], rest[8], rest[9]
    z, x, c = place()
    home = c == jnp.bitwise_and(z, 1)
    far_leaves = lax.shift_right_logical(z, 1) == x

    def store_sent(b, a, total):
        sent_ref[b, a] = total.astype(sent_ref.dtype)

    def store_kept(b, a, total):
        out_ref[b, a] = total
        sent_ref[b, a] = near_ref[b, a].astype(sent_ref.dtype)

    for leaves, store in ((True, store_sent), (False, store_kept)):
        for at_home, distance, pair in (
            (True, 2, (direct_a, direct_b)),
            (False, 3, (passed_a, passed_b)),
        ):

            @pl.when((far_leaves == leaves) & (home == at_home))
            def _(distance=distance, pair=pair, store=store):
                sizes = (lsize_ref, rsize_ref)
                partial_sums(z, distance, sizes, pair, psi_first, rights, store)


def shards(psi, left_ops, right_ops, term_blocks, left_sizes, right_sizes):
    n = 4
    sectors, tile = psi.shape[0], psi.shape[-1]
    block = functools.partial(jax.ShapeDtypeStruct, dtype=jnp.bfloat16)
    blocks = block((sectors, sectors, tile, tile))

    def over_op(array, step):
        return lax.ppermute(array, "op", [(o, o ^ step) for o in range(n)])

    def over_z(array, home_step, other_step):
        pairs = []
        for z in range(n):
            for o in range(n):
                step = home_step if o & 1 == z & 1 else other_step
                if step is not None:
                    pairs.append((z * n + o, (z ^ step) * n + (o & 2) + (z & 1)))
        return lax.ppermute(array, ("blk", "op"), pairs)

    left_sent, psi_own, psi_first, psi_second = pl.pallas_call(
        pack_kernel,
        out_shape=[block((2 * sectors * tile + ID_ROWS, tile))] + [blocks] * 3,
        in_specs=[SMEM, ANY, ANY],
        out_specs=[VMEM] * 4,
        scratch_shapes=[pltpu.SemaphoreType.DMA((2 * sectors + 3,))],
        compiler_params=pltpu.CompilerParams(vmem_limit_bytes=60 * 1024 * 1024),
        name="pack",
    )(term_blocks, psi, left_ops)
    direct_a = over_z(left_sent, 2, 1)
    direct_b = over_z(left_sent, 1, 2)
    first = over_z(psi_first, 2, 3)
    second = over_z(psi_second, 1, None)
    passed_a = over_z(direct_a, 1, None)
    passed_b = over_z(direct_b, 1, None)
    swapped = over_op(left_sent, 1)
    held, _ = lax.optimization_barrier((right_ops, left_sent))
    rights = [right_ops, over_op(held, 1)]

    def apply(kernel, outs, *operands):
        return pl.pallas_call(
            kernel,
            out_shape=[jax.ShapeDtypeStruct(blocks.shape, dtype) for dtype in outs],
            in_specs=[SMEM] * 2 + [VMEM] * len(operands),
            out_specs=[VMEM] * len(outs),
            compiler_params=PARAMS,
            cost_estimate=pl.CostEstimate(
                flops=64 * tile**3 * sectors**2, bytes_accessed=2**20, transcendentals=0
            ),
            name=kernel.__name__,
        )(left_sizes, right_sizes, *operands)

    (near,) = apply(
        near_kernel, [jnp.float32],
        left_sent, swapped, direct_a, direct_b, psi_own, second, *rights,
    )
    sent, far = apply(
        far_kernel, [jnp.bfloat16, jnp.float32],
        direct_a, direct_b, passed_a, passed_b, first, *rights, near,
    )
    arrived = over_op(sent, 2)
    far_left = lax.axis_index("blk") // 2 == lax.axis_index("op") // 2
    kept = jnp.where(far_left, near, far)
    return (kept + arrived.astype(jnp.float32)).astype(jnp.bfloat16)


def wide_shards(psi, left_ops, right_ops, term_blocks, left_sizes, right_sizes):
    sectors_here = psi.shape[0]
    tile_size = psi.shape[2]
    left_first = lax.axis_index("blk") * sectors_here
    positions = lax.broadcasted_iota(jnp.int32, (tile_size,), 0)
    left_local = lax.dynamic_slice_in_dim(left_sizes, left_first, sectors_here)
    left_keep = positions[None, :] < left_local[:, None]
    right_keep = positions[None, :] < right_sizes[:, None]
    keep_mask = (left_keep[:, None, :, None] & right_keep[None, :, None, :]).astype(jnp.bfloat16)
    masked = psi * keep_mask
    acting_count = left_ops.shape[0] // 2
    order = jnp.argsort(1 - term_blocks, axis=0, stable=True)[:acting_count]
    ids_local = lax.dynamic_slice_in_dim(order, left_first, sectors_here, 1)
    sector_index = lax.broadcasted_iota(jnp.int32, (acting_count, sectors_here), 1)
    picked = left_ops[ids_local, sector_index]
    applied = jnp.einsum(
        "kaim,abmj->kabij", picked, masked, preferred_element_type=jnp.float32
    ).astype(jnp.bfloat16)
    arrived = lax.all_to_all(applied, "blk", split_axis=2, concat_axis=1, tiled=True)
    right_picked = right_ops[order]
    partial_value = jnp.einsum(
        "kabij,kablj->bail", arrived, right_picked, preferred_element_type=jnp.float32
    )
    summed = lax.psum_scatter(
        partial_value.astype(jnp.bfloat16), "op", scatter_dimension=1, tiled=True
    ).astype(jnp.float32)
    row_count = summed.shape[1]
    op_first = lax.axis_index("op") * row_count
    left_share = lax.dynamic_slice_in_dim(left_sizes, op_first, row_count)
    right_local = lax.dynamic_slice_in_dim(right_sizes, left_first, sectors_here)
    rows_keep = positions[None, :] < left_share[:, None]
    cols_keep = positions[None, :] < right_local[:, None]
    out_keep = (cols_keep[:, None, None, :] & rows_keep[None, :, :, None]).astype(jnp.float32)
    return (summed * out_keep).astype(jnp.bfloat16)


def solution(mesh):
    in_specs = (
        P(("parts", "blk"), None, None, None),
        P(("parts", "op"), "blk", None, None),
        P(("parts", "op"), "blk", None, None),
        P(("parts", "op"), None),
        P("parts"),
        P("parts"),
    )
    out_specs = P(("parts", "blk"), "op", None, None)
    nz, no = mesh.shape["blk"], mesh.shape["op"]
    body = shards if nz == no == 4 else wide_shards
    return jax.shard_map(body, mesh=mesh, in_specs=in_specs, out_specs=out_specs, check_vma=False)
```

```python
import functools

import jax
import jax.numpy as jnp
from jax import lax
from jax.experimental import pallas as pl
from jax.experimental.pallas import tpu as pltpu
from jax.sharding import PartitionSpec as P

ANY = pl.BlockSpec(memory_space=pl.ANY)
SMEM = pl.BlockSpec(memory_space=pltpu.SMEM)
VMEM = pl.BlockSpec(memory_space=pltpu.VMEM)
PARAMS = pltpu.CompilerParams(vmem_limit_bytes=32 * 1024 * 1024)
ID_ROWS = 16


def acting_terms(blocks_ref, sector):
    first = jnp.int32(0)
    second = jnp.int32(0)
    for term in reversed(range(blocks_ref.shape[0])):
        acts = blocks_ref[term, sector] > 0
        second = jnp.where(acts, first, second)
        first = jnp.where(acts, term, first)
    return first, second


def place():
    op = lax.axis_index("op")
    return lax.axis_index("blk"), lax.shift_right_logical(op, 1), jnp.bitwise_and(op, 1)


def is_home():
    z, _, c = place()
    return c == jnp.bitwise_and(z, 1)


def pack_kernel(blocks_ref, psi_ref, left_ref, left_out, far_out, near_out, sem):
    z, x, _ = place()
    sectors, tile = psi_ref.shape[0], psi_ref.shape[-1]
    row = lax.broadcasted_iota(jnp.int32, (ID_ROWS, tile), 0)
    ids = jnp.zeros((ID_ROWS, tile), jnp.float32)
    copies = []
    for local in range(sectors):
        for term in acting_terms(blocks_ref, z * sectors + local):
            spot = len(copies)
            ids = jnp.where(row == spot, term.astype(jnp.float32), ids)
            copies.append(
                pltpu.make_async_copy(
                    left_ref.at[term, local], left_out.at[pl.ds(spot * tile, tile)], sem.at[spot]
                )
            )
    far = jnp.bitwise_xor(z, jnp.where(is_home(), 2, 3)) * sectors + x
    near = pl.ds(jnp.bitwise_xor(z, 1) * sectors, sectors)
    for columns, out in ((far, far_out), (near, near_out)):
        copies.append(pltpu.make_async_copy(psi_ref.at[:, columns], out, sem.at[len(copies)]))
    for copy in copies:
        copy.start()
    left_out[pl.ds(2 * sectors * tile, ID_ROWS)] = ids.astype(jnp.bfloat16)
    for copy in copies:
        copy.wait()


def partial_sums(z, distance, sizes, columns, psi, lefts, rights, store):
    lsize_ref, rsize_ref = sizes
    sectors = len(columns)
    owner = jnp.bitwise_xor(z, distance)
    for a in range(sectors):
        blocks = [psi(a, side) for side in range(sectors)]
        tile = blocks[0].shape[-1]
        rows = lax.broadcasted_iota(jnp.int32, (tile, tile), 0)
        lanes = lax.broadcasted_iota(jnp.int32, (tile, tile), 1)
        height = lsize_ref[owner * sectors + a]
        keeps = [(rows < height) & (lanes < rsize_ref[z * sectors + b]) for b in columns]
        wide = jnp.concatenate(
            [
                jnp.where(keep, block.astype(jnp.float32), 0.0).astype(jnp.bfloat16)
                for keep, block in zip(keeps, blocks)
            ],
            axis=1,
        )
        applied = []
        for left in lefts:
            both = jnp.dot(left(a), wide, preferred_element_type=jnp.float32).astype(jnp.bfloat16)
            applied += [both[:tile], both[tile:]]
        for side, b in enumerate(columns):
            picked = [right(a, slot, b) for right in rights for slot in range(2)]
            column = [part[:, side * tile : (side + 1) * tile] for part in applied]
            total = lax.dot_general(
                jnp.concatenate(column, axis=1),
                jnp.concatenate(picked, axis=1),
                (((1,), (1,)), ((), ())),
                preferred_element_type=jnp.float32,
            )
            store(b, a, jnp.where(keeps[side], total, 0.0))


def message(ref, right_ref):
    terms, sectors, tile = right_ref.shape[0], right_ref.shape[1], right_ref.shape[-1]
    ids = ref[pl.ds(2 * sectors * tile, ID_ROWS)].astype(jnp.float32)

    def left(a):
        return ref[pl.ds(2 * a * tile, 2 * tile)]

    def right(a, slot, b):
        spot = 2 * a + slot
        term = jnp.broadcast_to(ids[spot : spot + 1], (tile, tile))
        block = right_ref[0, b].astype(jnp.float32)
        for t in range(1, terms):
            block = jnp.where(term == t, right_ref[t, b].astype(jnp.float32), block)
        return block.astype(jnp.bfloat16)

    return left, right


def near_kernel(lsize_ref, rsize_ref, blocks_ref, *rest):
    psi_ref, left_ref, swapped, direct_a, direct_b, psi_near = rest[:6]
    right_own, right_other, out_ref = rest[6:]
    z, _, _ = place()
    sectors = out_ref.shape[0]
    sizes, columns = (lsize_ref, rsize_ref), range(sectors)

    def store(b, a, total):
        out_ref[b, a] = total

    @pl.when(is_home())
    def _():
        terms = [acting_terms(blocks_ref, z * sectors + a) for a in range(sectors)]
        left, right = message(swapped, right_other)
        partial_sums(
            z, 0, sizes, columns, lambda a, b: psi_ref[a, z * sectors + b],
            [lambda a: jnp.concatenate([left_ref[term, a] for term in terms[a]], axis=0), left],
            [lambda a, slot, b: right_own[terms[a][slot], b], right],
            store,
        )

    @pl.when(jnp.logical_not(is_home()))
    def _():
        pairs = [message(direct_b, right_own), message(direct_a, right_other)]
        lefts, rights = zip(*pairs)
        partial_sums(z, 1, sizes, columns, lambda a, b: psi_near[a, b], lefts, rights, store)


def far_kernel(at_home, lsize_ref, rsize_ref, *rest):
    first, second, psi_same, psi_other, right_own, right_other, near_ref = rest[:7]
    sent_ref, out_ref = rest[7:]
    z, x, _ = place()
    columns = (x, 1 - x)
    far_leaves = lax.shift_right_logical(z, 1) == x

    def psi(a, side):
        return (psi_same, psi_other)[side][a]

    def store_sent(b, a, total):
        sent_ref[b, a] = total.astype(sent_ref.dtype)

    def store_kept(b, a, total):
        out_ref[b, a] = total
        sent_ref[b, a] = near_ref[b, a].astype(sent_ref.dtype)

    for leaves, store in ((True, store_sent), (False, store_kept)):

        @pl.when((is_home() == at_home) & (far_leaves == leaves))
        def _(store=store):
            lefts, rights = zip(message(first, right_own), message(second, right_other))
            distance = 2 if at_home else 3
            partial_sums(z, distance, (lsize_ref, rsize_ref), columns, psi, lefts, rights, store)


def shards(psi, left_ops, right_ops, term_blocks, left_sizes, right_sizes):
    n = 4
    sectors, tile = psi.shape[0], psi.shape[-1]
    block = functools.partial(jax.ShapeDtypeStruct, dtype=jnp.bfloat16)
    out_shape = (sectors, sectors, tile, tile)

    def over_op(array, step):
        return lax.ppermute(array, "op", [(o, o ^ step) for o in range(n)])

    def over_both(array, target):
        pairs = []
        for z in range(n):
            for o in range(n):
                to = target(z, o >> 1, o & 1, o & 1 == z & 1)
                if to is not None:
                    pairs.append((z * n + o, to[0] * n + 2 * to[1] + to[2]))
        return lax.ppermute(array, ("blk", "op"), pairs)

    def over_z(array, home_step, other_step):
        def target(z, x, c, home):
            step = home_step if home else other_step
            return None if step is None else (z ^ step, x, z & 1)

        return over_both(array, target)

    left_sent, far_sent, near_sent = pl.pallas_call(
        pack_kernel,
        out_shape=[
            block((2 * sectors * tile + ID_ROWS, tile)),
            block((sectors, tile, tile)),
            block(out_shape),
        ],
        in_specs=[SMEM, ANY, ANY],
        out_specs=[VMEM] * 3,
        scratch_shapes=[pltpu.SemaphoreType.DMA((2 * sectors + 2,))],
        compiler_params=pltpu.CompilerParams(vmem_limit_bytes=60 * 1024 * 1024),
        name="pack",
    )(term_blocks, psi, left_ops)
    direct_a = over_z(left_sent, 2, 1)
    direct_b = over_z(left_sent, 1, 2)
    far_same = over_z(far_sent, 2, 3)
    far_other = over_op(far_same, 2)
    psi_near = over_z(near_sent, 1, None)
    passed_a = over_z(direct_a, 1, None)
    passed_b = over_z(direct_b, 1, None)
    swapped = over_op(left_sent, 1)
    held, _ = lax.optimization_barrier((right_ops, left_sent))
    rights = [right_ops, over_op(held, 1)]

    def apply(kernel, name, outs, scalars, *operands):
        return pl.pallas_call(
            kernel,
            out_shape=[jax.ShapeDtypeStruct(out_shape, dtype) for dtype in outs],
            in_specs=[SMEM] * len(scalars) + [VMEM] * len(operands),
            out_specs=[VMEM] * len(outs),
            compiler_params=PARAMS,
            cost_estimate=pl.CostEstimate(
                flops=64 * tile**3 * sectors**2, bytes_accessed=2**20, transcendentals=0
            ),
            name=name,
        )(*scalars, *operands)

    sizes = (left_sizes, right_sizes)
    (near,) = apply(
        near_kernel, "near", [jnp.float32], sizes + (term_blocks,),
        psi, left_ops, swapped, direct_a, direct_b, psi_near, *rights,
    )

    def far_part(at_home, first, second):
        sent, far = apply(
            functools.partial(far_kernel, at_home), "far_home" if at_home else "far_other",
            [jnp.bfloat16, jnp.float32], sizes, first, second, far_same, far_other, *rights, near,
        )
        arrived = over_both(
            sent, lambda z, x, c, home: (z, 1 - x, c) if home == at_home else None
        )
        return far, arrived

    home_far, home_arrived = far_part(True, direct_a, direct_b)
    other_far, other_arrived = far_part(False, passed_a, passed_b)
    z, op = lax.axis_index("blk"), lax.axis_index("op")
    home = z % 2 == op % 2
    far = jnp.where(home, home_far, other_far)
    arrived = jnp.where(home, home_arrived, other_arrived)
    kept = jnp.where(z // 2 == op // 2, near, far)
    return (kept + arrived.astype(jnp.float32)).astype(jnp.bfloat16)


def wide_shards(psi, left_ops, right_ops, term_blocks, left_sizes, right_sizes):
    sectors_here = psi.shape[0]
    tile_size = psi.shape[2]
    left_first = lax.axis_index("blk") * sectors_here
    positions = lax.broadcasted_iota(jnp.int32, (tile_size,), 0)
    left_local = lax.dynamic_slice_in_dim(left_sizes, left_first, sectors_here)
    left_keep = positions[None, :] < left_local[:, None]
    right_keep = positions[None, :] < right_sizes[:, None]
    keep_mask = (left_keep[:, None, :, None] & right_keep[None, :, None, :]).astype(jnp.bfloat16)
    masked = psi * keep_mask
    acting_count = left_ops.shape[0] // 2
    order = jnp.argsort(1 - term_blocks, axis=0, stable=True)[:acting_count]
    ids_local = lax.dynamic_slice_in_dim(order, left_first, sectors_here, 1)
    sector_index = lax.broadcasted_iota(jnp.int32, (acting_count, sectors_here), 1)
    picked = left_ops[ids_local, sector_index]
    applied = jnp.einsum(
        "kaim,abmj->kabij", picked, masked, preferred_element_type=jnp.float32
    ).astype(jnp.bfloat16)
    arrived = lax.all_to_all(applied, "blk", split_axis=2, concat_axis=1, tiled=True)
    right_picked = right_ops[order]
    partial_value = jnp.einsum(
        "kabij,kablj->bail", arrived, right_picked, preferred_element_type=jnp.float32
    )
    summed = lax.psum_scatter(
        partial_value.astype(jnp.bfloat16), "op", scatter_dimension=1, tiled=True
    ).astype(jnp.float32)
    row_count = summed.shape[1]
    op_first = lax.axis_index("op") * row_count
    left_share = lax.dynamic_slice_in_dim(left_sizes, op_first, row_count)
    right_local = lax.dynamic_slice_in_dim(right_sizes, left_first, sectors_here)
    rows_keep = positions[None, :] < left_share[:, None]
    cols_keep = positions[None, :] < right_local[:, None]
    out_keep = (cols_keep[:, None, None, :] & rows_keep[None, :, :, None]).astype(jnp.float32)
    return (summed * out_keep).astype(jnp.bfloat16)


def solution(mesh):
    in_specs = (
        P(("parts", "blk"), None, None, None),
        P(("parts", "op"), "blk", None, None),
        P(("parts", "op"), "blk", None, None),
        P(("parts", "op"), None),
        P("parts"),
        P("parts"),
    )
    out_specs = P(("parts", "blk"), "op", None, None)
    nz, no = mesh.shape["blk"], mesh.shape["op"]
    body = shards if nz == no == 4 else wide_shards
    return jax.shard_map(body, mesh=mesh, in_specs=in_specs, out_specs=out_specs, check_vma=False)
```

```python
import functools

import jax
import jax.numpy as jnp
from jax import lax
from jax.experimental import pallas as pl
from jax.experimental.pallas import tpu as pltpu
from jax.sharding import PartitionSpec as P

ANY = pl.BlockSpec(memory_space=pl.ANY)
SMEM = pl.BlockSpec(memory_space=pltpu.SMEM)
VMEM = pl.BlockSpec(memory_space=pltpu.VMEM)
PARAMS = pltpu.CompilerParams(vmem_limit_bytes=32 * 1024 * 1024)
ID_ROWS = 16


def acting_terms(blocks_ref, sector):
    first = jnp.int32(0)
    second = jnp.int32(0)
    for term in reversed(range(blocks_ref.shape[0])):
        acts = blocks_ref[term, sector] > 0
        second = jnp.where(acts, first, second)
        first = jnp.where(acts, term, first)
    return first, second


def place():
    op = lax.axis_index("op")
    return lax.axis_index("blk"), lax.shift_right_logical(op, 1), jnp.bitwise_and(op, 1)


def is_home():
    z, _, c = place()
    return c == jnp.bitwise_and(z, 1)


def pack_kernel(blocks_ref, psi_ref, left_ref, left_out, side_out, far_out, sem):
    z, _, _ = place()
    sectors, tile = psi_ref.shape[0], psi_ref.shape[-1]
    count = 2 * sectors
    row = lax.broadcasted_iota(jnp.int32, (ID_ROWS, tile), 0)
    ids = jnp.zeros((ID_ROWS, tile), jnp.float32)
    picked = []
    for local in range(sectors):
        for term in acting_terms(blocks_ref, z * sectors + local):
            ids = jnp.where(row == len(picked), term.astype(jnp.float32), ids)
            picked.append(left_ref.at[term, local])
    near = jnp.bitwise_xor(z, 1) * sectors
    asked = [psi_ref.at[a, near + b] for a in range(sectors) for b in range(sectors)]

    def copies(sources, out, first):
        return [
            pltpu.make_async_copy(source, out.at[pl.ds(spot * tile, tile)], sem.at[first + spot])
            for spot, source in enumerate(sources)
        ]

    far = pl.ds(jnp.bitwise_xor(z, jnp.where(is_home(), 2, 3)) * sectors, sectors)
    plain = copies(picked, left_out, 0)
    plain.append(pltpu.make_async_copy(psi_ref.at[:, far], far_out, sem.at[2 * count]))
    for copy in plain:
        copy.start()
    for at_home, sources in ((True, asked), (False, picked)):

        @pl.when(is_home() == at_home)
        def _(sources=sources):
            for copy in copies(sources, side_out, count):
                copy.start()

    for out in (left_out, side_out):
        out[pl.ds(count * tile, ID_ROWS)] = ids.astype(jnp.bfloat16)
    for copy in plain + copies(picked, side_out, count):
        copy.wait()


def keep_mask(z, distance, sizes, a, b, sectors, tile):
    lsize_ref, rsize_ref = sizes
    rows = lax.broadcasted_iota(jnp.int32, (tile, tile), 0)
    lanes = lax.broadcasted_iota(jnp.int32, (tile, tile), 1)
    height = lsize_ref[jnp.bitwise_xor(z, distance) * sectors + a]
    return (rows < height) & (lanes < rsize_ref[z * sectors + b])


def wide_psi(z, distance, sizes, a, blocks):
    tile = blocks[0].shape[-1]
    cut = []
    for b, block in enumerate(blocks):
        keep = keep_mask(z, distance, sizes, a, b, len(blocks), tile)
        cut.append(jnp.where(keep, block.astype(jnp.float32), 0.0).astype(jnp.bfloat16))
    return jnp.concatenate(cut, axis=1)


def partial_sums(z, distance, sizes, sectors, psi, lefts, rights, store):
    for a in range(sectors):
        wide = psi(a)
        tile = wide.shape[0]
        applied = []
        for left in lefts:
            both = jnp.dot(left(a), wide, preferred_element_type=jnp.float32).astype(jnp.bfloat16)
            applied += [both[:tile], both[tile:]]
        for b in range(sectors):
            picked = [right(a, slot, b) for right in rights for slot in range(2)]
            column = [part[:, b * tile : (b + 1) * tile] for part in applied]
            total = lax.dot_general(
                jnp.concatenate(column, axis=1),
                jnp.concatenate(picked, axis=1),
                (((1,), (1,)), ((), ())),
                preferred_element_type=jnp.float32,
            )
            keep = keep_mask(z, distance, sizes, a, b, sectors, tile)
            store(b, a, jnp.where(keep, total, 0.0))


def message(ref, right_ref):
    terms, sectors, tile = right_ref.shape[0], right_ref.shape[1], right_ref.shape[-1]
    ids = ref[pl.ds(2 * sectors * tile, ID_ROWS)].astype(jnp.float32)

    def left(a):
        return ref[pl.ds(2 * a * tile, 2 * tile)]

    def right(a, slot, b):
        spot = 2 * a + slot
        term = jnp.broadcast_to(ids[spot : spot + 1], (tile, tile))
        block = right_ref[0, b].astype(jnp.float32)
        for t in range(1, terms):
            block = jnp.where(term == t, right_ref[t, b].astype(jnp.float32), block)
        return block.astype(jnp.bfloat16)

    return left, right


def near_kernel(lsize_ref, rsize_ref, blocks_ref, *rest):
    psi_ref, left_ref, side, direct_a, direct_b, psi_far, right_hbm, right_other = rest[:8]
    out_ref, wide_ref, right_own, sem = rest[8:]
    z, _, _ = place()
    sectors, tile = out_ref.shape[0], out_ref.shape[-1]
    sizes = (lsize_ref, rsize_ref)
    copy = pltpu.make_async_copy(right_hbm, right_own, sem)
    copy.start()
    distance = jnp.where(is_home(), 2, 3)
    for a in range(sectors):
        wide_ref[a] = wide_psi(z, distance, sizes, a, [psi_far[a, b] for b in range(sectors)])
    copy.wait()

    def store(b, a, total):
        out_ref[b, a] = total

    @pl.when(is_home())
    def _():
        terms = [acting_terms(blocks_ref, z * sectors + a) for a in range(sectors)]
        left, right = message(side, right_other)

        def psi(a):
            return wide_psi(z, 0, sizes, a, [psi_ref[a, z * sectors + b] for b in range(sectors)])

        partial_sums(
            z, 0, sizes, sectors, psi,
            [lambda a: jnp.concatenate([left_ref[term, a] for term in terms[a]], axis=0), left],
            [lambda a, slot, b: right_own[terms[a][slot], b], right],
            store,
        )

    @pl.when(jnp.logical_not(is_home()))
    def _():
        lefts, rights = zip(message(direct_b, right_own), message(direct_a, right_other))

        def psi(a):
            spots = [pl.ds((sectors * a + b) * tile, tile) for b in range(sectors)]
            return wide_psi(z, 1, sizes, a, [side[spot] for spot in spots])

        partial_sums(z, 1, sizes, sectors, psi, lefts, rights, store)


def far_kernel(lsize_ref, rsize_ref, *rest):
    direct_a, direct_b, passed_a, passed_b, wide_ref, right_own, right_other, near_ref = rest[:8]
    sent_ref, out_ref = rest[8:]
    z, x, _ = place()
    sectors = out_ref.shape[0]
    far_leaves = lax.shift_right_logical(z, 1) == x

    def store_sent(b, a, total):
        sent_ref[b, a] = total.astype(sent_ref.dtype)

    def store_kept(b, a, total):
        out_ref[b, a] = total
        sent_ref[b, a] = near_ref[b, a].astype(sent_ref.dtype)

    for leaves, store in ((True, store_sent), (False, store_kept)):
        for at_home, distance, first, second in (
            (True, 2, direct_a, direct_b),
            (False, 3, passed_a, passed_b),
        ):

            @pl.when((is_home() == at_home) & (far_leaves == leaves))
            def _(store=store, distance=distance, first=first, second=second):
                lefts, rights = zip(message(first, right_own), message(second, right_other))
                sizes = (lsize_ref, rsize_ref)
                partial_sums(
                    z, distance, sizes, sectors, lambda a: wide_ref[a], lefts, rights, store
                )


def shards(psi, left_ops, right_ops, term_blocks, left_sizes, right_sizes):
    n = 4
    sectors, tile = psi.shape[0], psi.shape[-1]
    block = functools.partial(jax.ShapeDtypeStruct, dtype=jnp.bfloat16)
    out_shape = (sectors, sectors, tile, tile)
    message_shape = (2 * sectors * tile + ID_ROWS, tile)

    def over_op(array, step):
        return lax.ppermute(array, "op", [(o, o ^ step) for o in range(n)])

    def over_z(array, home_step, other_step):
        pairs = []
        for z in range(n):
            for o in range(n):
                step = home_step if o & 1 == z & 1 else other_step
                pairs.append((z * n + o, (z ^ step) * n + (o & 2) + (z & 1)))
        return lax.ppermute(array, ("blk", "op"), pairs)

    psi_hbm, left_hbm, right_hbm, blocks_hbm = [
        pltpu.with_memory_space_constraint(array, pltpu.HBM)
        for array in (psi, left_ops, right_ops, term_blocks)
    ]
    left_sent, side_sent, far_sent = pl.pallas_call(
        pack_kernel,
        out_shape=[block(message_shape), block(message_shape), block(out_shape)],
        in_specs=[SMEM, ANY, ANY],
        out_specs=[VMEM] * 3,
        scratch_shapes=[pltpu.SemaphoreType.DMA((4 * sectors + 1,))],
        compiler_params=PARAMS,
        name="pack",
    )(blocks_hbm, psi_hbm, left_hbm)
    direct_a = over_z(left_sent, 2, 1)
    direct_b = over_z(left_sent, 1, 2)
    psi_far = over_z(far_sent, 2, 3)
    side = over_z(side_sent, 1, 0)
    passed_a = over_z(direct_a, 1, 0)
    passed_b = over_z(direct_b, 1, 0)
    held, _ = lax.optimization_barrier((right_ops, left_sent))
    right_other = over_op(held, 1)

    def apply(kernel, name, outs, scalars, operands, scratch):
        return pl.pallas_call(
            kernel,
            out_shape=outs,
            in_specs=[SMEM] * len(scalars) + [spec for _, spec in operands],
            out_specs=[VMEM] * len(outs),
            scratch_shapes=scratch,
            compiler_params=PARAMS,
            cost_estimate=pl.CostEstimate(
                flops=64 * tile**3 * sectors**2, bytes_accessed=2**20, transcendentals=0
            ),
            name=name,
        )(*scalars, *[array for array, _ in operands])

    sizes = (left_sizes, right_sizes)
    total = jax.ShapeDtypeStruct(out_shape, jnp.float32)
    inside = [psi, left_ops, side, direct_a, direct_b, psi_far]
    near, wide, right_own = apply(
        near_kernel, "near",
        [total, block((sectors, tile, sectors * tile)), block(right_ops.shape)],
        sizes + (term_blocks,),
        [(array, VMEM) for array in inside] + [(right_hbm, ANY), (right_other, VMEM)],
        [pltpu.SemaphoreType.DMA(())],
    )
    inside = [direct_a, direct_b, passed_a, passed_b, wide, right_own, right_other, near]
    sent, far = apply(
        far_kernel, "far", [block(out_shape), total], sizes,
        [(array, VMEM) for array in inside], [],
    )
    arrived = over_op(sent, 2)
    kept = jnp.where(lax.axis_index("blk") // 2 == lax.axis_index("op") // 2, near, far)
    return (kept + arrived.astype(jnp.float32)).astype(jnp.bfloat16)


def wide_shards(psi, left_ops, right_ops, term_blocks, left_sizes, right_sizes):
    sectors_here = psi.shape[0]
    tile_size = psi.shape[2]
    left_first = lax.axis_index("blk") * sectors_here
    positions = lax.broadcasted_iota(jnp.int32, (tile_size,), 0)
    left_local = lax.dynamic_slice_in_dim(left_sizes, left_first, sectors_here)
    left_keep = positions[None, :] < left_local[:, None]
    right_keep = positions[None, :] < right_sizes[:, None]
    keep_mask = (left_keep[:, None, :, None] & right_keep[None, :, None, :]).astype(jnp.bfloat16)
    masked = psi * keep_mask
    acting_count = left_ops.shape[0] // 2
    order = jnp.argsort(1 - term_blocks, axis=0, stable=True)[:acting_count]
    ids_local = lax.dynamic_slice_in_dim(order, left_first, sectors_here, 1)
    sector_index = lax.broadcasted_iota(jnp.int32, (acting_count, sectors_here), 1)
    picked = left_ops[ids_local, sector_index]
    applied = jnp.einsum(
        "kaim,abmj->kabij", picked, masked, preferred_element_type=jnp.float32
    ).astype(jnp.bfloat16)
    arrived = lax.all_to_all(applied, "blk", split_axis=2, concat_axis=1, tiled=True)
    right_picked = right_ops[order]
    partial_value = jnp.einsum(
        "kabij,kablj->bail", arrived, right_picked, preferred_element_type=jnp.float32
    )
    summed = lax.psum_scatter(
        partial_value.astype(jnp.bfloat16), "op", scatter_dimension=1, tiled=True
    ).astype(jnp.float32)
    row_count = summed.shape[1]
    op_first = lax.axis_index("op") * row_count
    left_share = lax.dynamic_slice_in_dim(left_sizes, op_first, row_count)
    right_local = lax.dynamic_slice_in_dim(right_sizes, left_first, sectors_here)
    rows_keep = positions[None, :] < left_share[:, None]
    cols_keep = positions[None, :] < right_local[:, None]
    out_keep = (cols_keep[:, None, None, :] & rows_keep[None, :, :, None]).astype(jnp.float32)
    return (summed * out_keep).astype(jnp.bfloat16)


def solution(mesh):
    in_specs = (
        P(("parts", "blk"), None, None, None),
        P(("parts", "op"), "blk", None, None),
        P(("parts", "op"), "blk", None, None),
        P(("parts", "op"), None),
        P("parts"),
        P("parts"),
    )
    out_specs = P(("parts", "blk"), "op", None, None)
    nz, no = mesh.shape["blk"], mesh.shape["op"]
    body = shards if nz == no == 4 else wide_shards
    return jax.shard_map(body, mesh=mesh, in_specs=in_specs, out_specs=out_specs, check_vma=False)
```

```python
import functools

import jax
import jax.numpy as jnp
from jax import lax
from jax.experimental import pallas as pl
from jax.experimental.pallas import tpu as pltpu
from jax.sharding import PartitionSpec as P

ANY = pl.BlockSpec(memory_space=pl.ANY)
SMEM = pl.BlockSpec(memory_space=pltpu.SMEM)
VMEM = pl.BlockSpec(memory_space=pltpu.VMEM)
PARAMS = pltpu.CompilerParams(vmem_limit_bytes=32 * 1024 * 1024)
ID_ROWS = 16


def acting_terms(blocks_ref, sector):
    first = jnp.int32(0)
    second = jnp.int32(0)
    for term in reversed(range(blocks_ref.shape[0])):
        acts = blocks_ref[term, sector] > 0
        second = jnp.where(acts, first, second)
        first = jnp.where(acts, term, first)
    return first, second


def place():
    op = lax.axis_index("op")
    return lax.axis_index("blk"), lax.shift_right_logical(op, 1), jnp.bitwise_and(op, 1)


def is_home():
    z, _, c = place()
    return c == jnp.bitwise_and(z, 1)


def pack_kernel(blocks_ref, psi_ref, left_ref, right_ref, *rest):
    left_out, side_out, far_out, right_out, sem = rest
    z, x, _ = place()
    sectors, tile = psi_ref.shape[0], psi_ref.shape[-1]
    count = 2 * sectors
    row = lax.broadcasted_iota(jnp.int32, (ID_ROWS, tile), 0)
    ids = jnp.zeros((ID_ROWS, tile), jnp.float32)
    picked = []
    for local in range(sectors):
        for term in acting_terms(blocks_ref, z * sectors + local):
            ids = jnp.where(row == len(picked), term.astype(jnp.float32), ids)
            picked.append(left_ref.at[term, local])
    near = jnp.bitwise_xor(z, 1) * sectors
    asked = [psi_ref.at[a, near + b] for a in range(sectors) for b in range(sectors)]

    def copies(sources, out, first):
        return [
            pltpu.make_async_copy(source, out.at[pl.ds(spot * tile, tile)], sem.at[first + spot])
            for spot, source in enumerate(sources)
        ]

    far = jnp.bitwise_xor(z, jnp.where(is_home(), 2, 3)) * sectors + x
    plain = copies(picked, left_out, 0)
    plain.append(pltpu.make_async_copy(psi_ref.at[:, far], far_out, sem.at[2 * count]))
    plain.append(pltpu.make_async_copy(right_ref, right_out, sem.at[2 * count + 1]))
    for copy in plain:
        copy.start()
    for at_home, sources in ((True, asked), (False, picked)):

        @pl.when(is_home() == at_home)
        def _(sources=sources):
            for copy in copies(sources, side_out, count):
                copy.start()

    for out in (left_out, side_out):
        out[pl.ds(count * tile, ID_ROWS)] = ids.astype(jnp.bfloat16)
    for copy in plain + copies(picked, side_out, count):
        copy.wait()


def keep_mask(z, distance, sizes, a, b, sectors, tile):
    lsize_ref, rsize_ref = sizes
    rows = lax.broadcasted_iota(jnp.int32, (tile, tile), 0)
    lanes = lax.broadcasted_iota(jnp.int32, (tile, tile), 1)
    height = lsize_ref[jnp.bitwise_xor(z, distance) * sectors + a]
    return (rows < height) & (lanes < rsize_ref[z * sectors + b])


def wide_psi(z, distance, sizes, a, columns, blocks):
    tile = blocks[0].shape[-1]
    cut = []
    for b, block in zip(columns, blocks):
        keep = keep_mask(z, distance, sizes, a, b, len(blocks), tile)
        cut.append(jnp.where(keep, block.astype(jnp.float32), 0.0).astype(jnp.bfloat16))
    return jnp.concatenate(cut, axis=1)


def partial_sums(z, distance, sizes, columns, psi, lefts, rights, store):
    sectors = len(columns)
    for a in range(sectors):
        wide = psi(a)
        tile = wide.shape[0]
        applied = []
        for left in lefts:
            both = jnp.dot(left(a), wide, preferred_element_type=jnp.float32).astype(jnp.bfloat16)
            applied += [both[:tile], both[tile:]]
        for side, b in enumerate(columns):
            picked = [right(a, slot, b) for right in rights for slot in range(2)]
            column = [part[:, side * tile : (side + 1) * tile] for part in applied]
            total = lax.dot_general(
                jnp.concatenate(column, axis=1),
                jnp.concatenate(picked, axis=1),
                (((1,), (1,)), ((), ())),
                preferred_element_type=jnp.float32,
            )
            keep = keep_mask(z, distance, sizes, a, b, sectors, tile)
            store(b, a, jnp.where(keep, total, 0.0))


def message(ref, right_ref):
    terms, sectors, tile = right_ref.shape[0], right_ref.shape[1], right_ref.shape[-1]
    ids = ref[pl.ds(2 * sectors * tile, ID_ROWS)].astype(jnp.float32)

    def left(a):
        return ref[pl.ds(2 * a * tile, 2 * tile)]

    def right(a, slot, b):
        spot = 2 * a + slot
        term = jnp.broadcast_to(ids[spot : spot + 1], (tile, tile))
        block = right_ref[0, b].astype(jnp.float32)
        for t in range(1, terms):
            block = jnp.where(term == t, right_ref[t, b].astype(jnp.float32), block)
        return block.astype(jnp.bfloat16)

    return left, right


def mask_kernel(lsize_ref, rsize_ref, psi_same, psi_other, wide_ref):
    z, x, _ = place()
    far = jnp.where(is_home(), 2, 3)
    for a in range(psi_same.shape[0]):
        blocks = [psi_same[a], psi_other[a]]
        wide_ref[a] = wide_psi(z, far, (lsize_ref, rsize_ref), a, (x, 1 - x), blocks)


def near_kernel(lsize_ref, rsize_ref, blocks_ref, *rest):
    psi_ref, left_ref, side, direct_a, direct_b, right_own, right_other, out_ref = rest
    z, _, _ = place()
    sectors, tile = out_ref.shape[0], out_ref.shape[-1]
    sizes, columns = (lsize_ref, rsize_ref), range(sectors)

    def store(b, a, total):
        out_ref[b, a] = total

    def masked(distance, a, blocks):
        return wide_psi(z, distance, sizes, a, columns, blocks)

    @pl.when(is_home())
    def _():
        terms = [acting_terms(blocks_ref, z * sectors + a) for a in columns]
        left, right = message(side, right_other)
        partial_sums(
            z, 0, sizes, columns,
            lambda a: masked(0, a, [psi_ref[a, z * sectors + b] for b in columns]),
            [lambda a: jnp.concatenate([left_ref[term, a] for term in terms[a]], axis=0), left],
            [lambda a, slot, b: right_own[terms[a][slot], b], right],
            store,
        )

    @pl.when(jnp.logical_not(is_home()))
    def _():
        lefts, rights = zip(message(direct_b, right_own), message(direct_a, right_other))

        def psi(a):
            return masked(1, a, [side[pl.ds((sectors * a + b) * tile, tile)] for b in columns])

        partial_sums(z, 1, sizes, columns, psi, lefts, rights, store)


def far_kernel(lsize_ref, rsize_ref, *rest):
    direct_a, direct_b, passed_a, passed_b, right_own, right_other = rest[:6]
    near_ref, wide_ref, sent_ref, out_ref = rest[6:]
    z, x, _ = place()
    columns = (x, 1 - x)
    far_leaves = lax.shift_right_logical(z, 1) == x

    def store_sent(b, a, total):
        sent_ref[b, a] = total.astype(sent_ref.dtype)

    def store_kept(b, a, total):
        out_ref[b, a] = total
        sent_ref[b, a] = near_ref[b, a].astype(sent_ref.dtype)

    for leaves, store in ((True, store_sent), (False, store_kept)):
        for at_home, distance, first, second in (
            (True, 2, direct_a, direct_b),
            (False, 3, passed_a, passed_b),
        ):

            @pl.when((is_home() == at_home) & (far_leaves == leaves))
            def _(store=store, distance=distance, first=first, second=second):
                lefts, rights = zip(message(first, right_own), message(second, right_other))
                sizes = (lsize_ref, rsize_ref)
                partial_sums(
                    z, distance, sizes, columns, lambda a: wide_ref[a], lefts, rights, store
                )


def shards(psi, left_ops, right_ops, term_blocks, left_sizes, right_sizes):
    n = 4
    sectors, tile = psi.shape[0], psi.shape[-1]
    block = functools.partial(jax.ShapeDtypeStruct, dtype=jnp.bfloat16)
    out_shape = (sectors, sectors, tile, tile)
    message_shape = (2 * sectors * tile + ID_ROWS, tile)

    def over_op(array, step):
        return lax.ppermute(array, "op", [(o, o ^ step) for o in range(n)])

    def over_z(array, home_step, other_step):
        pairs = []
        for z in range(n):
            for o in range(n):
                step = home_step if o & 1 == z & 1 else other_step
                pairs.append((z * n + o, (z ^ step) * n + (o & 2) + (z & 1)))
        return lax.ppermute(array, ("blk", "op"), pairs)

    psi_hbm, left_hbm, right_hbm, blocks_hbm = [
        pltpu.with_memory_space_constraint(array, pltpu.HBM)
        for array in (psi, left_ops, right_ops, term_blocks)
    ]
    left_sent, side_sent, far_sent, right_own = pl.pallas_call(
        pack_kernel,
        out_shape=[
            block(message_shape),
            block(message_shape),
            block((sectors, tile, tile)),
            block(right_ops.shape),
        ],
        in_specs=[SMEM, ANY, ANY, ANY],
        out_specs=[VMEM] * 4,
        scratch_shapes=[pltpu.SemaphoreType.DMA((4 * sectors + 2,))],
        compiler_params=PARAMS,
        name="pack",
    )(blocks_hbm, psi_hbm, left_hbm, right_hbm)
    direct_a = over_z(left_sent, 2, 1)
    direct_b = over_z(left_sent, 1, 2)
    far_same = over_z(far_sent, 2, 3)
    far_other = over_op(far_same, 2)
    side = over_z(side_sent, 1, 0)
    passed_a = over_z(direct_a, 1, 0)
    passed_b = over_z(direct_b, 1, 0)
    right_other = over_op(right_own, 1)

    def apply(kernel, name, outs, scalars, operands):
        return pl.pallas_call(
            kernel,
            out_shape=outs,
            in_specs=[SMEM] * len(scalars) + [VMEM] * len(operands),
            out_specs=[VMEM] * len(outs),
            compiler_params=PARAMS,
            cost_estimate=pl.CostEstimate(
                flops=64 * tile**3 * sectors**2, bytes_accessed=2**20, transcendentals=0
            ),
            name=name,
        )(*scalars, *operands)

    sizes = (left_sizes, right_sizes)
    rights = [right_own, right_other]
    total = jax.ShapeDtypeStruct(out_shape, jnp.float32)
    (near,) = apply(
        near_kernel, "near", [total], sizes + (term_blocks,),
        [psi, left_ops, side, direct_a, direct_b] + rights,
    )
    (wide,) = apply(
        mask_kernel, "mask", [block((sectors, tile, sectors * tile))], sizes,
        [far_same, far_other],
    )
    sent, far = apply(
        far_kernel, "far", [block(out_shape), total], sizes,
        [direct_a, direct_b, passed_a, passed_b] + rights + [near, wide],
    )
    arrived = over_op(sent, 2)
    kept = jnp.where(lax.axis_index("blk") // 2 == lax.axis_index("op") // 2, near, far)
    return (kept + arrived.astype(jnp.float32)).astype(jnp.bfloat16)


def wide_shards(psi, left_ops, right_ops, term_blocks, left_sizes, right_sizes):
    sectors_here = psi.shape[0]
    tile_size = psi.shape[2]
    left_first = lax.axis_index("blk") * sectors_here
    positions = lax.broadcasted_iota(jnp.int32, (tile_size,), 0)
    left_local = lax.dynamic_slice_in_dim(left_sizes, left_first, sectors_here)
    left_keep = positions[None, :] < left_local[:, None]
    right_keep = positions[None, :] < right_sizes[:, None]
    keep_mask = (left_keep[:, None, :, None] & right_keep[None, :, None, :]).astype(jnp.bfloat16)
    masked = psi * keep_mask
    acting_count = left_ops.shape[0] // 2
    order = jnp.argsort(1 - term_blocks, axis=0, stable=True)[:acting_count]
    ids_local = lax.dynamic_slice_in_dim(order, left_first, sectors_here, 1)
    sector_index = lax.broadcasted_iota(jnp.int32, (acting_count, sectors_here), 1)
    picked = left_ops[ids_local, sector_index]
    applied = jnp.einsum(
        "kaim,abmj->kabij", picked, masked, preferred_element_type=jnp.float32
    ).astype(jnp.bfloat16)
    arrived = lax.all_to_all(applied, "blk", split_axis=2, concat_axis=1, tiled=True)
    right_picked = right_ops[order]
    partial_value = jnp.einsum(
        "kabij,kablj->bail", arrived, right_picked, preferred_element_type=jnp.float32
    )
    summed = lax.psum_scatter(
        partial_value.astype(jnp.bfloat16), "op", scatter_dimension=1, tiled=True
    ).astype(jnp.float32)
    row_count = summed.shape[1]
    op_first = lax.axis_index("op") * row_count
    left_share = lax.dynamic_slice_in_dim(left_sizes, op_first, row_count)
    right_local = lax.dynamic_slice_in_dim(right_sizes, left_first, sectors_here)
    rows_keep = positions[None, :] < left_share[:, None]
    cols_keep = positions[None, :] < right_local[:, None]
    out_keep = (cols_keep[:, None, None, :] & rows_keep[None, :, :, None]).astype(jnp.float32)
    return (summed * out_keep).astype(jnp.bfloat16)


def solution(mesh):
    in_specs = (
        P(("parts", "blk"), None, None, None),
        P(("parts", "op"), "blk", None, None),
        P(("parts", "op"), "blk", None, None),
        P(("parts", "op"), None),
        P("parts"),
        P("parts"),
    )
    out_specs = P(("parts", "blk"), "op", None, None)
    nz, no = mesh.shape["blk"], mesh.shape["op"]
    body = shards if nz == no == 4 else wide_shards
    return jax.shard_map(body, mesh=mesh, in_specs=in_specs, out_specs=out_specs, check_vma=False)
```

```python
import functools

import jax
import jax.numpy as jnp
from jax import lax
from jax.experimental import pallas as pl
from jax.experimental.pallas import tpu as pltpu
from jax.sharding import PartitionSpec as P

ANY = pl.BlockSpec(memory_space=pl.ANY)
SMEM = pl.BlockSpec(memory_space=pltpu.SMEM)
VMEM = pl.BlockSpec(memory_space=pltpu.VMEM)
PARAMS = pltpu.CompilerParams(vmem_limit_bytes=32 * 1024 * 1024)
ID_ROWS = 16


def acting_terms(blocks_ref, sector):
    first = jnp.int32(0)
    second = jnp.int32(0)
    for term in reversed(range(blocks_ref.shape[0])):
        acts = blocks_ref[term, sector] > 0
        second = jnp.where(acts, first, second)
        first = jnp.where(acts, term, first)
    return first, second


def place():
    op = lax.axis_index("op")
    return lax.axis_index("blk"), lax.shift_right_logical(op, 1), jnp.bitwise_and(op, 1)


def is_home():
    z, _, c = place()
    return c == jnp.bitwise_and(z, 1)


def pack_kernel(blocks_ref, psi_ref, left_ref, right_ref, *rest):
    left_out, side_out, far_out, right_out, sem = rest
    z, _, _ = place()
    sectors, tile = psi_ref.shape[0], psi_ref.shape[-1]
    count = 2 * sectors
    row = lax.broadcasted_iota(jnp.int32, (ID_ROWS, tile), 0)
    ids = jnp.zeros((ID_ROWS, tile), jnp.float32)
    picked = []
    for local in range(sectors):
        for term in acting_terms(blocks_ref, z * sectors + local):
            ids = jnp.where(row == len(picked), term.astype(jnp.float32), ids)
            picked.append(left_ref.at[term, local])
    near = jnp.bitwise_xor(z, 1) * sectors
    asked = [psi_ref.at[a, near + b] for a in range(sectors) for b in range(sectors)]

    def copies(sources, out, first):
        return [
            pltpu.make_async_copy(source, out.at[pl.ds(spot * tile, tile)], sem.at[first + spot])
            for spot, source in enumerate(sources)
        ]

    far = pl.ds(jnp.bitwise_xor(z, jnp.where(is_home(), 2, 3)) * sectors, sectors)
    plain = copies(picked, left_out, 0)
    plain.append(pltpu.make_async_copy(psi_ref.at[:, far], far_out, sem.at[2 * count]))
    plain.append(pltpu.make_async_copy(right_ref, right_out, sem.at[2 * count + 1]))
    for copy in plain:
        copy.start()
    for at_home, sources in ((True, asked), (False, picked)):

        @pl.when(is_home() == at_home)
        def _(sources=sources):
            for copy in copies(sources, side_out, count):
                copy.start()

    for out in (left_out, side_out):
        out[pl.ds(count * tile, ID_ROWS)] = ids.astype(jnp.bfloat16)
    for copy in plain + copies(picked, side_out, count):
        copy.wait()


def keep_mask(z, distance, sizes, a, b, sectors, tile):
    lsize_ref, rsize_ref = sizes
    rows = lax.broadcasted_iota(jnp.int32, (tile, tile), 0)
    lanes = lax.broadcasted_iota(jnp.int32, (tile, tile), 1)
    height = lsize_ref[jnp.bitwise_xor(z, distance) * sectors + a]
    return (rows < height) & (lanes < rsize_ref[z * sectors + b])


def wide_psi(z, distance, sizes, a, columns, blocks):
    tile = blocks[0].shape[-1]
    cut = []
    for b, block in zip(columns, blocks):
        keep = keep_mask(z, distance, sizes, a, b, len(blocks), tile)
        cut.append(jnp.where(keep, block.astype(jnp.float32), 0.0).astype(jnp.bfloat16))
    return jnp.concatenate(cut, axis=1)


def partial_sums(z, distance, sizes, columns, psi, lefts, rights, store):
    sectors = len(columns)
    for a in range(sectors):
        wide = psi(a)
        tile = wide.shape[0]
        applied = []
        for left in lefts:
            both = jnp.dot(left(a), wide, preferred_element_type=jnp.float32).astype(jnp.bfloat16)
            applied += [both[:tile], both[tile:]]
        for side, b in enumerate(columns):
            picked = [right(a, slot, b) for right in rights for slot in range(2)]
            column = [part[:, side * tile : (side + 1) * tile] for part in applied]
            total = lax.dot_general(
                jnp.concatenate(column, axis=1),
                jnp.concatenate(picked, axis=1),
                (((1,), (1,)), ((), ())),
                preferred_element_type=jnp.float32,
            )
            keep = keep_mask(z, distance, sizes, a, b, sectors, tile)
            store(b, a, jnp.where(keep, total, 0.0))


def message(ref, right_ref):
    terms, sectors, tile = right_ref.shape[0], right_ref.shape[1], right_ref.shape[-1]
    ids = ref[pl.ds(2 * sectors * tile, ID_ROWS)].astype(jnp.float32)

    def left(a):
        return ref[pl.ds(2 * a * tile, 2 * tile)]

    def right(a, slot, b):
        spot = 2 * a + slot
        term = jnp.broadcast_to(ids[spot : spot + 1], (tile, tile))
        block = right_ref[0, b].astype(jnp.float32)
        for t in range(1, terms):
            block = jnp.where(term == t, right_ref[t, b].astype(jnp.float32), block)
        return block.astype(jnp.bfloat16)

    return left, right


def mask_kernel(lsize_ref, rsize_ref, psi_ref, wide_ref):
    z, _, _ = place()
    far = jnp.where(is_home(), 2, 3)
    columns = range(psi_ref.shape[1])
    for a in range(psi_ref.shape[0]):
        blocks = [psi_ref[a, b] for b in columns]
        wide_ref[a] = wide_psi(z, far, (lsize_ref, rsize_ref), a, columns, blocks)


def near_kernel(lsize_ref, rsize_ref, blocks_ref, *rest):
    psi_ref, left_ref, side, direct_a, direct_b, right_own, right_other, out_ref = rest
    z, _, _ = place()
    sectors, tile = out_ref.shape[0], out_ref.shape[-1]
    sizes, columns = (lsize_ref, rsize_ref), range(sectors)

    def store(b, a, total):
        out_ref[b, a] = total

    def masked(distance, a, blocks):
        return wide_psi(z, distance, sizes, a, columns, blocks)

    @pl.when(is_home())
    def _():
        terms = [acting_terms(blocks_ref, z * sectors + a) for a in columns]
        left, right = message(side, right_other)
        partial_sums(
            z, 0, sizes, columns,
            lambda a: masked(0, a, [psi_ref[a, z * sectors + b] for b in columns]),
            [lambda a: jnp.concatenate([left_ref[term, a] for term in terms[a]], axis=0), left],
            [lambda a, slot, b: right_own[terms[a][slot], b], right],
            store,
        )

    @pl.when(jnp.logical_not(is_home()))
    def _():
        lefts, rights = zip(message(direct_b, right_own), message(direct_a, right_other))

        def psi(a):
            return masked(1, a, [side[pl.ds((sectors * a + b) * tile, tile)] for b in columns])

        partial_sums(z, 1, sizes, columns, psi, lefts, rights, store)


def far_kernel(lsize_ref, rsize_ref, *rest):
    direct_a, direct_b, passed_a, passed_b, right_own, right_other = rest[:6]
    near_ref, wide_ref, sent_ref, out_ref = rest[6:]
    z, x, _ = place()
    columns = range(out_ref.shape[0])
    far_leaves = lax.shift_right_logical(z, 1) == x

    def store_sent(b, a, total):
        sent_ref[b, a] = total.astype(sent_ref.dtype)

    def store_kept(b, a, total):
        out_ref[b, a] = total
        sent_ref[b, a] = near_ref[b, a].astype(sent_ref.dtype)

    for leaves, store in ((True, store_sent), (False, store_kept)):
        for at_home, distance, first, second in (
            (True, 2, direct_a, direct_b),
            (False, 3, passed_a, passed_b),
        ):

            @pl.when((is_home() == at_home) & (far_leaves == leaves))
            def _(store=store, distance=distance, first=first, second=second):
                lefts, rights = zip(message(first, right_own), message(second, right_other))
                sizes = (lsize_ref, rsize_ref)
                partial_sums(
                    z, distance, sizes, columns, lambda a: wide_ref[a], lefts, rights, store
                )


def shards(psi, left_ops, right_ops, term_blocks, left_sizes, right_sizes):
    n = 4
    sectors, tile = psi.shape[0], psi.shape[-1]
    block = functools.partial(jax.ShapeDtypeStruct, dtype=jnp.bfloat16)
    out_shape = (sectors, sectors, tile, tile)
    message_shape = (2 * sectors * tile + ID_ROWS, tile)

    def over_op(array, step):
        return lax.ppermute(array, "op", [(o, o ^ step) for o in range(n)])

    def over_z(array, home_step, other_step):
        pairs = []
        for z in range(n):
            for o in range(n):
                step = home_step if o & 1 == z & 1 else other_step
                pairs.append((z * n + o, (z ^ step) * n + (o & 2) + (z & 1)))
        return lax.ppermute(array, ("blk", "op"), pairs)

    psi_hbm, left_hbm, right_hbm, blocks_hbm = [
        pltpu.with_memory_space_constraint(array, pltpu.HBM)
        for array in (psi, left_ops, right_ops, term_blocks)
    ]
    left_sent, side_sent, far_sent, right_own = pl.pallas_call(
        pack_kernel,
        out_shape=[
            block(message_shape),
            block(message_shape),
            block(out_shape),
            block(right_ops.shape),
        ],
        in_specs=[SMEM, ANY, ANY, ANY],
        out_specs=[VMEM] * 4,
        scratch_shapes=[pltpu.SemaphoreType.DMA((4 * sectors + 2,))],
        compiler_params=PARAMS,
        name="pack",
    )(blocks_hbm, psi_hbm, left_hbm, right_hbm)
    direct_a = over_z(left_sent, 2, 1)
    direct_b = over_z(left_sent, 1, 2)
    psi_far = over_z(far_sent, 2, 3)
    side = over_z(side_sent, 1, 0)
    passed_a = over_z(direct_a, 1, 0)
    passed_b = over_z(direct_b, 1, 0)
    right_other = over_op(right_own, 1)

    def apply(kernel, name, outs, scalars, operands):
        return pl.pallas_call(
            kernel,
            out_shape=outs,
            in_specs=[SMEM] * len(scalars) + [VMEM] * len(operands),
            out_specs=[VMEM] * len(outs),
            compiler_params=PARAMS,
            cost_estimate=pl.CostEstimate(
                flops=64 * tile**3 * sectors**2, bytes_accessed=2**20, transcendentals=0
            ),
            name=name,
        )(*scalars, *operands)

    sizes = (left_sizes, right_sizes)
    rights = [right_own, right_other]
    total = jax.ShapeDtypeStruct(out_shape, jnp.float32)
    (near,) = apply(
        near_kernel, "near", [total], sizes + (term_blocks,),
        [psi, left_ops, side, direct_a, direct_b] + rights,
    )
    psi_turn, near = lax.optimization_barrier((psi_far, near))
    (wide,) = apply(
        mask_kernel, "mask", [block((sectors, tile, sectors * tile))], sizes,
        [psi_turn],
    )
    sent, far = apply(
        far_kernel, "far", [block(out_shape), total], sizes,
        [direct_a, direct_b, passed_a, passed_b] + rights + [near, wide],
    )
    arrived = over_op(sent, 2)
    kept = jnp.where(lax.axis_index("blk") // 2 == lax.axis_index("op") // 2, near, far)
    return (kept + arrived.astype(jnp.float32)).astype(jnp.bfloat16)


def wide_shards(psi, left_ops, right_ops, term_blocks, left_sizes, right_sizes):
    sectors_here = psi.shape[0]
    tile_size = psi.shape[2]
    left_first = lax.axis_index("blk") * sectors_here
    positions = lax.broadcasted_iota(jnp.int32, (tile_size,), 0)
    left_local = lax.dynamic_slice_in_dim(left_sizes, left_first, sectors_here)
    left_keep = positions[None, :] < left_local[:, None]
    right_keep = positions[None, :] < right_sizes[:, None]
    keep_mask = (left_keep[:, None, :, None] & right_keep[None, :, None, :]).astype(jnp.bfloat16)
    masked = psi * keep_mask
    acting_count = left_ops.shape[0] // 2
    order = jnp.argsort(1 - term_blocks, axis=0, stable=True)[:acting_count]
    ids_local = lax.dynamic_slice_in_dim(order, left_first, sectors_here, 1)
    sector_index = lax.broadcasted_iota(jnp.int32, (acting_count, sectors_here), 1)
    picked = left_ops[ids_local, sector_index]
    applied = jnp.einsum(
        "kaim,abmj->kabij", picked, masked, preferred_element_type=jnp.float32
    ).astype(jnp.bfloat16)
    arrived = lax.all_to_all(applied, "blk", split_axis=2, concat_axis=1, tiled=True)
    right_picked = right_ops[order]
    partial_value = jnp.einsum(
        "kabij,kablj->bail", arrived, right_picked, preferred_element_type=jnp.float32
    )
    summed = lax.psum_scatter(
        partial_value.astype(jnp.bfloat16), "op", scatter_dimension=1, tiled=True
    ).astype(jnp.float32)
    row_count = summed.shape[1]
    op_first = lax.axis_index("op") * row_count
    left_share = lax.dynamic_slice_in_dim(left_sizes, op_first, row_count)
    right_local = lax.dynamic_slice_in_dim(right_sizes, left_first, sectors_here)
    rows_keep = positions[None, :] < left_share[:, None]
    cols_keep = positions[None, :] < right_local[:, None]
    out_keep = (cols_keep[:, None, None, :] & rows_keep[None, :, :, None]).astype(jnp.float32)
    return (summed * out_keep).astype(jnp.bfloat16)


def solution(mesh):
    in_specs = (
        P(("parts", "blk"), None, None, None),
        P(("parts", "op"), "blk", None, None),
        P(("parts", "op"), "blk", None, None),
        P(("parts", "op"), None),
        P("parts"),
        P("parts"),
    )
    out_specs = P(("parts", "blk"), "op", None, None)
    nz, no = mesh.shape["blk"], mesh.shape["op"]
    body = shards if nz == no == 4 else wide_shards
    return jax.shard_map(body, mesh=mesh, in_specs=in_specs, out_specs=out_specs, check_vma=False)
```

```python
import functools

import jax
import jax.numpy as jnp
from jax import lax
from jax.experimental import pallas as pl
from jax.experimental.pallas import tpu as pltpu
from jax.sharding import PartitionSpec as P

ANY = pl.BlockSpec(memory_space=pl.ANY)
SMEM = pl.BlockSpec(memory_space=pltpu.SMEM)
VMEM = pl.BlockSpec(memory_space=pltpu.VMEM)
PARAMS = pltpu.CompilerParams(vmem_limit_bytes=32 * 1024 * 1024)
ID_ROWS = 16


def acting_terms(blocks_ref, sector):
    first = jnp.int32(0)
    second = jnp.int32(0)
    for term in reversed(range(blocks_ref.shape[0])):
        acts = blocks_ref[term, sector] > 0
        second = jnp.where(acts, first, second)
        first = jnp.where(acts, term, first)
    return first, second


def place():
    op = lax.axis_index("op")
    return lax.axis_index("blk"), lax.shift_right_logical(op, 1), jnp.bitwise_and(op, 1)


def is_home():
    z, _, c = place()
    return c == jnp.bitwise_and(z, 1)


def pack_kernel(blocks_ref, psi_ref, left_ref, right_ref, *rest):
    left_out, side_out, far_out, right_out, sem = rest
    z, _, _ = place()
    sectors, tile = psi_ref.shape[0], psi_ref.shape[-1]
    count = 2 * sectors
    row = lax.broadcasted_iota(jnp.int32, (ID_ROWS, tile), 0)
    ids = jnp.zeros((ID_ROWS, tile), jnp.float32)
    picked = []
    for local in range(sectors):
        for term in acting_terms(blocks_ref, z * sectors + local):
            ids = jnp.where(row == len(picked), term.astype(jnp.float32), ids)
            picked.append(left_ref.at[term, local])
    near = jnp.bitwise_xor(z, 1) * sectors
    asked = [psi_ref.at[a, near + b] for a in range(sectors) for b in range(sectors)]

    def copies(sources, out, first):
        return [
            pltpu.make_async_copy(source, out.at[pl.ds(spot * tile, tile)], sem.at[first + spot])
            for spot, source in enumerate(sources)
        ]

    far = pl.ds(jnp.bitwise_xor(z, jnp.where(is_home(), 2, 3)) * sectors, sectors)
    plain = copies(picked, left_out, 0)
    plain.append(pltpu.make_async_copy(psi_ref.at[:, far], far_out, sem.at[2 * count]))
    plain.append(pltpu.make_async_copy(right_ref, right_out, sem.at[2 * count + 1]))
    for copy in plain:
        copy.start()
    for at_home, sources in ((True, asked), (False, picked)):

        @pl.when(is_home() == at_home)
        def _(sources=sources):
            for copy in copies(sources, side_out, count):
                copy.start()

    for out in (left_out, side_out):
        out[pl.ds(count * tile, ID_ROWS)] = ids.astype(jnp.bfloat16)
    for copy in plain + copies(picked, side_out, count):
        copy.wait()


def keep_mask(z, distance, sizes, a, b, sectors, tile):
    lsize_ref, rsize_ref = sizes
    rows = lax.broadcasted_iota(jnp.int32, (tile, tile), 0)
    lanes = lax.broadcasted_iota(jnp.int32, (tile, tile), 1)
    height = lsize_ref[jnp.bitwise_xor(z, distance) * sectors + a]
    return (rows < height) & (lanes < rsize_ref[z * sectors + b])


def wide_psi(z, distance, sizes, a, columns, blocks):
    tile = blocks[0].shape[-1]
    cut = []
    for b, block in zip(columns, blocks):
        keep = keep_mask(z, distance, sizes, a, b, len(blocks), tile)
        cut.append(jnp.where(keep, block.astype(jnp.float32), 0.0).astype(jnp.bfloat16))
    return jnp.concatenate(cut, axis=1)


def partial_sums(z, distance, sizes, columns, psi, lefts, rights, store):
    sectors = len(columns)
    for a in range(sectors):
        wide = psi(a)
        tile = wide.shape[0]
        applied = []
        for left in lefts:
            both = jnp.dot(left(a), wide, preferred_element_type=jnp.float32).astype(jnp.bfloat16)
            applied += [both[:tile], both[tile:]]
        for side, b in enumerate(columns):
            picked = [right(a, slot, b) for right in rights for slot in range(2)]
            column = [part[:, side * tile : (side + 1) * tile] for part in applied]
            total = lax.dot_general(
                jnp.concatenate(column, axis=1),
                jnp.concatenate(picked, axis=1),
                (((1,), (1,)), ((), ())),
                preferred_element_type=jnp.float32,
            )
            keep = keep_mask(z, distance, sizes, a, b, sectors, tile)
            store(b, a, jnp.where(keep, total, 0.0))


def message(ref, right_ref):
    terms, sectors, tile = right_ref.shape[0], right_ref.shape[1], right_ref.shape[-1]
    ids = ref[pl.ds(2 * sectors * tile, ID_ROWS)].astype(jnp.float32)

    def left(a):
        return ref[pl.ds(2 * a * tile, 2 * tile)]

    def right(a, slot, b):
        spot = 2 * a + slot
        term = jnp.broadcast_to(ids[spot : spot + 1], (tile, tile))
        block = right_ref[0, b].astype(jnp.float32)
        for t in range(1, terms):
            block = jnp.where(term == t, right_ref[t, b].astype(jnp.float32), block)
        return block.astype(jnp.bfloat16)

    return left, right


def mask_kernel(lsize_ref, rsize_ref, psi_ref, wide_ref):
    z, _, _ = place()
    far = jnp.where(is_home(), 2, 3)
    columns = range(psi_ref.shape[1])
    for a in range(psi_ref.shape[0]):
        blocks = [psi_ref[a, b] for b in columns]
        wide_ref[a] = wide_psi(z, far, (lsize_ref, rsize_ref), a, columns, blocks)


def near_kernel(lsize_ref, rsize_ref, blocks_ref, *rest):
    psi_ref, left_ref, side, direct_a, direct_b, right_own, right_other = rest[:7]
    out_ref, sent_ref = rest[7:]
    z, _, _ = place()
    sectors, tile = out_ref.shape[0], out_ref.shape[-1]
    sizes, columns = (lsize_ref, rsize_ref), range(sectors)

    def store(b, a, total):
        out_ref[b, a] = total
        sent_ref[b, a] = total.astype(sent_ref.dtype)

    def masked(distance, a, blocks):
        return wide_psi(z, distance, sizes, a, columns, blocks)

    @pl.when(is_home())
    def _():
        terms = [acting_terms(blocks_ref, z * sectors + a) for a in columns]
        left, right = message(side, right_other)
        partial_sums(
            z, 0, sizes, columns,
            lambda a: masked(0, a, [psi_ref[a, z * sectors + b] for b in columns]),
            [lambda a: jnp.concatenate([left_ref[term, a] for term in terms[a]], axis=0), left],
            [lambda a, slot, b: right_own[terms[a][slot], b], right],
            store,
        )

    @pl.when(jnp.logical_not(is_home()))
    def _():
        lefts, rights = zip(message(direct_b, right_own), message(direct_a, right_other))

        def psi(a):
            return masked(1, a, [side[pl.ds((sectors * a + b) * tile, tile)] for b in columns])

        partial_sums(z, 1, sizes, columns, psi, lefts, rights, store)


def far_kernel(lsize_ref, rsize_ref, *rest):
    direct_a, direct_b, passed_a, passed_b, right_own, right_other, wide_ref = rest[:7]
    out_ref, sent_ref = rest[7:]
    z, _, _ = place()
    columns = range(out_ref.shape[0])

    def store(b, a, total):
        out_ref[b, a] = total
        sent_ref[b, a] = total.astype(sent_ref.dtype)

    for at_home, distance, first, second in (
        (True, 2, direct_a, direct_b),
        (False, 3, passed_a, passed_b),
    ):

        @pl.when(is_home() == at_home)
        def _(distance=distance, first=first, second=second):
            lefts, rights = zip(message(first, right_own), message(second, right_other))
            sizes = (lsize_ref, rsize_ref)
            partial_sums(z, distance, sizes, columns, lambda a: wide_ref[a], lefts, rights, store)


def shards(psi, left_ops, right_ops, term_blocks, left_sizes, right_sizes):
    n = 4
    sectors, tile = psi.shape[0], psi.shape[-1]
    block = functools.partial(jax.ShapeDtypeStruct, dtype=jnp.bfloat16)
    out_shape = (sectors, sectors, tile, tile)
    message_shape = (2 * sectors * tile + ID_ROWS, tile)

    def over_op(array, step):
        return lax.ppermute(array, "op", [(o, o ^ step) for o in range(n)])

    def over_z(array, home_step, other_step):
        pairs = []
        for z in range(n):
            for o in range(n):
                step = home_step if o & 1 == z & 1 else other_step
                pairs.append((z * n + o, (z ^ step) * n + (o & 2) + (z & 1)))
        return lax.ppermute(array, ("blk", "op"), pairs)

    psi_hbm, left_hbm, right_hbm, blocks_hbm = [
        pltpu.with_memory_space_constraint(array, pltpu.HBM)
        for array in (psi, left_ops, right_ops, term_blocks)
    ]
    left_sent, side_sent, far_sent, right_own = pl.pallas_call(
        pack_kernel,
        out_shape=[
            block(message_shape),
            block(message_shape),
            block(out_shape),
            block(right_ops.shape),
        ],
        in_specs=[SMEM, ANY, ANY, ANY],
        out_specs=[VMEM] * 4,
        scratch_shapes=[pltpu.SemaphoreType.DMA((4 * sectors + 2,))],
        compiler_params=PARAMS,
        name="pack",
    )(blocks_hbm, psi_hbm, left_hbm, right_hbm)
    direct_a = over_z(left_sent, 2, 1)
    direct_b = over_z(left_sent, 1, 2)
    psi_far = over_z(far_sent, 2, 3)
    side = over_z(side_sent, 1, 0)
    passed_a = over_z(direct_a, 1, 0)
    passed_b = over_z(direct_b, 1, 0)
    right_other = over_op(right_own, 1)

    def apply(kernel, name, outs, scalars, operands):
        return pl.pallas_call(
            kernel,
            out_shape=outs,
            in_specs=[SMEM] * len(scalars) + [VMEM] * len(operands),
            out_specs=[VMEM] * len(outs),
            compiler_params=PARAMS,
            cost_estimate=pl.CostEstimate(
                flops=64 * tile**3 * sectors**2, bytes_accessed=2**20, transcendentals=0
            ),
            name=name,
        )(*scalars, *operands)

    sizes = (left_sizes, right_sizes)
    rights = [right_own, right_other]
    sums = [jax.ShapeDtypeStruct(out_shape, jnp.float32), block(out_shape)]
    near, near_sent = apply(
        near_kernel, "near", sums, sizes + (term_blocks,),
        [psi, left_ops, side, direct_a, direct_b] + rights,
    )
    near_arrived = over_op(near_sent, 2)
    psi_turn, _ = lax.optimization_barrier((psi_far, near_sent))
    (wide,) = apply(
        mask_kernel, "mask", [block((sectors, tile, sectors * tile))], sizes, [psi_turn]
    )
    far, far_sent_on = apply(
        far_kernel, "far", sums, sizes,
        [direct_a, direct_b, passed_a, passed_b] + rights + [wide],
    )
    pairs = [
        (z * n + 2 * (z // 2) + c, z * n + 2 * (1 - z // 2) + c) for z in range(n) for c in range(2)
    ]
    far_arrived = lax.ppermute(far_sent_on, ("blk", "op"), pairs)
    owns_near = lax.axis_index("blk") // 2 == lax.axis_index("op") // 2
    kept = jnp.where(owns_near, near, far)
    arrived = jnp.where(owns_near, near_arrived, far_arrived)
    return (kept + arrived.astype(jnp.float32)).astype(jnp.bfloat16)


def wide_shards(psi, left_ops, right_ops, term_blocks, left_sizes, right_sizes):
    sectors_here = psi.shape[0]
    tile_size = psi.shape[2]
    left_first = lax.axis_index("blk") * sectors_here
    positions = lax.broadcasted_iota(jnp.int32, (tile_size,), 0)
    left_local = lax.dynamic_slice_in_dim(left_sizes, left_first, sectors_here)
    left_keep = positions[None, :] < left_local[:, None]
    right_keep = positions[None, :] < right_sizes[:, None]
    keep_mask = (left_keep[:, None, :, None] & right_keep[None, :, None, :]).astype(jnp.bfloat16)
    masked = psi * keep_mask
    acting_count = left_ops.shape[0] // 2
    order = jnp.argsort(1 - term_blocks, axis=0, stable=True)[:acting_count]
    ids_local = lax.dynamic_slice_in_dim(order, left_first, sectors_here, 1)
    sector_index = lax.broadcasted_iota(jnp.int32, (acting_count, sectors_here), 1)
    picked = left_ops[ids_local, sector_index]
    applied = jnp.einsum(
        "kaim,abmj->kabij", picked, masked, preferred_element_type=jnp.float32
    ).astype(jnp.bfloat16)
    arrived = lax.all_to_all(applied, "blk", split_axis=2, concat_axis=1, tiled=True)
    right_picked = right_ops[order]
    partial_value = jnp.einsum(
        "kabij,kablj->bail", arrived, right_picked, preferred_element_type=jnp.float32
    )
    summed = lax.psum_scatter(
        partial_value.astype(jnp.bfloat16), "op", scatter_dimension=1, tiled=True
    ).astype(jnp.float32)
    row_count = summed.shape[1]
    op_first = lax.axis_index("op") * row_count
    left_share = lax.dynamic_slice_in_dim(left_sizes, op_first, row_count)
    right_local = lax.dynamic_slice_in_dim(right_sizes, left_first, sectors_here)
    rows_keep = positions[None, :] < left_share[:, None]
    cols_keep = positions[None, :] < right_local[:, None]
    out_keep = (cols_keep[:, None, None, :] & rows_keep[None, :, :, None]).astype(jnp.float32)
    return (summed * out_keep).astype(jnp.bfloat16)


def solution(mesh):
    in_specs = (
        P(("parts", "blk"), None, None, None),
        P(("parts", "op"), "blk", None, None),
        P(("parts", "op"), "blk", None, None),
        P(("parts", "op"), None),
        P("parts"),
        P("parts"),
    )
    out_specs = P(("parts", "blk"), "op", None, None)
    nz, no = mesh.shape["blk"], mesh.shape["op"]
    body = shards if nz == no == 4 else wide_shards
    return jax.shard_map(body, mesh=mesh, in_specs=in_specs, out_specs=out_specs, check_vma=False)
```

```python
import functools

import jax
import jax.numpy as jnp
from jax import lax
from jax.experimental import pallas as pl
from jax.experimental.pallas import tpu as pltpu
from jax.sharding import PartitionSpec as P

ANY = pl.BlockSpec(memory_space=pl.ANY)
SMEM = pl.BlockSpec(memory_space=pltpu.SMEM)
VMEM = pl.BlockSpec(memory_space=pltpu.VMEM)
PARAMS = pltpu.CompilerParams(vmem_limit_bytes=32 * 1024 * 1024)
ID_ROWS = 16


def acting_terms(blocks_ref, sector):
    first = jnp.int32(0)
    second = jnp.int32(0)
    for term in reversed(range(blocks_ref.shape[0])):
        acts = blocks_ref[term, sector] > 0
        second = jnp.where(acts, first, second)
        first = jnp.where(acts, term, first)
    return first, second


def place():
    op = lax.axis_index("op")
    return lax.axis_index("blk"), lax.shift_right_logical(op, 1), jnp.bitwise_and(op, 1)


def is_home():
    z, _, c = place()
    return c == jnp.bitwise_and(z, 1)


def pack_kernel(blocks_ref, psi_ref, left_ref, right_ref, *rest):
    left_out, side_out, far_out, right_out, sem = rest
    z, x, _ = place()
    sectors, tile = psi_ref.shape[0], psi_ref.shape[-1]
    count = 2 * sectors
    row = lax.broadcasted_iota(jnp.int32, (ID_ROWS, tile), 0)
    ids = jnp.zeros((ID_ROWS, tile), jnp.float32)
    picked = []
    for local in range(sectors):
        for term in acting_terms(blocks_ref, z * sectors + local):
            ids = jnp.where(row == len(picked), term.astype(jnp.float32), ids)
            picked.append(left_ref.at[term, local])
    near = jnp.bitwise_xor(z, 1) * sectors
    asked = [psi_ref.at[a, near + b] for a in range(sectors) for b in range(sectors)]

    def copies(sources, out, first):
        return [
            pltpu.make_async_copy(source, out.at[pl.ds(spot * tile, tile)], sem.at[first + spot])
            for spot, source in enumerate(sources)
        ]

    far = jnp.bitwise_xor(z, jnp.where(is_home(), 2, 3)) * sectors + x
    plain = copies(picked, left_out, 0)
    plain.append(pltpu.make_async_copy(psi_ref.at[:, far], far_out, sem.at[2 * count]))
    plain.append(pltpu.make_async_copy(right_ref, right_out, sem.at[2 * count + 1]))
    for copy in plain:
        copy.start()
    for at_home, sources in ((True, asked), (False, picked)):

        @pl.when(is_home() == at_home)
        def _(sources=sources):
            for copy in copies(sources, side_out, count):
                copy.start()

    for out in (left_out, side_out):
        out[pl.ds(count * tile, ID_ROWS)] = ids.astype(jnp.bfloat16)
    for copy in plain + copies(picked, side_out, count):
        copy.wait()


def keep_mask(z, distance, sizes, a, b, sectors, tile):
    lsize_ref, rsize_ref = sizes
    rows = lax.broadcasted_iota(jnp.int32, (tile, tile), 0)
    lanes = lax.broadcasted_iota(jnp.int32, (tile, tile), 1)
    height = lsize_ref[jnp.bitwise_xor(z, distance) * sectors + a]
    return (rows < height) & (lanes < rsize_ref[z * sectors + b])


def wide_psi(z, distance, sizes, a, columns, blocks):
    tile = blocks[0].shape[-1]
    cut = []
    for b, block in zip(columns, blocks):
        keep = keep_mask(z, distance, sizes, a, b, len(blocks), tile)
        cut.append(jnp.where(keep, block.astype(jnp.float32), 0.0).astype(jnp.bfloat16))
    return jnp.concatenate(cut, axis=1)


def partial_sums(z, distance, sizes, columns, psi, lefts, rights, store):
    sectors = len(columns)
    for a in range(sectors):
        wide = psi(a)
        tile = wide.shape[0]
        applied = []
        for left in lefts:
            both = jnp.dot(left(a), wide, preferred_element_type=jnp.float32).astype(jnp.bfloat16)
            applied += [both[:tile], both[tile:]]
        for side, b in enumerate(columns):
            picked = [right(a, slot, b) for right in rights for slot in range(2)]
            column = [part[:, side * tile : (side + 1) * tile] for part in applied]
            total = lax.dot_general(
                jnp.concatenate(column, axis=1),
                jnp.concatenate(picked, axis=1),
                (((1,), (1,)), ((), ())),
                preferred_element_type=jnp.float32,
            )
            keep = keep_mask(z, distance, sizes, a, b, sectors, tile)
            store(b, a, jnp.where(keep, total, 0.0))


def message(ref, right_ref):
    terms, sectors, tile = right_ref.shape[0], right_ref.shape[1], right_ref.shape[-1]
    ids = ref[pl.ds(2 * sectors * tile, ID_ROWS)].astype(jnp.float32)

    def left(a):
        return ref[pl.ds(2 * a * tile, 2 * tile)]

    def right(a, slot, b):
        spot = 2 * a + slot
        term = jnp.broadcast_to(ids[spot : spot + 1], (tile, tile))
        block = right_ref[0, b].astype(jnp.float32)
        for t in range(1, terms):
            block = jnp.where(term == t, right_ref[t, b].astype(jnp.float32), block)
        return block.astype(jnp.bfloat16)

    return left, right


def mask_kernel(lsize_ref, rsize_ref, psi_same, psi_other, wide_ref):
    z, x, _ = place()
    far = jnp.where(is_home(), 2, 3)
    for a in range(psi_same.shape[0]):
        blocks = [psi_same[a], psi_other[a]]
        wide_ref[a] = wide_psi(z, far, (lsize_ref, rsize_ref), a, (x, 1 - x), blocks)


def near_kernel(lsize_ref, rsize_ref, blocks_ref, *rest):
    psi_ref, left_ref, side, direct_a, direct_b, right_own, right_other, out_ref = rest
    z, _, _ = place()
    sectors, tile = out_ref.shape[0], out_ref.shape[-1]
    sizes, columns = (lsize_ref, rsize_ref), range(sectors)

    def store(b, a, total):
        out_ref[b, a] = total

    def masked(distance, a, blocks):
        return wide_psi(z, distance, sizes, a, columns, blocks)

    @pl.when(is_home())
    def _():
        terms = [acting_terms(blocks_ref, z * sectors + a) for a in columns]
        left, right = message(side, right_other)
        partial_sums(
            z, 0, sizes, columns,
            lambda a: masked(0, a, [psi_ref[a, z * sectors + b] for b in columns]),
            [lambda a: jnp.concatenate([left_ref[term, a] for term in terms[a]], axis=0), left],
            [lambda a, slot, b: right_own[terms[a][slot], b], right],
            store,
        )

    @pl.when(jnp.logical_not(is_home()))
    def _():
        lefts, rights = zip(message(direct_b, right_own), message(direct_a, right_other))

        def psi(a):
            return masked(1, a, [side[pl.ds((sectors * a + b) * tile, tile)] for b in columns])

        partial_sums(z, 1, sizes, columns, psi, lefts, rights, store)


def far_kernel(lsize_ref, rsize_ref, *rest):
    direct_a, direct_b, passed_a, passed_b, right_own, right_other = rest[:6]
    near_ref, wide_ref, sent_ref, out_ref = rest[6:]
    z, x, _ = place()
    columns = (x, 1 - x)
    far_leaves = lax.shift_right_logical(z, 1) == x

    def store_sent(b, a, total):
        sent_ref[b, a] = total.astype(sent_ref.dtype)

    def store_kept(b, a, total):
        out_ref[b, a] = total
        sent_ref[b, a] = near_ref[b, a].astype(sent_ref.dtype)

    for leaves, store in ((True, store_sent), (False, store_kept)):
        for at_home, distance, first, second in (
            (True, 2, direct_a, direct_b),
            (False, 3, passed_a, passed_b),
        ):

            @pl.when((is_home() == at_home) & (far_leaves == leaves))
            def _(store=store, distance=distance, first=first, second=second):
                lefts, rights = zip(message(first, right_own), message(second, right_other))
                sizes = (lsize_ref, rsize_ref)
                partial_sums(
                    z, distance, sizes, columns, lambda a: wide_ref[a], lefts, rights, store
                )


def shards(psi, left_ops, right_ops, term_blocks, left_sizes, right_sizes):
    n = 4
    sectors, tile = psi.shape[0], psi.shape[-1]
    block = functools.partial(jax.ShapeDtypeStruct, dtype=jnp.bfloat16)
    out_shape = (sectors, sectors, tile, tile)
    message_shape = (2 * sectors * tile + ID_ROWS, tile)

    def over_op(array, step):
        return lax.ppermute(array, "op", [(o, o ^ step) for o in range(n)])

    def over_z(array, home_step, other_step):
        pairs = []
        for z in range(n):
            for o in range(n):
                step = home_step if o & 1 == z & 1 else other_step
                pairs.append((z * n + o, (z ^ step) * n + (o & 2) + (z & 1)))
        return lax.ppermute(array, ("blk", "op"), pairs)

    psi_hbm, left_hbm, right_hbm, blocks_hbm = [
        pltpu.with_memory_space_constraint(array, pltpu.HBM)
        for array in (psi, left_ops, right_ops, term_blocks)
    ]
    left_sent, side_sent, far_sent, right_own = pl.pallas_call(
        pack_kernel,
        out_shape=[
            block(message_shape),
            block(message_shape),
            block((sectors, tile, tile)),
            block(right_ops.shape),
        ],
        in_specs=[SMEM, ANY, ANY, ANY],
        out_specs=[VMEM] * 4,
        scratch_shapes=[pltpu.SemaphoreType.DMA((4 * sectors + 2,))],
        compiler_params=PARAMS,
        name="pack",
    )(blocks_hbm, psi_hbm, left_hbm, right_hbm)
    direct_a = over_z(left_sent, 2, 1)
    direct_b = over_z(left_sent, 1, 2)
    far_same = over_z(far_sent, 2, 3)
    far_other = over_op(far_same, 2)
    side = over_z(side_sent, 1, 0)
    passed_a = over_z(direct_a, 1, 0)
    passed_b = over_z(direct_b, 1, 0)
    right_other = over_op(right_own, 1)

    def apply(kernel, name, outs, scalars, operands):
        return pl.pallas_call(
            kernel,
            out_shape=outs,
            in_specs=[SMEM] * len(scalars) + [VMEM] * len(operands),
            out_specs=[VMEM] * len(outs),
            compiler_params=PARAMS,
            cost_estimate=pl.CostEstimate(
                flops=64 * tile**3 * sectors**2, bytes_accessed=2**20, transcendentals=0
            ),
            name=name,
        )(*scalars, *operands)

    sizes = (left_sizes, right_sizes)
    rights = [right_own, right_other]
    total = jax.ShapeDtypeStruct(out_shape, jnp.float32)
    (near,) = apply(
        near_kernel, "near", [total], sizes + (term_blocks,),
        [psi, left_ops, side, direct_a, direct_b] + rights,
    )
    other_turn, near = lax.optimization_barrier((far_other, near))
    (wide,) = apply(
        mask_kernel, "mask", [block((sectors, tile, sectors * tile))], sizes,
        [far_same, other_turn],
    )
    sent, far = apply(
        far_kernel, "far", [block(out_shape), total], sizes,
        [direct_a, direct_b, passed_a, passed_b] + rights + [near, wide],
    )
    arrived = over_op(sent, 2)
    kept = jnp.where(lax.axis_index("blk") // 2 == lax.axis_index("op") // 2, near, far)
    return (kept + arrived.astype(jnp.float32)).astype(jnp.bfloat16)


def wide_shards(psi, left_ops, right_ops, term_blocks, left_sizes, right_sizes):
    sectors_here = psi.shape[0]
    tile_size = psi.shape[2]
    left_first = lax.axis_index("blk") * sectors_here
    positions = lax.broadcasted_iota(jnp.int32, (tile_size,), 0)
    left_local = lax.dynamic_slice_in_dim(left_sizes, left_first, sectors_here)
    left_keep = positions[None, :] < left_local[:, None]
    right_keep = positions[None, :] < right_sizes[:, None]
    keep_mask = (left_keep[:, None, :, None] & right_keep[None, :, None, :]).astype(jnp.bfloat16)
    masked = psi * keep_mask
    acting_count = left_ops.shape[0] // 2
    order = jnp.argsort(1 - term_blocks, axis=0, stable=True)[:acting_count]
    ids_local = lax.dynamic_slice_in_dim(order, left_first, sectors_here, 1)
    sector_index = lax.broadcasted_iota(jnp.int32, (acting_count, sectors_here), 1)
    picked = left_ops[ids_local, sector_index]
    applied = jnp.einsum(
        "kaim,abmj->kabij", picked, masked, preferred_element_type=jnp.float32
    ).astype(jnp.bfloat16)
    arrived = lax.all_to_all(applied, "blk", split_axis=2, concat_axis=1, tiled=True)
    right_picked = right_ops[order]
    partial_value = jnp.einsum(
        "kabij,kablj->bail", arrived, right_picked, preferred_element_type=jnp.float32
    )
    summed = lax.psum_scatter(
        partial_value.astype(jnp.bfloat16), "op", scatter_dimension=1, tiled=True
    ).astype(jnp.float32)
    row_count = summed.shape[1]
    op_first = lax.axis_index("op") * row_count
    left_share = lax.dynamic_slice_in_dim(left_sizes, op_first, row_count)
    right_local = lax.dynamic_slice_in_dim(right_sizes, left_first, sectors_here)
    rows_keep = positions[None, :] < left_share[:, None]
    cols_keep = positions[None, :] < right_local[:, None]
    out_keep = (cols_keep[:, None, None, :] & rows_keep[None, :, :, None]).astype(jnp.float32)
    return (summed * out_keep).astype(jnp.bfloat16)


def solution(mesh):
    in_specs = (
        P(("parts", "blk"), None, None, None),
        P(("parts", "op"), "blk", None, None),
        P(("parts", "op"), "blk", None, None),
        P(("parts", "op"), None),
        P("parts"),
        P("parts"),
    )
    out_specs = P(("parts", "blk"), "op", None, None)
    nz, no = mesh.shape["blk"], mesh.shape["op"]
    body = shards if nz == no == 4 else wide_shards
    return jax.shard_map(body, mesh=mesh, in_specs=in_specs, out_specs=out_specs, check_vma=False)
```

```python
import functools

import jax
import jax.numpy as jnp
from jax import lax
from jax.experimental import pallas as pl
from jax.experimental.pallas import tpu as pltpu
from jax.sharding import PartitionSpec as P

ANY = pl.BlockSpec(memory_space=pl.ANY)
SMEM = pl.BlockSpec(memory_space=pltpu.SMEM)
VMEM = pl.BlockSpec(memory_space=pltpu.VMEM)
PARAMS = pltpu.CompilerParams(vmem_limit_bytes=32 * 1024 * 1024)
ID_ROWS = 16
TERMS = 4


def acting_terms(blocks_ref, sector):
    first = jnp.int32(0)
    second = jnp.int32(0)
    for term in reversed(range(blocks_ref.shape[0])):
        acts = blocks_ref[term, sector] > 0
        second = jnp.where(acts, first, second)
        first = jnp.where(acts, term, first)
    return first, second


def place():
    op = lax.axis_index("op")
    return lax.axis_index("blk"), lax.shift_right_logical(op, 1), jnp.bitwise_and(op, 1)


def is_home():
    z, _, c = place()
    return c == jnp.bitwise_and(z, 1)


def pack_kernel(blocks_ref, psi_ref, left_ref, right_ref, *rest):
    left_out, both_out, swap_out, far_out, sem = rest
    z, _, _ = place()
    sectors, tile = psi_ref.shape[0], psi_ref.shape[-1]
    count = 2 * sectors
    begin = right_ref.shape[0]
    copies = []

    def bring(source, out, spot, rows):
        copies.append(
            pltpu.make_async_copy(source, out.at[pl.ds(spot, rows)], sem.at[len(copies)])
        )

    bring(right_ref, swap_out, 0, begin)
    row = lax.broadcasted_iota(jnp.int32, (ID_ROWS, tile), 0)
    ids = jnp.zeros((ID_ROWS, tile), jnp.float32)
    for local in range(sectors):
        for slot, term in enumerate(acting_terms(blocks_ref, z * sectors + local)):
            spot = 2 * local + slot
            ids = jnp.where(row == spot, term.astype(jnp.float32), ids)
            for out, first in ((left_out, 0), (both_out, 0), (swap_out, begin)):
                bring(left_ref.at[term, local], out, first + spot * tile, tile)
    beside = jnp.bitwise_xor(z, jnp.where(is_home(), 1, 2)) * sectors
    far = jnp.bitwise_xor(z, 3) * sectors
    for a in range(sectors):
        for b in range(sectors):
            spot = (sectors * a + b) * tile
            bring(psi_ref.at[a, beside + b], both_out, count * tile + ID_ROWS + spot, tile)
            bring(psi_ref.at[a, far + b], far_out, spot, tile)
    for copy in copies:
        copy.start()
    for out, first in ((left_out, 0), (both_out, 0), (swap_out, begin)):
        out[pl.ds(first + count * tile, ID_ROWS)] = ids.astype(jnp.bfloat16)
    for copy in copies:
        copy.wait()


def keep_mask(z, distance, sizes, a, b, sectors, tile):
    lsize_ref, rsize_ref = sizes
    rows = lax.broadcasted_iota(jnp.int32, (tile, tile), 0)
    lanes = lax.broadcasted_iota(jnp.int32, (tile, tile), 1)
    height = lsize_ref[jnp.bitwise_xor(z, distance) * sectors + a]
    return (rows < height) & (lanes < rsize_ref[z * sectors + b])


def wide_psi(z, distance, sizes, a, columns, blocks):
    tile = blocks[0].shape[-1]
    cut = []
    for b, block in zip(columns, blocks):
        keep = keep_mask(z, distance, sizes, a, b, len(blocks), tile)
        cut.append(jnp.where(keep, block.astype(jnp.float32), 0.0).astype(jnp.bfloat16))
    return jnp.concatenate(cut, axis=1)


def partial_sums(z, distance, sizes, columns, psi, lefts, rights, store):
    sectors = len(columns)
    for a in range(sectors):
        wide = psi(a)
        tile = wide.shape[0]
        applied = []
        for left in lefts:
            both = jnp.dot(left(a), wide, preferred_element_type=jnp.float32).astype(jnp.bfloat16)
            applied += [both[:tile], both[tile:]]
        for side, b in enumerate(columns):
            picked = [right(a, slot, b) for right in rights for slot in range(2)]
            column = [part[:, side * tile : (side + 1) * tile] for part in applied]
            total = lax.dot_general(
                jnp.concatenate(column, axis=1),
                jnp.concatenate(picked, axis=1),
                (((1,), (1,)), ((), ())),
                preferred_element_type=jnp.float32,
            )
            keep = keep_mask(z, distance, sizes, a, b, sectors, tile)
            store(b, a, jnp.where(keep, total, 0.0))


def message(ref, first, sectors, right_ref, terms=TERMS):
    tile = ref.shape[-1]
    ids = ref[pl.ds(first + 2 * sectors * tile, ID_ROWS)].astype(jnp.float32)

    def left(a):
        return ref[pl.ds(first + 2 * a * tile, 2 * tile)]

    def right(a, slot, b):
        spot = 2 * a + slot
        term = jnp.broadcast_to(ids[spot : spot + 1], (tile, tile))
        block = None
        for t in range(terms):
            other = right_ref[pl.ds((t * sectors + b) * tile, tile)].astype(jnp.float32)
            block = other if block is None else jnp.where(term == t, other, block)
        return block.astype(jnp.bfloat16)

    return left, right


def psi_rows(ref, first, a, sectors):
    tile = ref.shape[-1]
    return [ref[pl.ds(first + (sectors * a + b) * tile, tile)] for b in range(sectors)]


def near_kernel(lsize_ref, rsize_ref, *rest):
    psi_ref, left_own, swap_own, swapped, direct_a, direct_b, out_ref = rest
    z, _, _ = place()
    sectors, tile = out_ref.shape[0], out_ref.shape[-1]
    sizes, columns = (lsize_ref, rsize_ref), range(sectors)
    begin = swap_own.shape[0] - left_own.shape[0]

    def store(b, a, total):
        out_ref[b, a] = total

    for at_home in (True, False):

        @pl.when(is_home() == at_home)
        def _(at_home=at_home):
            if at_home:
                pair = [(left_own, 0, sectors, swap_own), (swapped, begin, sectors, swapped)]
            else:
                pair = [(direct_b, 0, sectors, swap_own), (direct_a, 0, sectors, swapped)]

            def psi(a):
                if at_home:
                    blocks = [psi_ref[a, z * sectors + b] for b in columns]
                else:
                    blocks = psi_rows(direct_b, left_own.shape[0], a, sectors)
                return wide_psi(z, 0 if at_home else 1, sizes, a, columns, blocks)

            lefts, rights = zip(*[message(*one) for one in pair])
            distance = 0 if at_home else 1
            partial_sums(z, distance, sizes, columns, psi, lefts, rights, store)


def mask_kernel(lsize_ref, rsize_ref, direct_b, psi_far, wide_ref):
    z, _, _ = place()
    sectors = wide_ref.shape[0]
    columns = range(sectors)
    sizes = (lsize_ref, rsize_ref)
    first = direct_b.shape[0] - psi_far.shape[0]
    for at_home, distance, ref, begin in ((True, 2, direct_b, first), (False, 3, psi_far, 0)):

        @pl.when(is_home() == at_home)
        def _(distance=distance, ref=ref, begin=begin):
            for a in columns:
                blocks = psi_rows(ref, begin, a, sectors)
                wide_ref[a] = wide_psi(z, distance, sizes, a, columns, blocks)


def far_kernel(lsize_ref, rsize_ref, *rest):
    direct_a, direct_b, passed_a, passed_b, swap_own, swapped = rest[:6]
    near_ref, wide_ref, sent_ref, out_ref = rest[6:]
    z, x, _ = place()
    sectors = out_ref.shape[0]
    far_leaves = lax.shift_right_logical(z, 1) == x

    def store_sent(b, a, total):
        sent_ref[b, a] = total.astype(sent_ref.dtype)

    def store_kept(b, a, total):
        out_ref[b, a] = total
        sent_ref[b, a] = near_ref[b, a].astype(sent_ref.dtype)

    for leaves, store in ((True, store_sent), (False, store_kept)):
        for at_home, distance, first, second in (
            (True, 2, direct_a, direct_b),
            (False, 3, passed_a, passed_b),
        ):

            @pl.when((is_home() == at_home) & (far_leaves == leaves))
            def _(store=store, distance=distance, first=first, second=second):
                pair = ((first, 0, sectors, swap_own), (second, 0, sectors, swapped))
                lefts, rights = zip(*[message(*one) for one in pair])
                sizes, columns = (lsize_ref, rsize_ref), range(sectors)
                partial_sums(
                    z, distance, sizes, columns, lambda a: wide_ref[a], lefts, rights, store
                )


def shards(psi, left_ops, right_ops, term_blocks, left_sizes, right_sizes):
    n = 4
    sectors, tile = psi.shape[0], psi.shape[-1]
    block = functools.partial(jax.ShapeDtypeStruct, dtype=jnp.bfloat16)
    out_shape = (sectors, sectors, tile, tile)

    def over_op(array, step):
        return lax.ppermute(array, "op", [(o, o ^ step) for o in range(n)])

    def over_z(array, home_step, other_step):
        pairs = []
        for z in range(n):
            for o in range(n):
                step = home_step if o & 1 == z & 1 else other_step
                pairs.append((z * n + o, (z ^ step) * n + (o & 2) + (z & 1)))
        return lax.ppermute(array, ("blk", "op"), pairs)

    def to_third(array):
        pairs = []
        for z in range(n):
            for o in range(n):
                to = (z, o) if o & 1 == z & 1 else (z ^ 3, (o & 2) + (z & 1))
                pairs.append((z * n + o, to[0] * n + to[1]))
        return lax.ppermute(array, ("blk", "op"), pairs)

    rights = right_ops.reshape(-1, tile)
    inputs = [
        pltpu.with_memory_space_constraint(array, pltpu.HBM)
        for array in (term_blocks, psi, left_ops, rights)
    ]
    rows, right_rows = 2 * sectors * tile + ID_ROWS, rights.shape[0]
    psi_count = sectors * sectors
    left_sent, both_sent, swap_sent, far_sent = pl.pallas_call(
        pack_kernel,
        out_shape=[
            block((rows, tile)),
            block((rows + psi_count * tile, tile)),
            block((right_rows + rows, tile)),
            block((psi_count * tile, tile)),
        ],
        in_specs=[SMEM, ANY, ANY, ANY],
        out_specs=[VMEM] * 4,
        scratch_shapes=[pltpu.SemaphoreType.DMA((1 + 6 * sectors + 2 * psi_count,))],
        compiler_params=PARAMS,
        name="pack",
    )(*inputs)
    direct_a = over_z(left_sent, 2, 1)
    direct_b = over_z(both_sent, 1, 2)
    psi_far = to_third(far_sent)
    swapped = over_op(swap_sent, 1)
    passed_a = over_z(direct_a, 1, 0)
    passed_b = over_z(direct_b[:rows], 1, 0)

    def apply(kernel, name, outs, scalars, operands):
        return pl.pallas_call(
            kernel,
            out_shape=outs,
            in_specs=[SMEM] * len(scalars) + [VMEM] * len(operands),
            out_specs=[VMEM] * len(outs),
            compiler_params=PARAMS,
            cost_estimate=pl.CostEstimate(
                flops=64 * tile**3 * sectors**2, bytes_accessed=2**20, transcendentals=0
            ),
            name=name,
        )(*scalars, *operands)

    sizes = (left_sizes, right_sizes)
    total = jax.ShapeDtypeStruct(out_shape, jnp.float32)
    (near,) = apply(
        near_kernel, "near", [total], sizes,
        [psi, left_sent, swap_sent, swapped, direct_a, direct_b],
    )
    psi_turn, near = lax.optimization_barrier((psi_far, near))
    (wide,) = apply(
        mask_kernel, "mask", [block((sectors, tile, sectors * tile))], sizes,
        [direct_b, psi_turn],
    )
    sent, far = apply(
        far_kernel, "far", [block(out_shape), total], sizes,
        [direct_a, direct_b, passed_a, passed_b, swap_sent, swapped, near, wide],
    )
    arrived = over_op(sent, 2)
    kept = jnp.where(lax.axis_index("blk") // 2 == lax.axis_index("op") // 2, near, far)
    return (kept + arrived.astype(jnp.float32)).astype(jnp.bfloat16)


def wide_shards(psi, left_ops, right_ops, term_blocks, left_sizes, right_sizes):
    sectors_here = psi.shape[0]
    tile_size = psi.shape[2]
    left_first = lax.axis_index("blk") * sectors_here
    positions = lax.broadcasted_iota(jnp.int32, (tile_size,), 0)
    left_local = lax.dynamic_slice_in_dim(left_sizes, left_first, sectors_here)
    left_keep = positions[None, :] < left_local[:, None]
    right_keep = positions[None, :] < right_sizes[:, None]
    keep_mask = (left_keep[:, None, :, None] & right_keep[None, :, None, :]).astype(jnp.bfloat16)
    masked = psi * keep_mask
    acting_count = left_ops.shape[0] // 2
    order = jnp.argsort(1 - term_blocks, axis=0, stable=True)[:acting_count]
    ids_local = lax.dynamic_slice_in_dim(order, left_first, sectors_here, 1)
    sector_index = lax.broadcasted_iota(jnp.int32, (acting_count, sectors_here), 1)
    picked = left_ops[ids_local, sector_index]
    applied = jnp.einsum(
        "kaim,abmj->kabij", picked, masked, preferred_element_type=jnp.float32
    ).astype(jnp.bfloat16)
    arrived = lax.all_to_all(applied, "blk", split_axis=2, concat_axis=1, tiled=True)
    right_picked = right_ops[order]
    partial_value = jnp.einsum(
        "kabij,kablj->bail", arrived, right_picked, preferred_element_type=jnp.float32
    )
    summed = lax.psum_scatter(
        partial_value.astype(jnp.bfloat16), "op", scatter_dimension=1, tiled=True
    ).astype(jnp.float32)
    row_count = summed.shape[1]
    op_first = lax.axis_index("op") * row_count
    left_share = lax.dynamic_slice_in_dim(left_sizes, op_first, row_count)
    right_local = lax.dynamic_slice_in_dim(right_sizes, left_first, sectors_here)
    rows_keep = positions[None, :] < left_share[:, None]
    cols_keep = positions[None, :] < right_local[:, None]
    out_keep = (cols_keep[:, None, None, :] & rows_keep[None, :, :, None]).astype(jnp.float32)
    return (summed * out_keep).astype(jnp.bfloat16)


def solution(mesh):
    in_specs = (
        P(("parts", "blk"), None, None, None),
        P(("parts", "op"), "blk", None, None),
        P(("parts", "op"), "blk", None, None),
        P(("parts", "op"), None),
        P("parts"),
        P("parts"),
    )
    out_specs = P(("parts", "blk"), "op", None, None)
    nz, no = mesh.shape["blk"], mesh.shape["op"]
    body = shards if nz == no == 4 else wide_shards
    return jax.shard_map(body, mesh=mesh, in_specs=in_specs, out_specs=out_specs, check_vma=False)
```

```python
import functools

import jax
import jax.numpy as jnp
from jax import lax
from jax.experimental import pallas as pl
from jax.experimental.pallas import tpu as pltpu
from jax.sharding import PartitionSpec as P

ANY = pl.BlockSpec(memory_space=pl.ANY)
SMEM = pl.BlockSpec(memory_space=pltpu.SMEM)
VMEM = pl.BlockSpec(memory_space=pltpu.VMEM)
PARAMS = pltpu.CompilerParams(vmem_limit_bytes=32 * 1024 * 1024)
ID_ROWS = 16
TERMS = 4


def acting_terms(blocks_ref, sector):
    first = jnp.int32(0)
    second = jnp.int32(0)
    for term in reversed(range(blocks_ref.shape[0])):
        acts = blocks_ref[term, sector] > 0
        second = jnp.where(acts, first, second)
        first = jnp.where(acts, term, first)
    return first, second


def place():
    op = lax.axis_index("op")
    return lax.axis_index("blk"), lax.shift_right_logical(op, 1), jnp.bitwise_and(op, 1)


def is_home():
    z, _, c = place()
    return c == jnp.bitwise_and(z, 1)


def pack_kernel(blocks_ref, psi_ref, left_ref, right_ref, *rest):
    a_out, b_out, swap_out, far_out, sem = rest
    z, _, _ = place()
    sectors, tile = psi_ref.shape[0], psi_ref.shape[-1]
    count = 2 * sectors
    begin = right_ref.shape[0]
    copies = []

    def bring(source, out, spot, rows):
        copies.append(
            pltpu.make_async_copy(source, out.at[pl.ds(spot, rows)], sem.at[len(copies)])
        )

    bring(right_ref, swap_out, 0, begin)
    row = lax.broadcasted_iota(jnp.int32, (ID_ROWS, tile), 0)
    ids = jnp.zeros((ID_ROWS, tile), jnp.float32)
    for local in range(sectors):
        for slot, term in enumerate(acting_terms(blocks_ref, z * sectors + local)):
            spot = 2 * local + slot
            ids = jnp.where(row == spot, term.astype(jnp.float32), ids)
            for out, first in ((a_out, 0), (b_out, 0), (swap_out, begin)):
                bring(left_ref.at[term, local], out, first + spot * tile, tile)
    far = jnp.bitwise_xor(z, 3) * sectors
    for a, out in enumerate((a_out, b_out)):
        steps = (2, 1) if a == 0 else (1, 2)
        beside = jnp.bitwise_xor(z, jnp.where(is_home(), *steps)) * sectors
        for b in range(sectors):
            bring(psi_ref.at[a, beside + b], out, count * tile + ID_ROWS + b * tile, tile)
            bring(psi_ref.at[a, far + b], far_out, (sectors * a + b) * tile, tile)
    for copy in copies:
        copy.start()
    for out, first in ((a_out, 0), (b_out, 0), (swap_out, begin)):
        out[pl.ds(first + count * tile, ID_ROWS)] = ids.astype(jnp.bfloat16)
    for copy in copies:
        copy.wait()


def keep_mask(z, distance, sizes, a, b, sectors, tile):
    lsize_ref, rsize_ref = sizes
    rows = lax.broadcasted_iota(jnp.int32, (tile, tile), 0)
    lanes = lax.broadcasted_iota(jnp.int32, (tile, tile), 1)
    height = lsize_ref[jnp.bitwise_xor(z, distance) * sectors + a]
    return (rows < height) & (lanes < rsize_ref[z * sectors + b])


def wide_psi(z, distance, sizes, a, columns, blocks):
    tile = blocks[0].shape[-1]
    cut = []
    for b, block in zip(columns, blocks):
        keep = keep_mask(z, distance, sizes, a, b, len(blocks), tile)
        cut.append(jnp.where(keep, block.astype(jnp.float32), 0.0).astype(jnp.bfloat16))
    return jnp.concatenate(cut, axis=1)


def partial_sums(z, distance, sizes, columns, psi, lefts, rights, store):
    sectors = len(columns)
    for a in range(sectors):
        wide = psi(a)
        tile = wide.shape[0]
        applied = []
        for left in lefts:
            both = jnp.dot(left(a), wide, preferred_element_type=jnp.float32).astype(jnp.bfloat16)
            applied += [both[:tile], both[tile:]]
        for side, b in enumerate(columns):
            picked = [right(a, slot, b) for right in rights for slot in range(2)]
            column = [part[:, side * tile : (side + 1) * tile] for part in applied]
            total = lax.dot_general(
                jnp.concatenate(column, axis=1),
                jnp.concatenate(picked, axis=1),
                (((1,), (1,)), ((), ())),
                preferred_element_type=jnp.float32,
            )
            keep = keep_mask(z, distance, sizes, a, b, sectors, tile)
            store(b, a, jnp.where(keep, total, 0.0))


def message(ref, first, sectors, right_ref, terms=TERMS):
    tile = ref.shape[-1]
    ids = ref[pl.ds(first + 2 * sectors * tile, ID_ROWS)].astype(jnp.float32)

    def left(a):
        return ref[pl.ds(first + 2 * a * tile, 2 * tile)]

    def right(a, slot, b):
        spot = 2 * a + slot
        term = jnp.broadcast_to(ids[spot : spot + 1], (tile, tile))
        block = None
        for t in range(terms):
            other = right_ref[pl.ds((t * sectors + b) * tile, tile)].astype(jnp.float32)
            block = other if block is None else jnp.where(term == t, other, block)
        return block.astype(jnp.bfloat16)

    return left, right


def psi_rows(ref, first, a, sectors):
    tile = ref.shape[-1]
    return [ref[pl.ds(first + (sectors * a + b) * tile, tile)] for b in range(sectors)]


def near_kernel(lsize_ref, rsize_ref, *rest):
    psi_ref, swap_own, swapped, direct_a, direct_b, out_ref = rest
    z, _, _ = place()
    sectors, tile = out_ref.shape[0], out_ref.shape[-1]
    sizes, columns = (lsize_ref, rsize_ref), range(sectors)
    rows = 2 * sectors * tile + ID_ROWS
    begin = swap_own.shape[0] - rows

    def store(b, a, total):
        out_ref[b, a] = total

    for at_home in (True, False):

        @pl.when(is_home() == at_home)
        def _(at_home=at_home):
            if at_home:
                pair = [(swap_own, begin, sectors, swap_own), (swapped, begin, sectors, swapped)]
            else:
                pair = [(direct_b, 0, sectors, swap_own), (direct_a, 0, sectors, swapped)]

            def psi(a):
                if at_home:
                    blocks = [psi_ref[a, z * sectors + b] for b in columns]
                else:
                    blocks = psi_rows((direct_a, direct_b)[a], rows, 0, sectors)
                return wide_psi(z, 0 if at_home else 1, sizes, a, columns, blocks)

            lefts, rights = zip(*[message(*one) for one in pair])
            distance = 0 if at_home else 1
            partial_sums(z, distance, sizes, columns, psi, lefts, rights, store)


def mask_kernel(lsize_ref, rsize_ref, direct_a, direct_b, psi_far, wide_ref):
    z, _, _ = place()
    sectors = wide_ref.shape[0]
    columns = range(sectors)
    sizes = (lsize_ref, rsize_ref)
    first = 2 * sectors * wide_ref.shape[1] + ID_ROWS
    for at_home, distance in ((True, 2), (False, 3)):

        @pl.when(is_home() == at_home)
        def _(at_home=at_home, distance=distance):
            for a in columns:
                if at_home:
                    blocks = psi_rows((direct_a, direct_b)[a], first, 0, sectors)
                else:
                    blocks = psi_rows(psi_far, 0, a, sectors)
                wide_ref[a] = wide_psi(z, distance, sizes, a, columns, blocks)


def far_kernel(lsize_ref, rsize_ref, *rest):
    direct_a, direct_b, passed_a, passed_b, swap_own, swapped = rest[:6]
    near_ref, wide_ref, sent_ref, out_ref = rest[6:]
    z, x, _ = place()
    sectors = out_ref.shape[0]
    far_leaves = lax.shift_right_logical(z, 1) == x

    def store_sent(b, a, total):
        sent_ref[b, a] = total.astype(sent_ref.dtype)

    def store_kept(b, a, total):
        out_ref[b, a] = total
        sent_ref[b, a] = near_ref[b, a].astype(sent_ref.dtype)

    for leaves, store in ((True, store_sent), (False, store_kept)):
        for at_home, distance, first, second in (
            (True, 2, direct_a, direct_b),
            (False, 3, passed_a, passed_b),
        ):

            @pl.when((is_home() == at_home) & (far_leaves == leaves))
            def _(store=store, distance=distance, first=first, second=second):
                pair = ((first, 0, sectors, swap_own), (second, 0, sectors, swapped))
                lefts, rights = zip(*[message(*one) for one in pair])
                sizes, columns = (lsize_ref, rsize_ref), range(sectors)
                partial_sums(
                    z, distance, sizes, columns, lambda a: wide_ref[a], lefts, rights, store
                )


def shards(psi, left_ops, right_ops, term_blocks, left_sizes, right_sizes):
    n = 4
    sectors, tile = psi.shape[0], psi.shape[-1]
    block = functools.partial(jax.ShapeDtypeStruct, dtype=jnp.bfloat16)
    out_shape = (sectors, sectors, tile, tile)

    def over_op(array, step):
        return lax.ppermute(array, "op", [(o, o ^ step) for o in range(n)])

    def over_z(array, home_step, other_step):
        pairs = []
        for z in range(n):
            for o in range(n):
                step = home_step if o & 1 == z & 1 else other_step
                pairs.append((z * n + o, (z ^ step) * n + (o & 2) + (z & 1)))
        return lax.ppermute(array, ("blk", "op"), pairs)

    def to_third(array):
        pairs = []
        for z in range(n):
            for o in range(n):
                to = (z, o) if o & 1 == z & 1 else (z ^ 3, (o & 2) + (z & 1))
                pairs.append((z * n + o, to[0] * n + to[1]))
        return lax.ppermute(array, ("blk", "op"), pairs)

    rights = right_ops.reshape(-1, tile)
    inputs = [
        pltpu.with_memory_space_constraint(array, pltpu.HBM)
        for array in (term_blocks, psi, left_ops, rights)
    ]
    rows, right_rows = 2 * sectors * tile + ID_ROWS, rights.shape[0]
    psi_count = sectors * sectors
    sent_a, sent_b, swap_sent, far_sent = pl.pallas_call(
        pack_kernel,
        out_shape=[
            block((rows + sectors * tile, tile)),
            block((rows + sectors * tile, tile)),
            block((right_rows + rows, tile)),
            block((psi_count * tile, tile)),
        ],
        in_specs=[SMEM, ANY, ANY, ANY],
        out_specs=[VMEM] * 4,
        scratch_shapes=[pltpu.SemaphoreType.DMA((1 + 6 * sectors + 2 * psi_count,))],
        compiler_params=PARAMS,
        name="pack",
    )(*inputs)
    direct_a = over_z(sent_a, 2, 1)
    direct_b = over_z(sent_b, 1, 2)
    psi_far = to_third(far_sent)
    swapped = over_op(swap_sent, 1)
    passed_a = over_z(direct_a[:rows], 1, 0)
    passed_b = over_z(direct_b[:rows], 1, 0)

    def apply(kernel, name, outs, scalars, operands):
        return pl.pallas_call(
            kernel,
            out_shape=outs,
            in_specs=[SMEM] * len(scalars) + [VMEM] * len(operands),
            out_specs=[VMEM] * len(outs),
            compiler_params=PARAMS,
            cost_estimate=pl.CostEstimate(
                flops=64 * tile**3 * sectors**2, bytes_accessed=2**20, transcendentals=0
            ),
            name=name,
        )(*scalars, *operands)

    sizes = (left_sizes, right_sizes)
    total = jax.ShapeDtypeStruct(out_shape, jnp.float32)
    (near,) = apply(
        near_kernel, "near", [total], sizes,
        [psi, swap_sent, swapped, direct_a, direct_b],
    )
    psi_turn, near = lax.optimization_barrier((psi_far, near))
    (wide,) = apply(
        mask_kernel, "mask", [block((sectors, tile, sectors * tile))], sizes,
        [direct_a, direct_b, psi_turn],
    )
    sent, far = apply(
        far_kernel, "far", [block(out_shape), total], sizes,
        [direct_a, direct_b, passed_a, passed_b, swap_sent, swapped, near, wide],
    )
    arrived = over_op(sent, 2)
    kept = jnp.where(lax.axis_index("blk") // 2 == lax.axis_index("op") // 2, near, far)
    return (kept + arrived.astype(jnp.float32)).astype(jnp.bfloat16)


def wide_shards(psi, left_ops, right_ops, term_blocks, left_sizes, right_sizes):
    sectors_here = psi.shape[0]
    tile_size = psi.shape[2]
    left_first = lax.axis_index("blk") * sectors_here
    positions = lax.broadcasted_iota(jnp.int32, (tile_size,), 0)
    left_local = lax.dynamic_slice_in_dim(left_sizes, left_first, sectors_here)
    left_keep = positions[None, :] < left_local[:, None]
    right_keep = positions[None, :] < right_sizes[:, None]
    keep_mask = (left_keep[:, None, :, None] & right_keep[None, :, None, :]).astype(jnp.bfloat16)
    masked = psi * keep_mask
    acting_count = left_ops.shape[0] // 2
    order = jnp.argsort(1 - term_blocks, axis=0, stable=True)[:acting_count]
    ids_local = lax.dynamic_slice_in_dim(order, left_first, sectors_here, 1)
    sector_index = lax.broadcasted_iota(jnp.int32, (acting_count, sectors_here), 1)
    picked = left_ops[ids_local, sector_index]
    applied = jnp.einsum(
        "kaim,abmj->kabij", picked, masked, preferred_element_type=jnp.float32
    ).astype(jnp.bfloat16)
    arrived = lax.all_to_all(applied, "blk", split_axis=2, concat_axis=1, tiled=True)
    right_picked = right_ops[order]
    partial_value = jnp.einsum(
        "kabij,kablj->bail", arrived, right_picked, preferred_element_type=jnp.float32
    )
    summed = lax.psum_scatter(
        partial_value.astype(jnp.bfloat16), "op", scatter_dimension=1, tiled=True
    ).astype(jnp.float32)
    row_count = summed.shape[1]
    op_first = lax.axis_index("op") * row_count
    left_share = lax.dynamic_slice_in_dim(left_sizes, op_first, row_count)
    right_local = lax.dynamic_slice_in_dim(right_sizes, left_first, sectors_here)
    rows_keep = positions[None, :] < left_share[:, None]
    cols_keep = positions[None, :] < right_local[:, None]
    out_keep = (cols_keep[:, None, None, :] & rows_keep[None, :, :, None]).astype(jnp.float32)
    return (summed * out_keep).astype(jnp.bfloat16)


def solution(mesh):
    in_specs = (
        P(("parts", "blk"), None, None, None),
        P(("parts", "op"), "blk", None, None),
        P(("parts", "op"), "blk", None, None),
        P(("parts", "op"), None),
        P("parts"),
        P("parts"),
    )
    out_specs = P(("parts", "blk"), "op", None, None)
    nz, no = mesh.shape["blk"], mesh.shape["op"]
    body = shards if nz == no == 4 else wide_shards
    return jax.shard_map(body, mesh=mesh, in_specs=in_specs, out_specs=out_specs, check_vma=False)
```

```python
import functools

import jax
import jax.numpy as jnp
from jax import lax
from jax.experimental import pallas as pl
from jax.experimental.pallas import tpu as pltpu
from jax.sharding import PartitionSpec as P

ANY = pl.BlockSpec(memory_space=pl.ANY)
SMEM = pl.BlockSpec(memory_space=pltpu.SMEM)
VMEM = pl.BlockSpec(memory_space=pltpu.VMEM)
PARAMS = pltpu.CompilerParams(vmem_limit_bytes=32 * 1024 * 1024)
ID_ROWS = 16
FAR_PAD = 32


def acting_terms(blocks_ref, sector):
    first = jnp.int32(0)
    second = jnp.int32(0)
    for term in reversed(range(blocks_ref.shape[0])):
        acts = blocks_ref[term, sector] > 0
        second = jnp.where(acts, first, second)
        first = jnp.where(acts, term, first)
    return first, second


def place():
    op = lax.axis_index("op")
    return lax.axis_index("blk"), lax.shift_right_logical(op, 1), jnp.bitwise_and(op, 1)


def is_home():
    z, _, c = place()
    return c == jnp.bitwise_and(z, 1)


def pack_kernel(blocks_ref, psi_ref, left_ref, right_ref, *rest):
    left_out, side_out, far_out, right_out, sem = rest
    z, _, _ = place()
    sectors, tile = psi_ref.shape[0], psi_ref.shape[-1]
    count = 2 * sectors
    row = lax.broadcasted_iota(jnp.int32, (ID_ROWS, tile), 0)
    ids = jnp.zeros((ID_ROWS, tile), jnp.float32)
    picked = []
    for local in range(sectors):
        for term in acting_terms(blocks_ref, z * sectors + local):
            ids = jnp.where(row == len(picked), term.astype(jnp.float32), ids)
            picked.append(left_ref.at[term, local])
    near = jnp.bitwise_xor(z, 1) * sectors
    asked = [psi_ref.at[a, near + b] for a in range(sectors) for b in range(sectors)]

    def copies(sources, out, first):
        return [
            pltpu.make_async_copy(source, out.at[pl.ds(spot * tile, tile)], sem.at[first + spot])
            for spot, source in enumerate(sources)
        ]

    far = jnp.bitwise_xor(z, jnp.where(is_home(), 2, 3)) * sectors
    plain = copies(picked, left_out, 0)
    plain.append(pltpu.make_async_copy(right_ref, right_out, sem.at[2 * count]))
    wanted = [psi_ref.at[a, far + b] for a in range(sectors) for b in range(sectors)]
    plain += copies(wanted, far_out, 2 * count + 1)
    for copy in plain:
        copy.start()
    for at_home, sources in ((True, asked), (False, picked)):

        @pl.when(is_home() == at_home)
        def _(sources=sources):
            for copy in copies(sources, side_out, count):
                copy.start()

    for out in (left_out, side_out):
        out[pl.ds(count * tile, ID_ROWS)] = ids.astype(jnp.bfloat16)
    far_out[pl.ds(count * tile, FAR_PAD)] = jnp.zeros((FAR_PAD, tile), jnp.bfloat16)
    for copy in plain + copies(picked, side_out, count):
        copy.wait()


def keep_mask(z, distance, sizes, a, b, sectors, tile):
    lsize_ref, rsize_ref = sizes
    rows = lax.broadcasted_iota(jnp.int32, (tile, tile), 0)
    lanes = lax.broadcasted_iota(jnp.int32, (tile, tile), 1)
    height = lsize_ref[jnp.bitwise_xor(z, distance) * sectors + a]
    return (rows < height) & (lanes < rsize_ref[z * sectors + b])


def wide_psi(z, distance, sizes, a, columns, blocks):
    tile = blocks[0].shape[-1]
    cut = []
    for b, block in zip(columns, blocks):
        keep = keep_mask(z, distance, sizes, a, b, len(blocks), tile)
        cut.append(jnp.where(keep, block.astype(jnp.float32), 0.0).astype(jnp.bfloat16))
    return jnp.concatenate(cut, axis=1)


def partial_sums(z, distance, sizes, columns, psi, lefts, rights, store):
    sectors = len(columns)
    for a in range(sectors):
        wide = psi(a)
        tile = wide.shape[0]
        applied = []
        for left in lefts:
            both = jnp.dot(left(a), wide, preferred_element_type=jnp.float32).astype(jnp.bfloat16)
            applied += [both[:tile], both[tile:]]
        for side, b in enumerate(columns):
            picked = [right(a, slot, b) for right in rights for slot in range(2)]
            column = [part[:, side * tile : (side + 1) * tile] for part in applied]
            total = lax.dot_general(
                jnp.concatenate(column, axis=1),
                jnp.concatenate(picked, axis=1),
                (((1,), (1,)), ((), ())),
                preferred_element_type=jnp.float32,
            )
            keep = keep_mask(z, distance, sizes, a, b, sectors, tile)
            store(b, a, jnp.where(keep, total, 0.0))


def message(ref, right_ref):
    terms, sectors, tile = right_ref.shape[0], right_ref.shape[1], right_ref.shape[-1]
    ids = ref[pl.ds(2 * sectors * tile, ID_ROWS)].astype(jnp.float32)

    def left(a):
        return ref[pl.ds(2 * a * tile, 2 * tile)]

    def right(a, slot, b):
        spot = 2 * a + slot
        term = jnp.broadcast_to(ids[spot : spot + 1], (tile, tile))
        block = right_ref[0, b].astype(jnp.float32)
        for t in range(1, terms):
            block = jnp.where(term == t, right_ref[t, b].astype(jnp.float32), block)
        return block.astype(jnp.bfloat16)

    return left, right


def near_kernel(lsize_ref, rsize_ref, blocks_ref, *rest):
    psi_ref, left_ref, side, direct_a, direct_b, right_own, right_other, out_ref = rest
    z, _, _ = place()
    sectors, tile = out_ref.shape[0], out_ref.shape[-1]
    sizes, columns = (lsize_ref, rsize_ref), range(sectors)

    def store(b, a, total):
        out_ref[b, a] = total

    def masked(distance, a, blocks):
        return wide_psi(z, distance, sizes, a, columns, blocks)

    @pl.when(is_home())
    def _():
        terms = [acting_terms(blocks_ref, z * sectors + a) for a in columns]
        left, right = message(side, right_other)
        partial_sums(
            z, 0, sizes, columns,
            lambda a: masked(0, a, [psi_ref[a, z * sectors + b] for b in columns]),
            [lambda a: jnp.concatenate([left_ref[term, a] for term in terms[a]], axis=0), left],
            [lambda a, slot, b: right_own[terms[a][slot], b], right],
            store,
        )

    @pl.when(jnp.logical_not(is_home()))
    def _():
        lefts, rights = zip(message(direct_b, right_own), message(direct_a, right_other))

        def psi(a):
            return masked(1, a, [side[pl.ds((sectors * a + b) * tile, tile)] for b in columns])

        partial_sums(z, 1, sizes, columns, psi, lefts, rights, store)


def far_kernel(lsize_ref, rsize_ref, *rest):
    direct_a, direct_b, passed_a, passed_b, right_own, right_other = rest[:6]
    near_ref, psi_ref, sent_ref, out_ref = rest[6:]
    z, x, _ = place()
    sectors, tile = out_ref.shape[0], out_ref.shape[-1]
    columns = range(sectors)
    far_leaves = lax.shift_right_logical(z, 1) == x

    def store_sent(b, a, total):
        sent_ref[b, a] = total.astype(sent_ref.dtype)

    def store_kept(b, a, total):
        out_ref[b, a] = total
        sent_ref[b, a] = near_ref[b, a].astype(sent_ref.dtype)

    for leaves, store in ((True, store_sent), (False, store_kept)):
        for at_home, distance, first, second in (
            (True, 2, direct_a, direct_b),
            (False, 3, passed_a, passed_b),
        ):

            @pl.when((is_home() == at_home) & (far_leaves == leaves))
            def _(store=store, distance=distance, first=first, second=second):
                lefts, rights = zip(message(first, right_own), message(second, right_other))
                sizes = (lsize_ref, rsize_ref)

                def psi(a):
                    blocks = [psi_ref[pl.ds((sectors * a + b) * tile, tile)] for b in columns]
                    return wide_psi(z, distance, sizes, a, columns, blocks)

                partial_sums(z, distance, sizes, columns, psi, lefts, rights, store)


def shards(psi, left_ops, right_ops, term_blocks, left_sizes, right_sizes):
    n = 4
    sectors, tile = psi.shape[0], psi.shape[-1]
    block = functools.partial(jax.ShapeDtypeStruct, dtype=jnp.bfloat16)
    out_shape = (sectors, sectors, tile, tile)
    message_shape = (2 * sectors * tile + ID_ROWS, tile)

    def over_op(array, step):
        return lax.ppermute(array, "op", [(o, o ^ step) for o in range(n)])

    def over_z(array, home_step, other_step):
        pairs = []
        for z in range(n):
            for o in range(n):
                step = home_step if o & 1 == z & 1 else other_step
                pairs.append((z * n + o, (z ^ step) * n + (o & 2) + (z & 1)))
        return lax.ppermute(array, ("blk", "op"), pairs)

    psi_hbm, left_hbm, right_hbm, blocks_hbm = [
        pltpu.with_memory_space_constraint(array, pltpu.HBM)
        for array in (psi, left_ops, right_ops, term_blocks)
    ]
    left_sent, side_sent, far_sent, right_own = pl.pallas_call(
        pack_kernel,
        out_shape=[
            block(message_shape),
            block(message_shape),
            block((sectors * sectors * tile + FAR_PAD, tile)),
            block(right_ops.shape),
        ],
        in_specs=[SMEM, ANY, ANY, ANY],
        out_specs=[VMEM] * 4,
        scratch_shapes=[pltpu.SemaphoreType.DMA((4 * sectors + 1 + sectors**2,))],
        compiler_params=PARAMS,
        name="pack",
    )(blocks_hbm, psi_hbm, left_hbm, right_hbm)
    direct_a = over_z(left_sent, 2, 1)
    direct_b = over_z(left_sent, 1, 2)
    psi_far = over_z(far_sent, 2, 3)
    side = over_z(side_sent, 1, 0)
    passed_a = over_z(direct_a, 1, 0)
    passed_b = over_z(direct_b, 1, 0)
    right_other = over_op(right_own, 1)

    def apply(kernel, name, outs, scalars, operands):
        return pl.pallas_call(
            kernel,
            out_shape=outs,
            in_specs=[SMEM] * len(scalars) + [VMEM] * len(operands),
            out_specs=[VMEM] * len(outs),
            compiler_params=PARAMS,
            cost_estimate=pl.CostEstimate(
                flops=64 * tile**3 * sectors**2, bytes_accessed=2**20, transcendentals=0
            ),
            name=name,
        )(*scalars, *operands)

    sizes = (left_sizes, right_sizes)
    rights = [right_own, right_other]
    total = jax.ShapeDtypeStruct(out_shape, jnp.float32)
    (near,) = apply(
        near_kernel, "near", [total], sizes + (term_blocks,),
        [psi, left_ops, side, direct_a, direct_b] + rights,
    )
    sent, far = apply(
        far_kernel, "far", [block(out_shape), total], sizes,
        [direct_a, direct_b, passed_a, passed_b] + rights + [near, psi_far],
    )
    arrived = over_op(sent, 2)
    kept = jnp.where(lax.axis_index("blk") // 2 == lax.axis_index("op") // 2, near, far)
    return (kept + arrived.astype(jnp.float32)).astype(jnp.bfloat16)


def wide_shards(psi, left_ops, right_ops, term_blocks, left_sizes, right_sizes):
    sectors_here = psi.shape[0]
    tile_size = psi.shape[2]
    left_first = lax.axis_index("blk") * sectors_here
    positions = lax.broadcasted_iota(jnp.int32, (tile_size,), 0)
    left_local = lax.dynamic_slice_in_dim(left_sizes, left_first, sectors_here)
    left_keep = positions[None, :] < left_local[:, None]
    right_keep = positions[None, :] < right_sizes[:, None]
    keep_mask = (left_keep[:, None, :, None] & right_keep[None, :, None, :]).astype(jnp.bfloat16)
    masked = psi * keep_mask
    acting_count = left_ops.shape[0] // 2
    order = jnp.argsort(1 - term_blocks, axis=0, stable=True)[:acting_count]
    ids_local = lax.dynamic_slice_in_dim(order, left_first, sectors_here, 1)
    sector_index = lax.broadcasted_iota(jnp.int32, (acting_count, sectors_here), 1)
    picked = left_ops[ids_local, sector_index]
    applied = jnp.einsum(
        "kaim,abmj->kabij", picked, masked, preferred_element_type=jnp.float32
    ).astype(jnp.bfloat16)
    arrived = lax.all_to_all(applied, "blk", split_axis=2, concat_axis=1, tiled=True)
    right_picked = right_ops[order]
    partial_value = jnp.einsum(
        "kabij,kablj->bail", arrived, right_picked, preferred_element_type=jnp.float32
    )
    summed = lax.psum_scatter(
        partial_value.astype(jnp.bfloat16), "op", scatter_dimension=1, tiled=True
    ).astype(jnp.float32)
    row_count = summed.shape[1]
    op_first = lax.axis_index("op") * row_count
    left_share = lax.dynamic_slice_in_dim(left_sizes, op_first, row_count)
    right_local = lax.dynamic_slice_in_dim(right_sizes, left_first, sectors_here)
    rows_keep = positions[None, :] < left_share[:, None]
    cols_keep = positions[None, :] < right_local[:, None]
    out_keep = (cols_keep[:, None, None, :] & rows_keep[None, :, :, None]).astype(jnp.float32)
    return (summed * out_keep).astype(jnp.bfloat16)


def solution(mesh):
    in_specs = (
        P(("parts", "blk"), None, None, None),
        P(("parts", "op"), "blk", None, None),
        P(("parts", "op"), "blk", None, None),
        P(("parts", "op"), None),
        P("parts"),
        P("parts"),
    )
    out_specs = P(("parts", "blk"), "op", None, None)
    nz, no = mesh.shape["blk"], mesh.shape["op"]
    body = shards if nz == no == 4 else wide_shards
    return jax.shard_map(body, mesh=mesh, in_specs=in_specs, out_specs=out_specs, check_vma=False)
```

```python
import functools

import jax
import jax.numpy as jnp
from jax import lax
from jax.experimental import pallas as pl
from jax.experimental.pallas import tpu as pltpu
from jax.sharding import PartitionSpec as P

ANY = pl.BlockSpec(memory_space=pl.ANY)
SMEM = pl.BlockSpec(memory_space=pltpu.SMEM)
VMEM = pl.BlockSpec(memory_space=pltpu.VMEM)
PARAMS = pltpu.CompilerParams(vmem_limit_bytes=32 * 1024 * 1024)
ID_ROWS = 16
FAR_PAD = 32


def acting_terms(blocks_ref, sector):
    first = jnp.int32(0)
    second = jnp.int32(0)
    for term in reversed(range(blocks_ref.shape[0])):
        acts = blocks_ref[term, sector] > 0
        second = jnp.where(acts, first, second)
        first = jnp.where(acts, term, first)
    return first, second


def place():
    op = lax.axis_index("op")
    return lax.axis_index("blk"), lax.shift_right_logical(op, 1), jnp.bitwise_and(op, 1)


def is_home():
    z, _, c = place()
    return c == jnp.bitwise_and(z, 1)


def pack_kernel(blocks_ref, psi_ref, left_ref, right_ref, *rest):
    left_out, side_out, far_out, right_out, sem = rest
    z, _, _ = place()
    sectors, tile = psi_ref.shape[0], psi_ref.shape[-1]
    count = 2 * sectors
    row = lax.broadcasted_iota(jnp.int32, (ID_ROWS, tile), 0)
    ids = jnp.zeros((ID_ROWS, tile), jnp.float32)
    picked = []
    for local in range(sectors):
        for term in acting_terms(blocks_ref, z * sectors + local):
            ids = jnp.where(row == len(picked), term.astype(jnp.float32), ids)
            picked.append(left_ref.at[term, local])
    near = jnp.bitwise_xor(z, 1) * sectors
    asked = [psi_ref.at[a, near + b] for a in range(sectors) for b in range(sectors)]

    def copies(sources, out, first):
        return [
            pltpu.make_async_copy(source, out.at[pl.ds(spot * tile, tile)], sem.at[first + spot])
            for spot, source in enumerate(sources)
        ]

    far = jnp.bitwise_xor(z, jnp.where(is_home(), 2, 3)) * sectors
    plain = copies(picked, left_out, 0)
    plain.append(pltpu.make_async_copy(right_ref, right_out, sem.at[2 * count]))
    wanted = [psi_ref.at[a, far + b] for a in range(sectors) for b in range(sectors)]
    plain += copies(wanted, far_out, 2 * count + 1)
    for copy in plain:
        copy.start()
    for at_home, sources in ((True, asked), (False, picked)):

        @pl.when(is_home() == at_home)
        def _(sources=sources):
            for copy in copies(sources, side_out, count):
                copy.start()

    for out in (left_out, side_out):
        out[pl.ds(count * tile, ID_ROWS)] = ids.astype(jnp.bfloat16)
    far_out[pl.ds(count * tile, FAR_PAD)] = jnp.zeros((FAR_PAD, tile), jnp.bfloat16)
    for copy in plain + copies(picked, side_out, count):
        copy.wait()


def keep_mask(z, distance, sizes, a, b, sectors, tile):
    lsize_ref, rsize_ref = sizes
    rows = lax.broadcasted_iota(jnp.int32, (tile, tile), 0)
    lanes = lax.broadcasted_iota(jnp.int32, (tile, tile), 1)
    height = lsize_ref[jnp.bitwise_xor(z, distance) * sectors + a]
    return (rows < height) & (lanes < rsize_ref[z * sectors + b])


def wide_psi(z, distance, sizes, a, columns, blocks):
    tile = blocks[0].shape[-1]
    cut = []
    for b, block in zip(columns, blocks):
        keep = keep_mask(z, distance, sizes, a, b, len(blocks), tile)
        cut.append(jnp.where(keep, block.astype(jnp.float32), 0.0).astype(jnp.bfloat16))
    return jnp.concatenate(cut, axis=1)


def partial_sums(z, distance, sizes, columns, psi, lefts, rights, store):
    sectors = len(columns)
    for a in range(sectors):
        wide = psi(a)
        tile = wide.shape[0]
        applied = []
        for left in lefts:
            both = jnp.dot(left(a), wide, preferred_element_type=jnp.float32).astype(jnp.bfloat16)
            applied += [both[:tile], both[tile:]]
        for side, b in enumerate(columns):
            picked = [right(a, slot, b) for right in rights for slot in range(2)]
            column = [part[:, side * tile : (side + 1) * tile] for part in applied]
            total = lax.dot_general(
                jnp.concatenate(column, axis=1),
                jnp.concatenate(picked, axis=1),
                (((1,), (1,)), ((), ())),
                preferred_element_type=jnp.float32,
            )
            keep = keep_mask(z, distance, sizes, a, b, sectors, tile)
            store(b, a, jnp.where(keep, total, 0.0))


def message(ref, right_ref):
    terms, sectors, tile = right_ref.shape[0], right_ref.shape[1], right_ref.shape[-1]
    ids = ref[pl.ds(2 * sectors * tile, ID_ROWS)].astype(jnp.float32)

    def left(a):
        return ref[pl.ds(2 * a * tile, 2 * tile)]

    def right(a, slot, b):
        spot = 2 * a + slot
        term = jnp.broadcast_to(ids[spot : spot + 1], (tile, tile))
        block = right_ref[0, b].astype(jnp.float32)
        for t in range(1, terms):
            block = jnp.where(term == t, right_ref[t, b].astype(jnp.float32), block)
        return block.astype(jnp.bfloat16)

    return left, right


def near_kernel(lsize_ref, rsize_ref, blocks_ref, *rest):
    psi_ref, left_ref, side, direct_a, direct_b, right_own, right_other, out_ref = rest
    z, _, _ = place()
    sectors, tile = out_ref.shape[0], out_ref.shape[-1]
    sizes, columns = (lsize_ref, rsize_ref), range(sectors)

    def store(b, a, total):
        out_ref[b, a] = total

    def masked(distance, a, blocks):
        return wide_psi(z, distance, sizes, a, columns, blocks)

    @pl.when(is_home())
    def _():
        terms = [acting_terms(blocks_ref, z * sectors + a) for a in columns]
        left, right = message(side, right_other)
        partial_sums(
            z, 0, sizes, columns,
            lambda a: masked(0, a, [psi_ref[a, z * sectors + b] for b in columns]),
            [lambda a: jnp.concatenate([left_ref[term, a] for term in terms[a]], axis=0), left],
            [lambda a, slot, b: right_own[terms[a][slot], b], right],
            store,
        )

    @pl.when(jnp.logical_not(is_home()))
    def _():
        lefts, rights = zip(message(direct_b, right_own), message(direct_a, right_other))

        def psi(a):
            return masked(1, a, [side[pl.ds((sectors * a + b) * tile, tile)] for b in columns])

        partial_sums(z, 1, sizes, columns, psi, lefts, rights, store)


def far_kernel(lsize_ref, rsize_ref, *rest):
    direct_a, direct_b, passed_a, passed_b, right_own, right_other = rest[:6]
    near_ref, psi_ref, out_ref = rest[6:9]
    sent_refs = rest[9:]
    z, x, _ = place()
    sectors, tile = out_ref.shape[0], out_ref.shape[-1]
    columns = range(sectors)
    far_leaves = lax.shift_right_logical(z, 1) == x

    def store_sent(b, a, total):
        sent_refs[b][a] = total.astype(sent_refs[b].dtype)

    def store_kept(b, a, total):
        out_ref[b, a] = total
        sent_refs[b][a] = near_ref[b, a].astype(sent_refs[b].dtype)

    for leaves, store in ((True, store_sent), (False, store_kept)):
        for at_home, distance, first, second in (
            (True, 2, direct_a, direct_b),
            (False, 3, passed_a, passed_b),
        ):

            @pl.when((is_home() == at_home) & (far_leaves == leaves))
            def _(store=store, distance=distance, first=first, second=second):
                lefts, rights = zip(message(first, right_own), message(second, right_other))
                sizes = (lsize_ref, rsize_ref)

                def psi(a):
                    blocks = [psi_ref[pl.ds((sectors * a + b) * tile, tile)] for b in columns]
                    return wide_psi(z, distance, sizes, a, columns, blocks)

                partial_sums(z, distance, sizes, columns, psi, lefts, rights, store)


def shards(psi, left_ops, right_ops, term_blocks, left_sizes, right_sizes):
    n = 4
    sectors, tile = psi.shape[0], psi.shape[-1]
    block = functools.partial(jax.ShapeDtypeStruct, dtype=jnp.bfloat16)
    out_shape = (sectors, sectors, tile, tile)
    message_shape = (2 * sectors * tile + ID_ROWS, tile)

    def over_op(array, step):
        return lax.ppermute(array, "op", [(o, o ^ step) for o in range(n)])

    def over_z(array, home_step, other_step):
        pairs = []
        for z in range(n):
            for o in range(n):
                step = home_step if o & 1 == z & 1 else other_step
                pairs.append((z * n + o, (z ^ step) * n + (o & 2) + (z & 1)))
        return lax.ppermute(array, ("blk", "op"), pairs)

    psi_hbm, left_hbm, right_hbm, blocks_hbm = [
        pltpu.with_memory_space_constraint(array, pltpu.HBM)
        for array in (psi, left_ops, right_ops, term_blocks)
    ]
    left_sent, side_sent, far_sent, right_own = pl.pallas_call(
        pack_kernel,
        out_shape=[
            block(message_shape),
            block(message_shape),
            block((sectors * sectors * tile + FAR_PAD, tile)),
            block(right_ops.shape),
        ],
        in_specs=[SMEM, ANY, ANY, ANY],
        out_specs=[VMEM] * 4,
        scratch_shapes=[pltpu.SemaphoreType.DMA((4 * sectors + 1 + sectors**2,))],
        compiler_params=PARAMS,
        name="pack",
    )(blocks_hbm, psi_hbm, left_hbm, right_hbm)
    direct_a = over_z(left_sent, 2, 1)
    direct_b = over_z(left_sent, 1, 2)
    psi_far = over_z(far_sent, 2, 3)
    side = over_z(side_sent, 1, 0)
    passed_a = over_z(direct_a, 1, 0)
    passed_b = over_z(direct_b, 1, 0)
    right_other = over_op(right_own, 1)

    def apply(kernel, name, outs, scalars, operands):
        return pl.pallas_call(
            kernel,
            out_shape=outs,
            in_specs=[SMEM] * len(scalars) + [VMEM] * len(operands),
            out_specs=[VMEM] * len(outs),
            compiler_params=PARAMS,
            cost_estimate=pl.CostEstimate(
                flops=64 * tile**3 * sectors**2, bytes_accessed=2**20, transcendentals=0
            ),
            name=name,
        )(*scalars, *operands)

    sizes = (left_sizes, right_sizes)
    rights = [right_own, right_other]
    total = jax.ShapeDtypeStruct(out_shape, jnp.float32)
    (near,) = apply(
        near_kernel, "near", [total], sizes + (term_blocks,),
        [psi, left_ops, side, direct_a, direct_b] + rights,
    )
    far, *sent = apply(
        far_kernel, "far", [total] + [block((sectors, tile, tile))] * sectors, sizes,
        [direct_a, direct_b, passed_a, passed_b] + rights + [near, psi_far],
    )
    first, second = [over_op(part, 2)[None] for part in sent]
    places = lax.broadcasted_iota(jnp.int32, out_shape, 0)
    arrived = jnp.where(places == 0, first, second)
    kept = jnp.where(lax.axis_index("blk") // 2 == lax.axis_index("op") // 2, near, far)
    return (kept + arrived.astype(jnp.float32)).astype(jnp.bfloat16)


def wide_shards(psi, left_ops, right_ops, term_blocks, left_sizes, right_sizes):
    sectors_here = psi.shape[0]
    tile_size = psi.shape[2]
    left_first = lax.axis_index("blk") * sectors_here
    positions = lax.broadcasted_iota(jnp.int32, (tile_size,), 0)
    left_local = lax.dynamic_slice_in_dim(left_sizes, left_first, sectors_here)
    left_keep = positions[None, :] < left_local[:, None]
    right_keep = positions[None, :] < right_sizes[:, None]
    keep_mask = (left_keep[:, None, :, None] & right_keep[None, :, None, :]).astype(jnp.bfloat16)
    masked = psi * keep_mask
    acting_count = left_ops.shape[0] // 2
    order = jnp.argsort(1 - term_blocks, axis=0, stable=True)[:acting_count]
    ids_local = lax.dynamic_slice_in_dim(order, left_first, sectors_here, 1)
    sector_index = lax.broadcasted_iota(jnp.int32, (acting_count, sectors_here), 1)
    picked = left_ops[ids_local, sector_index]
    applied = jnp.einsum(
        "kaim,abmj->kabij", picked, masked, preferred_element_type=jnp.float32
    ).astype(jnp.bfloat16)
    arrived = lax.all_to_all(applied, "blk", split_axis=2, concat_axis=1, tiled=True)
    right_picked = right_ops[order]
    partial_value = jnp.einsum(
        "kabij,kablj->bail", arrived, right_picked, preferred_element_type=jnp.float32
    )
    summed = lax.psum_scatter(
        partial_value.astype(jnp.bfloat16), "op", scatter_dimension=1, tiled=True
    ).astype(jnp.float32)
    row_count = summed.shape[1]
    op_first = lax.axis_index("op") * row_count
    left_share = lax.dynamic_slice_in_dim(left_sizes, op_first, row_count)
    right_local = lax.dynamic_slice_in_dim(right_sizes, left_first, sectors_here)
    rows_keep = positions[None, :] < left_share[:, None]
    cols_keep = positions[None, :] < right_local[:, None]
    out_keep = (cols_keep[:, None, None, :] & rows_keep[None, :, :, None]).astype(jnp.float32)
    return (summed * out_keep).astype(jnp.bfloat16)


def solution(mesh):
    in_specs = (
        P(("parts", "blk"), None, None, None),
        P(("parts", "op"), "blk", None, None),
        P(("parts", "op"), "blk", None, None),
        P(("parts", "op"), None),
        P("parts"),
        P("parts"),
    )
    out_specs = P(("parts", "blk"), "op", None, None)
    nz, no = mesh.shape["blk"], mesh.shape["op"]
    body = shards if nz == no == 4 else wide_shards
    return jax.shard_map(body, mesh=mesh, in_specs=in_specs, out_specs=out_specs, check_vma=False)
```

```python
import functools

import jax
import jax.numpy as jnp
from jax import lax
from jax.experimental import pallas as pl
from jax.experimental.pallas import tpu as pltpu
from jax.sharding import PartitionSpec as P

ANY = pl.BlockSpec(memory_space=pl.ANY)
SMEM = pl.BlockSpec(memory_space=pltpu.SMEM)
VMEM = pl.BlockSpec(memory_space=pltpu.VMEM)
PARAMS = pltpu.CompilerParams(vmem_limit_bytes=32 * 1024 * 1024)
ID_ROWS = 16
FAR_PAD = 32


def acting_terms(blocks_ref, sector):
    first = jnp.int32(0)
    second = jnp.int32(0)
    for term in reversed(range(blocks_ref.shape[0])):
        acts = blocks_ref[term, sector] > 0
        second = jnp.where(acts, first, second)
        first = jnp.where(acts, term, first)
    return first, second


def place():
    op = lax.axis_index("op")
    return lax.axis_index("blk"), lax.shift_right_logical(op, 1), jnp.bitwise_and(op, 1)


def is_home():
    z, _, c = place()
    return c == jnp.bitwise_and(z, 1)


def pack_kernel(blocks_hbm, psi_ref, left_ref, right_ref, *rest):
    left_out, side_out, far_out, right_out, blocks_ref, left_all, sem = rest
    z, _, _ = place()
    sectors, tile = psi_ref.shape[0], psi_ref.shape[-1]
    count = 2 * sectors
    near = jnp.bitwise_xor(z, 1) * sectors
    far = jnp.bitwise_xor(z, jnp.where(is_home(), 2, 3)) * sectors

    def psi_copies(column, out, first):
        return [
            pltpu.make_async_copy(
                psi_ref.at[a, column + b],
                out.at[pl.ds((sectors * a + b) * tile, tile)],
                sem.at[first + sectors * a + b],
            )
            for a in range(sectors)
            for b in range(sectors)
        ]

    table = pltpu.make_async_copy(blocks_hbm, blocks_ref, sem.at[0])
    lefts = pltpu.make_async_copy(left_ref, left_all, sem.at[1])
    others = [pltpu.make_async_copy(right_ref, right_out, sem.at[2])]
    others += psi_copies(far, far_out, 3)
    sides = psi_copies(near, side_out, 3 + sectors * sectors)
    for copy in [table, lefts] + others:
        copy.start()

    @pl.when(is_home())
    def _():
        for copy in sides:
            copy.start()

    far_out[pl.ds(count * tile, FAR_PAD)] = jnp.zeros((FAR_PAD, tile), jnp.bfloat16)
    table.wait()
    row = lax.broadcasted_iota(jnp.int32, (ID_ROWS, tile), 0)
    ids = jnp.zeros((ID_ROWS, tile), jnp.float32)
    picked = []
    for local in range(sectors):
        for term in acting_terms(blocks_ref, z * sectors + local):
            ids = jnp.where(row == len(picked), term.astype(jnp.float32), ids)
            picked.append((term, local))
    for out in (left_out, side_out):
        out[pl.ds(count * tile, ID_ROWS)] = ids.astype(jnp.bfloat16)
    lefts.wait()
    for spot, (term, local) in enumerate(picked):
        left_out[pl.ds(spot * tile, tile)] = left_all[term, local]

    @pl.when(is_home())
    def _():
        for copy in sides:
            copy.wait()

    @pl.when(jnp.logical_not(is_home()))
    def _():
        for spot, (term, local) in enumerate(picked):
            side_out[pl.ds(spot * tile, tile)] = left_all[term, local]

    for copy in others:
        copy.wait()


def keep_mask(z, distance, sizes, a, b, sectors, tile):
    lsize_ref, rsize_ref = sizes
    rows = lax.broadcasted_iota(jnp.int32, (tile, tile), 0)
    lanes = lax.broadcasted_iota(jnp.int32, (tile, tile), 1)
    height = lsize_ref[jnp.bitwise_xor(z, distance) * sectors + a]
    return (rows < height) & (lanes < rsize_ref[z * sectors + b])


def wide_psi(keep, a, blocks):
    cut = []
    for b, block in enumerate(blocks):
        cut.append(jnp.where(keep(a, b), block.astype(jnp.float32), 0.0).astype(jnp.bfloat16))
    return jnp.concatenate(cut, axis=1)


def partial_sums(sectors, keep, psi, lefts, rights, store):
    for a in range(sectors):
        wide = wide_psi(keep, a, psi(a))
        tile = wide.shape[0]
        applied = []
        for left in lefts:
            both = jnp.dot(left(a), wide, preferred_element_type=jnp.float32).astype(jnp.bfloat16)
            applied += [both[:tile], both[tile:]]
        for b in range(sectors):
            picked = [right(a, slot, b) for right in rights for slot in range(2)]
            column = [part[:, b * tile : (b + 1) * tile] for part in applied]
            total = lax.dot_general(
                jnp.concatenate(column, axis=1),
                jnp.concatenate(picked, axis=1),
                (((1,), (1,)), ((), ())),
                preferred_element_type=jnp.float32,
            )
            store(b, a, jnp.where(keep(a, b), total, 0.0))


def message(ref, right_ref):
    terms, sectors, tile = right_ref.shape[0], right_ref.shape[1], right_ref.shape[-1]
    ids = ref[pl.ds(2 * sectors * tile, ID_ROWS)].astype(jnp.float32)

    def left(a):
        return ref[pl.ds(2 * a * tile, 2 * tile)]

    def right(a, slot, b):
        spot = 2 * a + slot
        term = jnp.broadcast_to(ids[spot : spot + 1], (tile, tile))
        block = right_ref[0, b].astype(jnp.float32)
        for t in range(1, terms):
            block = jnp.where(term == t, right_ref[t, b].astype(jnp.float32), block)
        return block.astype(jnp.bfloat16)

    return left, right


def near_kernel(lsize_ref, rsize_ref, blocks_ref, *rest):
    psi_ref, left_ref, side, direct_a, direct_b, right_own, right_other = rest[:7]
    out_ref, mask_ref = rest[7:]
    z, _, _ = place()
    sectors, tile = out_ref.shape[0], out_ref.shape[-1]
    columns = range(sectors)

    def masks(distance):
        return lambda a, b: keep_mask(z, distance, (lsize_ref, rsize_ref), a, b, sectors, tile)

    far = masks(jnp.where(is_home(), 2, 3))
    for a in columns:
        for b in columns:
            mask_ref[a, b] = jnp.where(far(a, b), 1.0, 0.0).astype(mask_ref.dtype)

    def store(b, a, total):
        out_ref[b, a] = total

    @pl.when(is_home())
    def _():
        terms = [acting_terms(blocks_ref, z * sectors + a) for a in columns]
        left, right = message(side, right_other)
        partial_sums(
            sectors, masks(0),
            lambda a: [psi_ref[a, z * sectors + b] for b in columns],
            [lambda a: jnp.concatenate([left_ref[term, a] for term in terms[a]], axis=0), left],
            [lambda a, slot, b: right_own[terms[a][slot], b], right],
            store,
        )

    @pl.when(jnp.logical_not(is_home()))
    def _():
        lefts, rights = zip(message(direct_b, right_own), message(direct_a, right_other))

        def psi(a):
            return [side[pl.ds((sectors * a + b) * tile, tile)] for b in columns]

        partial_sums(sectors, masks(1), psi, lefts, rights, store)


def far_kernel(*refs):
    direct_a, direct_b, passed_a, passed_b, right_own, right_other = refs[:6]
    near_ref, mask_ref, psi_ref, sent_ref, out_ref = refs[6:]
    z, x, _ = place()
    sectors, tile = out_ref.shape[0], out_ref.shape[-1]
    far_leaves = lax.shift_right_logical(z, 1) == x

    def store_sent(b, a, total):
        sent_ref[b, a] = total.astype(sent_ref.dtype)

    def store_kept(b, a, total):
        out_ref[b, a] = total
        sent_ref[b, a] = near_ref[b, a].astype(sent_ref.dtype)

    def keep(a, b):
        return mask_ref[a, b].astype(jnp.float32) > 0

    def psi(a):
        return [psi_ref[pl.ds((sectors * a + b) * tile, tile)] for b in range(sectors)]

    for leaves, store in ((True, store_sent), (False, store_kept)):
        for at_home, first, second in (
            (True, direct_a, direct_b),
            (False, passed_a, passed_b),
        ):

            @pl.when((is_home() == at_home) & (far_leaves == leaves))
            def _(store=store, first=first, second=second):
                lefts, rights = zip(message(first, right_own), message(second, right_other))
                partial_sums(sectors, keep, psi, lefts, rights, store)


def shards(psi, left_ops, right_ops, term_blocks, left_sizes, right_sizes):
    n = 4
    sectors, tile = psi.shape[0], psi.shape[-1]
    block = functools.partial(jax.ShapeDtypeStruct, dtype=jnp.bfloat16)
    out_shape = (sectors, sectors, tile, tile)
    message_shape = (2 * sectors * tile + ID_ROWS, tile)

    def over_op(array, step):
        return lax.ppermute(array, "op", [(o, o ^ step) for o in range(n)])

    def over_z(array, home_step, other_step):
        pairs = []
        for z in range(n):
            for o in range(n):
                step = home_step if o & 1 == z & 1 else other_step
                pairs.append((z * n + o, (z ^ step) * n + (o & 2) + (z & 1)))
        return lax.ppermute(array, ("blk", "op"), pairs)

    psi_hbm, left_hbm, right_hbm, blocks_hbm = [
        pltpu.with_memory_space_constraint(array, pltpu.HBM)
        for array in (psi, left_ops, right_ops, term_blocks)
    ]
    left_sent, side_sent, far_sent, right_own = pl.pallas_call(
        pack_kernel,
        out_shape=[
            block(message_shape),
            block(message_shape),
            block((sectors * sectors * tile + FAR_PAD, tile)),
            block(right_ops.shape),
        ],
        in_specs=[ANY] * 4,
        out_specs=[VMEM] * 4,
        scratch_shapes=[
            pltpu.SMEM(term_blocks.shape, jnp.int32),
            pltpu.VMEM(left_ops.shape, jnp.bfloat16),
            pltpu.SemaphoreType.DMA((3 + 2 * sectors**2,)),
        ],
        compiler_params=PARAMS,
        name="pack",
    )(blocks_hbm, psi_hbm, left_hbm, right_hbm)
    direct_a = over_z(left_sent, 2, 1)
    direct_b = over_z(left_sent, 1, 2)
    psi_far = over_z(far_sent, 2, 3)
    side = over_z(side_sent, 1, 0)
    passed_a = over_z(direct_a, 1, 0)
    passed_b = over_z(direct_b, 1, 0)
    right_other = over_op(right_own, 1)

    def apply(kernel, name, outs, scalars, operands):
        return pl.pallas_call(
            kernel,
            out_shape=outs,
            in_specs=[SMEM] * len(scalars) + [VMEM] * len(operands),
            out_specs=[VMEM] * len(outs),
            compiler_params=PARAMS,
            cost_estimate=pl.CostEstimate(
                flops=64 * tile**3 * sectors**2, bytes_accessed=2**20, transcendentals=0
            ),
            name=name,
        )(*scalars, *operands)

    sizes = (left_sizes, right_sizes)
    rights = [right_own, right_other]
    total = jax.ShapeDtypeStruct(out_shape, jnp.float32)
    near, far_mask = apply(
        near_kernel, "near", [total, block(out_shape)], sizes + (term_blocks,),
        [psi, left_ops, side, direct_a, direct_b] + rights,
    )
    sent, far = apply(
        far_kernel, "far", [block(out_shape), total], (),
        [direct_a, direct_b, passed_a, passed_b] + rights + [near, far_mask, psi_far],
    )
    arrived = over_op(sent, 2)
    kept = jnp.where(lax.axis_index("blk") // 2 == lax.axis_index("op") // 2, near, far)
    return (kept + arrived.astype(jnp.float32)).astype(jnp.bfloat16)


def wide_shards(psi, left_ops, right_ops, term_blocks, left_sizes, right_sizes):
    sectors_here = psi.shape[0]
    tile_size = psi.shape[2]
    left_first = lax.axis_index("blk") * sectors_here
    positions = lax.broadcasted_iota(jnp.int32, (tile_size,), 0)
    left_local = lax.dynamic_slice_in_dim(left_sizes, left_first, sectors_here)
    left_keep = positions[None, :] < left_local[:, None]
    right_keep = positions[None, :] < right_sizes[:, None]
    keep_mask = (left_keep[:, None, :, None] & right_keep[None, :, None, :]).astype(jnp.bfloat16)
    masked = psi * keep_mask
    acting_count = left_ops.shape[0] // 2
    order = jnp.argsort(1 - term_blocks, axis=0, stable=True)[:acting_count]
    ids_local = lax.dynamic_slice_in_dim(order, left_first, sectors_here, 1)
    sector_index = lax.broadcasted_iota(jnp.int32, (acting_count, sectors_here), 1)
    picked = left_ops[ids_local, sector_index]
    applied = jnp.einsum(
        "kaim,abmj->kabij", picked, masked, preferred_element_type=jnp.float32
    ).astype(jnp.bfloat16)
    arrived = lax.all_to_all(applied, "blk", split_axis=2, concat_axis=1, tiled=True)
    right_picked = right_ops[order]
    partial_value = jnp.einsum(
        "kabij,kablj->bail", arrived, right_picked, preferred_element_type=jnp.float32
    )
    summed = lax.psum_scatter(
        partial_value.astype(jnp.bfloat16), "op", scatter_dimension=1, tiled=True
    ).astype(jnp.float32)
    row_count = summed.shape[1]
    op_first = lax.axis_index("op") * row_count
    left_share = lax.dynamic_slice_in_dim(left_sizes, op_first, row_count)
    right_local = lax.dynamic_slice_in_dim(right_sizes, left_first, sectors_here)
    rows_keep = positions[None, :] < left_share[:, None]
    cols_keep = positions[None, :] < right_local[:, None]
    out_keep = (cols_keep[:, None, None, :] & rows_keep[None, :, :, None]).astype(jnp.float32)
    return (summed * out_keep).astype(jnp.bfloat16)


def solution(mesh):
    in_specs = (
        P(("parts", "blk"), None, None, None),
        P(("parts", "op"), "blk", None, None),
        P(("parts", "op"), "blk", None, None),
        P(("parts", "op"), None),
        P("parts"),
        P("parts"),
    )
    out_specs = P(("parts", "blk"), "op", None, None)
    nz, no = mesh.shape["blk"], mesh.shape["op"]
    body = shards if nz == no == 4 else wide_shards
    return jax.shard_map(body, mesh=mesh, in_specs=in_specs, out_specs=out_specs, check_vma=False)
```

```python
import functools

import jax
import jax.numpy as jnp
from jax import lax
from jax.experimental import pallas as pl
from jax.experimental.pallas import tpu as pltpu
from jax.sharding import PartitionSpec as P

ANY = pl.BlockSpec(memory_space=pl.ANY)
SMEM = pl.BlockSpec(memory_space=pltpu.SMEM)
VMEM = pl.BlockSpec(memory_space=pltpu.VMEM)
PARAMS = pltpu.CompilerParams(vmem_limit_bytes=32 * 1024 * 1024)
ID_ROWS = 16
FAR_PAD = 32


def acting_terms(blocks_ref, sector):
    first = jnp.int32(0)
    second = jnp.int32(0)
    for term in reversed(range(blocks_ref.shape[0])):
        acts = blocks_ref[term, sector] > 0
        second = jnp.where(acts, first, second)
        first = jnp.where(acts, term, first)
    return first, second


def place():
    op = lax.axis_index("op")
    return lax.axis_index("blk"), lax.shift_right_logical(op, 1), jnp.bitwise_and(op, 1)


def is_home():
    z, _, c = place()
    return c == jnp.bitwise_and(z, 1)


def pack_kernel(blocks_hbm, psi_ref, left_ref, right_ref, *rest):
    left_out, side_out, far_out, right_out, blocks_ref, left_all, sem = rest
    z, _, _ = place()
    sectors, tile = psi_ref.shape[0], psi_ref.shape[-1]
    count = 2 * sectors
    near = jnp.bitwise_xor(z, 1) * sectors
    far = jnp.bitwise_xor(z, jnp.where(is_home(), 2, 3)) * sectors

    def psi_copies(column, out, first):
        return [
            pltpu.make_async_copy(
                psi_ref.at[a, column + b],
                out.at[pl.ds((sectors * a + b) * tile, tile)],
                sem.at[first + sectors * a + b],
            )
            for a in range(sectors)
            for b in range(sectors)
        ]

    table = pltpu.make_async_copy(blocks_hbm, blocks_ref, sem.at[0])
    lefts = pltpu.make_async_copy(left_ref, left_all, sem.at[1])
    others = [pltpu.make_async_copy(right_ref, right_out, sem.at[2])]
    others += psi_copies(far, far_out, 3)
    sides = psi_copies(near, side_out, 3 + sectors * sectors)
    for copy in [table, lefts] + others:
        copy.start()

    @pl.when(is_home())
    def _():
        for copy in sides:
            copy.start()

    far_out[pl.ds(count * tile, FAR_PAD)] = jnp.zeros((FAR_PAD, tile), jnp.bfloat16)
    table.wait()
    row = lax.broadcasted_iota(jnp.int32, (ID_ROWS, tile), 0)
    ids = jnp.zeros((ID_ROWS, tile), jnp.float32)
    picked = []
    for local in range(sectors):
        for term in acting_terms(blocks_ref, z * sectors + local):
            ids = jnp.where(row == len(picked), term.astype(jnp.float32), ids)
            picked.append((term, local))
    for out in (left_out, side_out):
        out[pl.ds(count * tile, ID_ROWS)] = ids.astype(jnp.bfloat16)
    lefts.wait()
    for spot, (term, local) in enumerate(picked):
        left_out[pl.ds(spot * tile, tile)] = left_all[term, local]

    @pl.when(is_home())
    def _():
        for copy in sides:
            copy.wait()

    @pl.when(jnp.logical_not(is_home()))
    def _():
        for spot, (term, local) in enumerate(picked):
            side_out[pl.ds(spot * tile, tile)] = left_all[term, local]

    for copy in others:
        copy.wait()


def keep_mask(z, distance, sizes, a, b, sectors, tile):
    lsize_ref, rsize_ref = sizes
    rows = lax.broadcasted_iota(jnp.int32, (tile, tile), 0)
    lanes = lax.broadcasted_iota(jnp.int32, (tile, tile), 1)
    height = lsize_ref[jnp.bitwise_xor(z, distance) * sectors + a]
    return (rows < height) & (lanes < rsize_ref[z * sectors + b])


def wide_psi(keep, a, blocks):
    cut = []
    for b, block in enumerate(blocks):
        cut.append(jnp.where(keep(a, b), block.astype(jnp.float32), 0.0).astype(jnp.bfloat16))
    return jnp.concatenate(cut, axis=1)


def partial_sums(sectors, keep, psi, lefts, rights, store):
    for a in range(sectors):
        wide = wide_psi(keep, a, psi(a))
        tile = wide.shape[0]
        applied = []
        for left in lefts:
            both = jnp.dot(left(a), wide, preferred_element_type=jnp.float32).astype(jnp.bfloat16)
            applied += [both[:tile], both[tile:]]
        for b in range(sectors):
            picked = [right(a, slot, b) for right in rights for slot in range(2)]
            column = [part[:, b * tile : (b + 1) * tile] for part in applied]
            total = lax.dot_general(
                jnp.concatenate(column, axis=1),
                jnp.concatenate(picked, axis=1),
                (((1,), (1,)), ((), ())),
                preferred_element_type=jnp.float32,
            )
            store(b, a, jnp.where(keep(a, b), total, 0.0))


def message(ref, right_ref):
    terms, sectors, tile = right_ref.shape[0], right_ref.shape[1], right_ref.shape[-1]
    ids = ref[pl.ds(2 * sectors * tile, ID_ROWS)].astype(jnp.float32)

    def left(a):
        return ref[pl.ds(2 * a * tile, 2 * tile)]

    def right(a, slot, b):
        spot = 2 * a + slot
        term = jnp.broadcast_to(ids[spot : spot + 1], (tile, tile))
        block = right_ref[0, b].astype(jnp.float32)
        for t in range(1, terms):
            block = jnp.where(term == t, right_ref[t, b].astype(jnp.float32), block)
        return block.astype(jnp.bfloat16)

    return left, right


def near_kernel(lsize_ref, rsize_ref, blocks_ref, *rest):
    psi_ref, left_ref, side, direct_a, direct_b, right_own, right_other = rest[:7]
    out_ref, mask_ref = rest[7:]
    z, _, _ = place()
    sectors, tile = out_ref.shape[0], out_ref.shape[-1]
    columns = range(sectors)

    def masks(distance):
        return lambda a, b: keep_mask(z, distance, (lsize_ref, rsize_ref), a, b, sectors, tile)

    far = masks(jnp.where(is_home(), 2, 3))
    for a in columns:
        for b in columns:
            mask_ref[a, b] = jnp.where(far(a, b), 1.0, 0.0).astype(mask_ref.dtype)

    def store(b, a, total):
        out_ref[b, a] = total

    @pl.when(is_home())
    def _():
        terms = [acting_terms(blocks_ref, z * sectors + a) for a in columns]
        left, right = message(side, right_other)
        partial_sums(
            sectors, masks(0),
            lambda a: [psi_ref[a, z * sectors + b] for b in columns],
            [lambda a: jnp.concatenate([left_ref[term, a] for term in terms[a]], axis=0), left],
            [lambda a, slot, b: right_own[terms[a][slot], b], right],
            store,
        )

    @pl.when(jnp.logical_not(is_home()))
    def _():
        lefts, rights = zip(message(direct_b, right_own), message(direct_a, right_other))

        def psi(a):
            return [side[pl.ds((sectors * a + b) * tile, tile)] for b in columns]

        partial_sums(sectors, masks(1), psi, lefts, rights, store)


def far_kernel(*refs):
    direct_a, direct_b, passed_a, passed_b, right_own, right_other = refs[:6]
    near_ref, mask_ref, psi_ref, sent_ref, out_ref = refs[6:]
    z, x, _ = place()
    sectors, tile = out_ref.shape[0], out_ref.shape[-1]
    far_leaves = lax.shift_right_logical(z, 1) == x

    def store_sent(b, a, total):
        sent_ref[b, a] = total.astype(sent_ref.dtype)

    def store_kept(b, a, total):
        out_ref[b, a] = total
        sent_ref[b, a] = near_ref[b, a].astype(sent_ref.dtype)

    def keep(a, b):
        return mask_ref[a, b].astype(jnp.float32) > 0

    def psi(a):
        return [psi_ref[pl.ds((sectors * a + b) * tile, tile)] for b in range(sectors)]

    for leaves, store in ((True, store_sent), (False, store_kept)):
        for at_home, first, second in (
            (True, direct_a, direct_b),
            (False, passed_a, passed_b),
        ):

            @pl.when((is_home() == at_home) & (far_leaves == leaves))
            def _(store=store, first=first, second=second):
                lefts, rights = zip(message(first, right_own), message(second, right_other))
                partial_sums(sectors, keep, psi, lefts, rights, store)


def shards(psi, left_ops, right_ops, term_blocks, left_sizes, right_sizes):
    n = 4
    sectors, tile = psi.shape[0], psi.shape[-1]
    block = functools.partial(jax.ShapeDtypeStruct, dtype=jnp.bfloat16)
    out_shape = (sectors, sectors, tile, tile)
    message_shape = (2 * sectors * tile + ID_ROWS, tile)

    def over_op(array, step):
        return lax.ppermute(array, "op", [(o, o ^ step) for o in range(n)])

    def over_z(array, home_step, other_step):
        pairs = []
        for z in range(n):
            for o in range(n):
                step = home_step if o & 1 == z & 1 else other_step
                pairs.append((z * n + o, (z ^ step) * n + (o & 2) + (z & 1)))
        return lax.ppermute(array, ("blk", "op"), pairs)

    psi_hbm, left_hbm, right_hbm, blocks_hbm = [
        pltpu.with_memory_space_constraint(array, pltpu.HBM)
        for array in (psi, left_ops, right_ops, term_blocks)
    ]
    left_sent, side_sent, far_sent, right_own = pl.pallas_call(
        pack_kernel,
        out_shape=[
            block(message_shape),
            block(message_shape),
            block((sectors * sectors * tile + FAR_PAD, tile)),
            block(right_ops.shape),
        ],
        in_specs=[ANY] * 4,
        out_specs=[VMEM] * 4,
        scratch_shapes=[
            pltpu.SMEM(term_blocks.shape, jnp.int32),
            pltpu.VMEM(left_ops.shape, jnp.bfloat16),
            pltpu.SemaphoreType.DMA((3 + 2 * sectors**2,)),
        ],
        compiler_params=PARAMS,
        name="pack",
    )(blocks_hbm, psi_hbm, left_hbm, right_hbm)
    direct_a = over_z(left_sent, 2, 1)
    direct_b = over_z(left_sent, 1, 2)
    psi_far = over_z(far_sent, 2, 3)
    side = over_z(side_sent, 1, 0)
    passed_a = over_z(direct_a, 1, 0)
    passed_b = over_z(direct_b, 1, 0)
    right_other = over_op(right_own, 1)

    def apply(kernel, name, outs, scalars, operands, cost):
        return pl.pallas_call(
            kernel,
            out_shape=outs,
            in_specs=[SMEM] * len(scalars) + [VMEM] * len(operands),
            out_specs=[VMEM] * len(outs),
            compiler_params=PARAMS,
            cost_estimate=pl.CostEstimate(
                flops=64 * cost**3, bytes_accessed=16 * cost**2, transcendentals=0
            ),
            name=name,
        )(*scalars, *operands)

    sizes = (left_sizes, right_sizes)
    rights = [right_own, right_other]
    total = jax.ShapeDtypeStruct(out_shape, jnp.float32)
    near, far_mask = apply(
        near_kernel, "near", [total, block(out_shape)], sizes + (term_blocks,),
        [psi, left_ops, side, direct_a, direct_b] + rights, 1,
    )
    sent, far = apply(
        far_kernel, "far", [block(out_shape), total], (),
        [direct_a, direct_b, passed_a, passed_b] + rights + [near, far_mask, psi_far], 2 * tile,
    )
    arrived = over_op(sent, 2)
    kept = jnp.where(lax.axis_index("blk") // 2 == lax.axis_index("op") // 2, near, far)
    return (kept + arrived.astype(jnp.float32)).astype(jnp.bfloat16)


def wide_shards(psi, left_ops, right_ops, term_blocks, left_sizes, right_sizes):
    sectors_here = psi.shape[0]
    tile_size = psi.shape[2]
    left_first = lax.axis_index("blk") * sectors_here
    positions = lax.broadcasted_iota(jnp.int32, (tile_size,), 0)
    left_local = lax.dynamic_slice_in_dim(left_sizes, left_first, sectors_here)
    left_keep = positions[None, :] < left_local[:, None]
    right_keep = positions[None, :] < right_sizes[:, None]
    keep_mask = (left_keep[:, None, :, None] & right_keep[None, :, None, :]).astype(jnp.bfloat16)
    masked = psi * keep_mask
    acting_count = left_ops.shape[0] // 2
    order = jnp.argsort(1 - term_blocks, axis=0, stable=True)[:acting_count]
    ids_local = lax.dynamic_slice_in_dim(order, left_first, sectors_here, 1)
    sector_index = lax.broadcasted_iota(jnp.int32, (acting_count, sectors_here), 1)
    picked = left_ops[ids_local, sector_index]
    applied = jnp.einsum(
        "kaim,abmj->kabij", picked, masked, preferred_element_type=jnp.float32
    ).astype(jnp.bfloat16)
    arrived = lax.all_to_all(applied, "blk", split_axis=2, concat_axis=1, tiled=True)
    right_picked = right_ops[order]
    partial_value = jnp.einsum(
        "kabij,kablj->bail", arrived, right_picked, preferred_element_type=jnp.float32
    )
    summed = lax.psum_scatter(
        partial_value.astype(jnp.bfloat16), "op", scatter_dimension=1, tiled=True
    ).astype(jnp.float32)
    row_count = summed.shape[1]
    op_first = lax.axis_index("op") * row_count
    left_share = lax.dynamic_slice_in_dim(left_sizes, op_first, row_count)
    right_local = lax.dynamic_slice_in_dim(right_sizes, left_first, sectors_here)
    rows_keep = positions[None, :] < left_share[:, None]
    cols_keep = positions[None, :] < right_local[:, None]
    out_keep = (cols_keep[:, None, None, :] & rows_keep[None, :, :, None]).astype(jnp.float32)
    return (summed * out_keep).astype(jnp.bfloat16)


def solution(mesh):
    in_specs = (
        P(("parts", "blk"), None, None, None),
        P(("parts", "op"), "blk", None, None),
        P(("parts", "op"), "blk", None, None),
        P(("parts", "op"), None),
        P("parts"),
        P("parts"),
    )
    out_specs = P(("parts", "blk"), "op", None, None)
    nz, no = mesh.shape["blk"], mesh.shape["op"]
    body = shards if nz == no == 4 else wide_shards
    return jax.shard_map(body, mesh=mesh, in_specs=in_specs, out_specs=out_specs, check_vma=False)
```

```python
import functools

import jax
import jax.numpy as jnp
from jax import lax
from jax.experimental import pallas as pl
from jax.experimental.pallas import tpu as pltpu
from jax.sharding import PartitionSpec as P

ANY = pl.BlockSpec(memory_space=pl.ANY)
SMEM = pl.BlockSpec(memory_space=pltpu.SMEM)
VMEM = pl.BlockSpec(memory_space=pltpu.VMEM)
PARAMS = pltpu.CompilerParams(vmem_limit_bytes=32 * 1024 * 1024)
ID_ROWS = 16
FAR_PAD = 32


def acting_terms(blocks_ref, sector):
    first = jnp.int32(0)
    second = jnp.int32(0)
    for term in reversed(range(blocks_ref.shape[0])):
        acts = blocks_ref[term, sector] > 0
        second = jnp.where(acts, first, second)
        first = jnp.where(acts, term, first)
    return first, second


def place():
    op = lax.axis_index("op")
    return lax.axis_index("blk"), lax.shift_right_logical(op, 1), jnp.bitwise_and(op, 1)


def is_home():
    z, _, c = place()
    return c == jnp.bitwise_and(z, 1)


def pack_kernel(blocks_hbm, psi_ref, left_ref, right_ref, *rest):
    left_out, side_out, far_out, right_out, blocks_ref, left_all, sem = rest
    z, _, _ = place()
    sectors, tile = psi_ref.shape[0], psi_ref.shape[-1]
    count = 2 * sectors
    near = jnp.bitwise_xor(z, 1) * sectors
    far = jnp.bitwise_xor(z, jnp.where(is_home(), 2, 3)) * sectors

    def psi_copies(column, out, first):
        return [
            pltpu.make_async_copy(
                psi_ref.at[a, column + b],
                out.at[pl.ds((sectors * a + b) * tile, tile)],
                sem.at[first + sectors * a + b],
            )
            for a in range(sectors)
            for b in range(sectors)
        ]

    table = pltpu.make_async_copy(blocks_hbm, blocks_ref, sem.at[0])
    lefts = pltpu.make_async_copy(left_ref, left_all, sem.at[1])
    others = [pltpu.make_async_copy(right_ref, right_out, sem.at[2])]
    others += psi_copies(far, far_out, 3)
    sides = psi_copies(near, side_out, 3 + sectors * sectors)
    for copy in [table, lefts] + others:
        copy.start()

    @pl.when(is_home())
    def _():
        for copy in sides:
            copy.start()

    far_out[pl.ds(count * tile, FAR_PAD)] = jnp.zeros((FAR_PAD, tile), jnp.bfloat16)
    table.wait()
    row = lax.broadcasted_iota(jnp.int32, (ID_ROWS, tile), 0)
    ids = jnp.zeros((ID_ROWS, tile), jnp.float32)
    picked = []
    for local in range(sectors):
        for term in acting_terms(blocks_ref, z * sectors + local):
            ids = jnp.where(row == len(picked), term.astype(jnp.float32), ids)
            picked.append((term, local))
    for out in (left_out, side_out):
        out[pl.ds(count * tile, ID_ROWS)] = ids.astype(jnp.bfloat16)
    lefts.wait()
    for spot, (term, local) in enumerate(picked):
        left_out[pl.ds(spot * tile, tile)] = left_all[term, local]

    @pl.when(is_home())
    def _():
        for copy in sides:
            copy.wait()

    @pl.when(jnp.logical_not(is_home()))
    def _():
        for spot, (term, local) in enumerate(picked):
            side_out[pl.ds(spot * tile, tile)] = left_all[term, local]

    for copy in others:
        copy.wait()


def keep_mask(z, distance, sizes, a, b, sectors, tile):
    lsize_ref, rsize_ref = sizes
    rows = lax.broadcasted_iota(jnp.int32, (tile, tile), 0)
    lanes = lax.broadcasted_iota(jnp.int32, (tile, tile), 1)
    height = lsize_ref[jnp.bitwise_xor(z, distance) * sectors + a]
    return (rows < height) & (lanes < rsize_ref[z * sectors + b])


def wide_psi(keep, a, blocks):
    cut = []
    for b, block in enumerate(blocks):
        cut.append(jnp.where(keep(a, b), block.astype(jnp.float32), 0.0).astype(jnp.bfloat16))
    return jnp.concatenate(cut, axis=1)


def partial_sums(sectors, keep, psi, lefts, rights, store):
    for a in range(sectors):
        wide = wide_psi(keep, a, psi(a))
        tile = wide.shape[0]
        applied = []
        for left in lefts:
            both = jnp.dot(left(a), wide, preferred_element_type=jnp.float32).astype(jnp.bfloat16)
            applied += [both[:tile], both[tile:]]
        for b in range(sectors):
            picked = [right(a, slot, b) for right in rights for slot in range(2)]
            column = [part[:, b * tile : (b + 1) * tile] for part in applied]
            total = lax.dot_general(
                jnp.concatenate(column, axis=1),
                jnp.concatenate(picked, axis=1),
                (((1,), (1,)), ((), ())),
                preferred_element_type=jnp.float32,
            )
            store(b, a, jnp.where(keep(a, b), total, 0.0))


def message(ref, right_ref):
    terms, sectors, tile = right_ref.shape[0], right_ref.shape[1], right_ref.shape[-1]
    ids = ref[pl.ds(2 * sectors * tile, ID_ROWS)].astype(jnp.float32)

    def left(a):
        return ref[pl.ds(2 * a * tile, 2 * tile)]

    def right(a, slot, b):
        spot = 2 * a + slot
        term = jnp.broadcast_to(ids[spot : spot + 1], (tile, tile))
        block = right_ref[0, b].astype(jnp.float32)
        for t in range(1, terms):
            block = jnp.where(term == t, right_ref[t, b].astype(jnp.float32), block)
        return block.astype(jnp.bfloat16)

    return left, right


def near_kernel(lsize_ref, rsize_ref, blocks_ref, *rest):
    psi_ref, left_ref, side, direct_a, direct_b, right_own, right_other = rest[:7]
    out_ref, mask_ref = rest[7:]
    z, _, _ = place()
    sectors, tile = out_ref.shape[0], out_ref.shape[-1]
    columns = range(sectors)

    def masks(distance):
        return lambda a, b: keep_mask(z, distance, (lsize_ref, rsize_ref), a, b, sectors, tile)

    far = masks(jnp.where(is_home(), 2, 3))
    for a in columns:
        for b in columns:
            mask_ref[a, b] = jnp.where(far(a, b), 1.0, 0.0).astype(mask_ref.dtype)

    def store(b, a, total):
        out_ref[b, a] = total

    @pl.when(is_home())
    def _():
        terms = [acting_terms(blocks_ref, z * sectors + a) for a in columns]
        left, right = message(side, right_other)
        partial_sums(
            sectors, masks(0),
            lambda a: [psi_ref[a, z * sectors + b] for b in columns],
            [lambda a: jnp.concatenate([left_ref[term, a] for term in terms[a]], axis=0), left],
            [lambda a, slot, b: right_own[terms[a][slot], b], right],
            store,
        )

    @pl.when(jnp.logical_not(is_home()))
    def _():
        lefts, rights = zip(message(direct_b, right_own), message(direct_a, right_other))

        def psi(a):
            return [side[pl.ds((sectors * a + b) * tile, tile)] for b in columns]

        partial_sums(sectors, masks(1), psi, lefts, rights, store)


def far_kernel(*refs):
    direct_a, direct_b, passed_a, passed_b, right_own, right_other = refs[:6]
    near_ref, mask_ref, psi_ref, sent_ref, out_ref = refs[6:]
    z, x, _ = place()
    sectors, tile = out_ref.shape[0], out_ref.shape[-1]
    far_leaves = lax.shift_right_logical(z, 1) == x

    def store_sent(b, a, total):
        sent_ref[b, a] = total.astype(sent_ref.dtype)

    def store_kept(b, a, total):
        out_ref[b, a] = total
        sent_ref[b, a] = near_ref[b, a].astype(sent_ref.dtype)

    def keep(a, b):
        return mask_ref[a, b].astype(jnp.float32) > 0

    def psi(a):
        return [psi_ref[pl.ds((sectors * a + b) * tile, tile)] for b in range(sectors)]

    for leaves, store in ((True, store_sent), (False, store_kept)):
        for at_home, first, second in (
            (True, direct_a, direct_b),
            (False, passed_a, passed_b),
        ):

            @pl.when((is_home() == at_home) & (far_leaves == leaves))
            def _(store=store, first=first, second=second):
                lefts, rights = zip(message(first, right_own), message(second, right_other))
                partial_sums(sectors, keep, psi, lefts, rights, store)


def shards(psi, left_ops, right_ops, term_blocks, left_sizes, right_sizes):
    n = 4
    sectors, tile = psi.shape[0], psi.shape[-1]
    block = functools.partial(jax.ShapeDtypeStruct, dtype=jnp.bfloat16)
    out_shape = (sectors, sectors, tile, tile)
    message_shape = (2 * sectors * tile + ID_ROWS, tile)

    def over_op(array, step):
        return lax.ppermute(array, "op", [(o, o ^ step) for o in range(n)])

    def over_z(array, home_step, other_step):
        pairs = []
        for z in range(n):
            for o in range(n):
                step = home_step if o & 1 == z & 1 else other_step
                pairs.append((z * n + o, (z ^ step) * n + (o & 2) + (z & 1)))
        return lax.ppermute(array, ("blk", "op"), pairs)

    psi_hbm, left_hbm, right_hbm, blocks_hbm = [
        pltpu.with_memory_space_constraint(array, pltpu.HBM)
        for array in (psi, left_ops, right_ops, term_blocks)
    ]
    left_sent, side_sent, far_sent, right_own = pl.pallas_call(
        pack_kernel,
        out_shape=[
            block(message_shape),
            block(message_shape),
            block((sectors * sectors * tile + FAR_PAD, tile)),
            block(right_ops.shape),
        ],
        in_specs=[ANY] * 4,
        out_specs=[VMEM] * 4,
        scratch_shapes=[
            pltpu.SMEM(term_blocks.shape, jnp.int32),
            pltpu.VMEM(left_ops.shape, jnp.bfloat16),
            pltpu.SemaphoreType.DMA((3 + 2 * sectors**2,)),
        ],
        compiler_params=PARAMS,
        name="pack",
    )(blocks_hbm, psi_hbm, left_hbm, right_hbm)
    direct_a = over_z(left_sent, 2, 1)
    direct_b = over_z(left_sent, 1, 2)
    psi_far = over_z(far_sent, 2, 3)
    side = over_z(side_sent, 1, 0)
    passed_a = over_z(direct_a, 1, 0)
    passed_b = over_z(direct_b, 1, 0)
    right_other = over_op(right_own, 1)

    def apply(kernel, name, outs, scalars, operands, cost):
        return pl.pallas_call(
            kernel,
            out_shape=outs,
            in_specs=[SMEM] * len(scalars) + [VMEM] * len(operands),
            out_specs=[VMEM] * len(outs),
            compiler_params=PARAMS,
            cost_estimate=pl.CostEstimate(
                flops=64 * cost**3, bytes_accessed=16 * cost**2, transcendentals=0
            ),
            name=name,
        )(*scalars, *operands)

    sizes = (left_sizes, right_sizes)
    rights = [right_own, right_other]
    total = jax.ShapeDtypeStruct(out_shape, jnp.float32)
    near, far_mask = apply(
        near_kernel, "near", [total, block(out_shape)], sizes + (term_blocks,),
        [psi, left_ops, side, direct_a, direct_b] + rights, 1,
    )
    sent, far = apply(
        far_kernel, "far", [block(out_shape), total], (),
        [direct_a, direct_b, passed_a, passed_b] + rights + [near, far_mask, psi_far], 2 * tile,
    )
    arrived = over_op(sent, 2)
    kept = jnp.where(lax.axis_index("blk") // 2 == lax.axis_index("op") // 2, near, far)
    kept = lax.optimization_barrier(kept)
    return (kept + arrived.astype(jnp.float32)).astype(jnp.bfloat16)


def wide_shards(psi, left_ops, right_ops, term_blocks, left_sizes, right_sizes):
    sectors_here = psi.shape[0]
    tile_size = psi.shape[2]
    left_first = lax.axis_index("blk") * sectors_here
    positions = lax.broadcasted_iota(jnp.int32, (tile_size,), 0)
    left_local = lax.dynamic_slice_in_dim(left_sizes, left_first, sectors_here)
    left_keep = positions[None, :] < left_local[:, None]
    right_keep = positions[None, :] < right_sizes[:, None]
    keep_mask = (left_keep[:, None, :, None] & right_keep[None, :, None, :]).astype(jnp.bfloat16)
    masked = psi * keep_mask
    acting_count = left_ops.shape[0] // 2
    order = jnp.argsort(1 - term_blocks, axis=0, stable=True)[:acting_count]
    ids_local = lax.dynamic_slice_in_dim(order, left_first, sectors_here, 1)
    sector_index = lax.broadcasted_iota(jnp.int32, (acting_count, sectors_here), 1)
    picked = left_ops[ids_local, sector_index]
    applied = jnp.einsum(
        "kaim,abmj->kabij", picked, masked, preferred_element_type=jnp.float32
    ).astype(jnp.bfloat16)
    arrived = lax.all_to_all(applied, "blk", split_axis=2, concat_axis=1, tiled=True)
    right_picked = right_ops[order]
    partial_value = jnp.einsum(
        "kabij,kablj->bail", arrived, right_picked, preferred_element_type=jnp.float32
    )
    summed = lax.psum_scatter(
        partial_value.astype(jnp.bfloat16), "op", scatter_dimension=1, tiled=True
    ).astype(jnp.float32)
    row_count = summed.shape[1]
    op_first = lax.axis_index("op") * row_count
    left_share = lax.dynamic_slice_in_dim(left_sizes, op_first, row_count)
    right_local = lax.dynamic_slice_in_dim(right_sizes, left_first, sectors_here)
    rows_keep = positions[None, :] < left_share[:, None]
    cols_keep = positions[None, :] < right_local[:, None]
    out_keep = (cols_keep[:, None, None, :] & rows_keep[None, :, :, None]).astype(jnp.float32)
    return (summed * out_keep).astype(jnp.bfloat16)


def solution(mesh):
    in_specs = (
        P(("parts", "blk"), None, None, None),
        P(("parts", "op"), "blk", None, None),
        P(("parts", "op"), "blk", None, None),
        P(("parts", "op"), None),
        P("parts"),
        P("parts"),
    )
    out_specs = P(("parts", "blk"), "op", None, None)
    nz, no = mesh.shape["blk"], mesh.shape["op"]
    body = shards if nz == no == 4 else wide_shards
    return jax.shard_map(body, mesh=mesh, in_specs=in_specs, out_specs=out_specs, check_vma=False)
```

```python
import functools

import jax
import jax.numpy as jnp
from jax import lax
from jax.experimental import pallas as pl
from jax.experimental.pallas import tpu as pltpu
from jax.sharding import PartitionSpec as P

ANY = pl.BlockSpec(memory_space=pl.ANY)
SMEM = pl.BlockSpec(memory_space=pltpu.SMEM)
VMEM = pl.BlockSpec(memory_space=pltpu.VMEM)
PARAMS = pltpu.CompilerParams(vmem_limit_bytes=32 * 1024 * 1024)
ID_ROWS = 16
FAR_PAD = 32


def acting_terms(blocks_ref, sector):
    first = jnp.int32(0)
    second = jnp.int32(0)
    for term in reversed(range(blocks_ref.shape[0])):
        acts = blocks_ref[term, sector] > 0
        second = jnp.where(acts, first, second)
        first = jnp.where(acts, term, first)
    return first, second


def place():
    op = lax.axis_index("op")
    return lax.axis_index("blk"), lax.shift_right_logical(op, 1), jnp.bitwise_and(op, 1)


def is_home():
    z, _, c = place()
    return c == jnp.bitwise_and(z, 1)


def pack_kernel(blocks_hbm, psi_ref, left_ref, right_ref, *rest):
    left_out, side_out, far_out, right_out, blocks_ref, left_all, sem = rest
    z, _, _ = place()
    sectors, tile = psi_ref.shape[0], psi_ref.shape[-1]
    count = 2 * sectors
    near = jnp.bitwise_xor(z, 1) * sectors
    far = jnp.bitwise_xor(z, jnp.where(is_home(), 2, 3)) * sectors

    def psi_copies(column, out, first):
        return [
            pltpu.make_async_copy(
                psi_ref.at[a, column + b],
                out.at[pl.ds((sectors * a + b) * tile, tile)],
                sem.at[first + sectors * a + b],
            )
            for a in range(sectors)
            for b in range(sectors)
        ]

    table = pltpu.make_async_copy(blocks_hbm, blocks_ref, sem.at[0])
    lefts = pltpu.make_async_copy(left_ref, left_all, sem.at[1])
    others = [pltpu.make_async_copy(right_ref, right_out, sem.at[2])]
    others += psi_copies(far, far_out, 3)
    sides = psi_copies(near, side_out, 3 + sectors * sectors)
    for copy in [table, lefts] + others:
        copy.start()

    @pl.when(is_home())
    def _():
        for copy in sides:
            copy.start()

    far_out[pl.ds(count * tile, FAR_PAD)] = jnp.zeros((FAR_PAD, tile), jnp.bfloat16)
    table.wait()
    row = lax.broadcasted_iota(jnp.int32, (ID_ROWS, tile), 0)
    ids = jnp.zeros((ID_ROWS, tile), jnp.float32)
    picked = []
    for local in range(sectors):
        for term in acting_terms(blocks_ref, z * sectors + local):
            ids = jnp.where(row == len(picked), term.astype(jnp.float32), ids)
            picked.append((term, local))
    for out in (left_out, side_out):
        out[pl.ds(count * tile, ID_ROWS)] = ids.astype(jnp.bfloat16)
    lefts.wait()
    for spot, (term, local) in enumerate(picked):
        left_out[pl.ds(spot * tile, tile)] = left_all[term, local]

    @pl.when(is_home())
    def _():
        for copy in sides:
            copy.wait()

    @pl.when(jnp.logical_not(is_home()))
    def _():
        for spot, (term, local) in enumerate(picked):
            side_out[pl.ds(spot * tile, tile)] = left_all[term, local]

    for copy in others:
        copy.wait()


def keep_mask(z, distance, sizes, a, b, sectors, tile):
    lsize_ref, rsize_ref = sizes
    rows = lax.broadcasted_iota(jnp.int32, (tile, tile), 0)
    lanes = lax.broadcasted_iota(jnp.int32, (tile, tile), 1)
    height = lsize_ref[jnp.bitwise_xor(z, distance) * sectors + a]
    return (rows < height) & (lanes < rsize_ref[z * sectors + b])


def wide_psi(keep, a, blocks):
    cut = []
    for b, block in enumerate(blocks):
        cut.append(jnp.where(keep(a, b), block.astype(jnp.float32), 0.0).astype(jnp.bfloat16))
    return jnp.concatenate(cut, axis=1)


def partial_sums(sectors, keep, psi, lefts, rights, store):
    for a in range(sectors):
        wide = wide_psi(keep, a, psi(a))
        tile = wide.shape[0]
        applied = []
        for left in lefts:
            both = jnp.dot(left(a), wide, preferred_element_type=jnp.float32).astype(jnp.bfloat16)
            applied += [both[:tile], both[tile:]]
        for b in range(sectors):
            picked = [right(a, slot, b) for right in rights for slot in range(2)]
            column = [part[:, b * tile : (b + 1) * tile] for part in applied]
            total = lax.dot_general(
                jnp.concatenate(column, axis=1),
                jnp.concatenate(picked, axis=1),
                (((1,), (1,)), ((), ())),
                preferred_element_type=jnp.float32,
            )
            store(b, a, jnp.where(keep(a, b), total, 0.0))


def message(ref, right_ref):
    terms, sectors, tile = right_ref.shape[0], right_ref.shape[1], right_ref.shape[-1]
    ids = ref[pl.ds(2 * sectors * tile, ID_ROWS)].astype(jnp.float32)

    def left(a):
        return ref[pl.ds(2 * a * tile, 2 * tile)]

    def right(a, slot, b):
        spot = 2 * a + slot
        term = jnp.broadcast_to(ids[spot : spot + 1], (tile, tile))
        block = right_ref[0, b].astype(jnp.float32)
        for t in range(1, terms):
            block = jnp.where(term == t, right_ref[t, b].astype(jnp.float32), block)
        return block.astype(jnp.bfloat16)

    return left, right


def near_kernel(lsize_ref, rsize_ref, blocks_ref, *rest):
    psi_ref, left_ref, side, direct_a, direct_b, right_own, right_other = rest[:7]
    out_ref, mask_ref = rest[7:]
    z, _, _ = place()
    sectors, tile = out_ref.shape[0], out_ref.shape[-1]
    columns = range(sectors)

    def masks(distance):
        return lambda a, b: keep_mask(z, distance, (lsize_ref, rsize_ref), a, b, sectors, tile)

    far = masks(jnp.where(is_home(), 2, 3))
    for a in columns:
        for b in columns:
            mask_ref[a, b] = jnp.where(far(a, b), 1.0, 0.0).astype(mask_ref.dtype)

    def store(b, a, total):
        out_ref[b, a] = total

    @pl.when(is_home())
    def _():
        terms = [acting_terms(blocks_ref, z * sectors + a) for a in columns]
        left, right = message(side, right_other)
        partial_sums(
            sectors, masks(0),
            lambda a: [psi_ref[a, z * sectors + b] for b in columns],
            [lambda a: jnp.concatenate([left_ref[term, a] for term in terms[a]], axis=0), left],
            [lambda a, slot, b: right_own[terms[a][slot], b], right],
            store,
        )

    @pl.when(jnp.logical_not(is_home()))
    def _():
        lefts, rights = zip(message(direct_b, right_own), message(direct_a, right_other))

        def psi(a):
            return [side[pl.ds((sectors * a + b) * tile, tile)] for b in columns]

        partial_sums(sectors, masks(1), psi, lefts, rights, store)


def far_kernel(*refs):
    direct_a, direct_b, passed_a, passed_b, right_own, right_other = refs[:6]
    near_ref, mask_ref, psi_ref, sent_ref, out_ref = refs[6:]
    z, x, _ = place()
    sectors, tile = out_ref.shape[0], out_ref.shape[-1]
    far_leaves = lax.shift_right_logical(z, 1) == x

    def store_sent(b, a, total):
        sent_ref[b, a] = total.astype(sent_ref.dtype)

    def store_kept(b, a, total):
        out_ref[b, a] = total
        sent_ref[b, a] = near_ref[b, a].astype(sent_ref.dtype)

    def keep(a, b):
        return mask_ref[a, b].astype(jnp.float32) > 0

    def psi(a):
        return [psi_ref[pl.ds((sectors * a + b) * tile, tile)] for b in range(sectors)]

    for leaves, store in ((True, store_sent), (False, store_kept)):
        for at_home, first, second in (
            (True, direct_a, direct_b),
            (False, passed_a, passed_b),
        ):

            @pl.when((is_home() == at_home) & (far_leaves == leaves))
            def _(store=store, first=first, second=second):
                lefts, rights = zip(message(first, right_own), message(second, right_other))
                partial_sums(sectors, keep, psi, lefts, rights, store)


def shards(psi, left_ops, right_ops, term_blocks, left_sizes, right_sizes):
    n = 4
    sectors, tile = psi.shape[0], psi.shape[-1]
    block = functools.partial(jax.ShapeDtypeStruct, dtype=jnp.bfloat16)
    out_shape = (sectors, sectors, tile, tile)
    message_shape = (2 * sectors * tile + ID_ROWS, tile)

    def over_op(array, step):
        return lax.ppermute(array, "op", [(o, o ^ step) for o in range(n)])

    def over_z(array, home_step, other_step):
        pairs = []
        for z in range(n):
            for o in range(n):
                step = home_step if o & 1 == z & 1 else other_step
                pairs.append((z * n + o, (z ^ step) * n + (o & 2) + (z & 1)))
        return lax.ppermute(array, ("blk", "op"), pairs)

    psi_hbm, left_hbm, right_hbm, blocks_hbm = [
        pltpu.with_memory_space_constraint(array, pltpu.HBM)
        for array in (psi, left_ops, right_ops, term_blocks)
    ]
    left_sent, side_sent, far_sent, right_own = pl.pallas_call(
        pack_kernel,
        out_shape=[
            block(message_shape),
            block(message_shape),
            block((sectors * sectors * tile + FAR_PAD, tile)),
            block(right_ops.shape),
        ],
        in_specs=[ANY] * 4,
        out_specs=[VMEM] * 4,
        scratch_shapes=[
            pltpu.SMEM(term_blocks.shape, jnp.int32),
            pltpu.VMEM(left_ops.shape, jnp.bfloat16),
            pltpu.SemaphoreType.DMA((3 + 2 * sectors**2,)),
        ],
        compiler_params=PARAMS,
        name="pack",
    )(blocks_hbm, psi_hbm, left_hbm, right_hbm)
    direct_a = over_z(left_sent, 2, 1)
    direct_b = over_z(left_sent, 1, 2)
    psi_far = over_z(far_sent, 2, 3)
    side = over_z(side_sent, 1, 0)
    passed_a = over_z(direct_a, 1, 0)
    passed_b = over_z(direct_b, 1, 0)
    right_other = over_op(right_own, 1)

    def apply(kernel, name, outs, scalars, operands):
        return pl.pallas_call(
            kernel,
            out_shape=outs,
            in_specs=[SMEM] * len(scalars) + [VMEM] * len(operands),
            out_specs=[VMEM] * len(outs),
            compiler_params=PARAMS,
            cost_estimate=pl.CostEstimate(
                flops=64 * tile**3 * sectors**2, bytes_accessed=2**20, transcendentals=0
            ),
            name=name,
        )(*scalars, *operands)

    sizes = (left_sizes, right_sizes)
    rights = [right_own, right_other]
    total = jax.ShapeDtypeStruct(out_shape, jnp.float32)
    near, far_mask = apply(
        near_kernel, "near", [total, block(out_shape)], sizes + (term_blocks,),
        [psi, left_ops, side, direct_a, direct_b] + rights,
    )
    sent, far = apply(
        far_kernel, "far", [block(out_shape), total], (),
        [direct_a, direct_b, passed_a, passed_b] + rights + [near, far_mask, psi_far],
    )
    arrived = over_op(sent, 2)
    kept = jnp.where(lax.axis_index("blk") // 2 == lax.axis_index("op") // 2, near, far)
    kept = lax.optimization_barrier(kept)
    return (kept + arrived.astype(jnp.float32)).astype(jnp.bfloat16)


def wide_shards(psi, left_ops, right_ops, term_blocks, left_sizes, right_sizes):
    sectors_here = psi.shape[0]
    tile_size = psi.shape[2]
    left_first = lax.axis_index("blk") * sectors_here
    positions = lax.broadcasted_iota(jnp.int32, (tile_size,), 0)
    left_local = lax.dynamic_slice_in_dim(left_sizes, left_first, sectors_here)
    left_keep = positions[None, :] < left_local[:, None]
    right_keep = positions[None, :] < right_sizes[:, None]
    keep_mask = (left_keep[:, None, :, None] & right_keep[None, :, None, :]).astype(jnp.bfloat16)
    masked = psi * keep_mask
    acting_count = left_ops.shape[0] // 2
    order = jnp.argsort(1 - term_blocks, axis=0, stable=True)[:acting_count]
    ids_local = lax.dynamic_slice_in_dim(order, left_first, sectors_here, 1)
    sector_index = lax.broadcasted_iota(jnp.int32, (acting_count, sectors_here), 1)
    picked = left_ops[ids_local, sector_index]
    applied = jnp.einsum(
        "kaim,abmj->kabij", picked, masked, preferred_element_type=jnp.float32
    ).astype(jnp.bfloat16)
    arrived = lax.all_to_all(applied, "blk", split_axis=2, concat_axis=1, tiled=True)
    right_picked = right_ops[order]
    partial_value = jnp.einsum(
        "kabij,kablj->bail", arrived, right_picked, preferred_element_type=jnp.float32
    )
    summed = lax.psum_scatter(
        partial_value.astype(jnp.bfloat16), "op", scatter_dimension=1, tiled=True
    ).astype(jnp.float32)
    row_count = summed.shape[1]
    op_first = lax.axis_index("op") * row_count
    left_share = lax.dynamic_slice_in_dim(left_sizes, op_first, row_count)
    right_local = lax.dynamic_slice_in_dim(right_sizes, left_first, sectors_here)
    rows_keep = positions[None, :] < left_share[:, None]
    cols_keep = positions[None, :] < right_local[:, None]
    out_keep = (cols_keep[:, None, None, :] & rows_keep[None, :, :, None]).astype(jnp.float32)
    return (summed * out_keep).astype(jnp.bfloat16)


def solution(mesh):
    in_specs = (
        P(("parts", "blk"), None, None, None),
        P(("parts", "op"), "blk", None, None),
        P(("parts", "op"), "blk", None, None),
        P(("parts", "op"), None),
        P("parts"),
        P("parts"),
    )
    out_specs = P(("parts", "blk"), "op", None, None)
    nz, no = mesh.shape["blk"], mesh.shape["op"]
    body = shards if nz == no == 4 else wide_shards
    return jax.shard_map(body, mesh=mesh, in_specs=in_specs, out_specs=out_specs, check_vma=False)
```

```python
import functools

import jax
import jax.numpy as jnp
from jax import lax
from jax.experimental import pallas as pl
from jax.experimental.pallas import tpu as pltpu
from jax.sharding import PartitionSpec as P

ANY = pl.BlockSpec(memory_space=pl.ANY)
SMEM = pl.BlockSpec(memory_space=pltpu.SMEM)
VMEM = pl.BlockSpec(memory_space=pltpu.VMEM)
PARAMS = pltpu.CompilerParams(vmem_limit_bytes=32 * 1024 * 1024)
ID_ROWS = 16
FAR_PAD = 32


def acting_terms(blocks_ref, sector):
    first = jnp.int32(0)
    second = jnp.int32(0)
    for term in reversed(range(blocks_ref.shape[0])):
        acts = blocks_ref[term, sector] > 0
        second = jnp.where(acts, first, second)
        first = jnp.where(acts, term, first)
    return first, second


def place():
    op = lax.axis_index("op")
    return lax.axis_index("blk"), lax.shift_right_logical(op, 1), jnp.bitwise_and(op, 1)


def is_home():
    z, _, c = place()
    return c == jnp.bitwise_and(z, 1)


def pack_kernel(blocks_hbm, psi_ref, left_ref, right_ref, *rest):
    left_out, side_out, far_out, right_out, blocks_ref, left_all, sem = rest
    z, _, _ = place()
    sectors, tile = psi_ref.shape[0], psi_ref.shape[-1]
    count = 2 * sectors
    near = jnp.bitwise_xor(z, 1) * sectors
    far = jnp.bitwise_xor(z, jnp.where(is_home(), 2, 3)) * sectors

    def psi_copies(column, out, first):
        return [
            pltpu.make_async_copy(
                psi_ref.at[a, column + b],
                out.at[pl.ds((sectors * a + b) * tile, tile)],
                sem.at[first + sectors * a + b],
            )
            for a in range(sectors)
            for b in range(sectors)
        ]

    table = pltpu.make_async_copy(blocks_hbm, blocks_ref, sem.at[0])
    lefts = pltpu.make_async_copy(left_ref, left_all, sem.at[1])
    others = [pltpu.make_async_copy(right_ref, right_out, sem.at[2])]
    others += psi_copies(far, far_out, 3)
    sides = psi_copies(near, side_out, 3 + sectors * sectors)
    for copy in [table, lefts] + others:
        copy.start()

    @pl.when(is_home())
    def _():
        for copy in sides:
            copy.start()

    far_out[pl.ds(count * tile, FAR_PAD)] = jnp.zeros((FAR_PAD, tile), jnp.bfloat16)
    table.wait()
    row = lax.broadcasted_iota(jnp.int32, (ID_ROWS, tile), 0)
    ids = jnp.zeros((ID_ROWS, tile), jnp.float32)
    picked = []
    for local in range(sectors):
        for term in acting_terms(blocks_ref, z * sectors + local):
            ids = jnp.where(row == len(picked), term.astype(jnp.float32), ids)
            picked.append((term, local))
    for out in (left_out, side_out):
        out[pl.ds(count * tile, ID_ROWS)] = ids.astype(jnp.bfloat16)
    lefts.wait()
    for spot, (term, local) in enumerate(picked):
        left_out[pl.ds(spot * tile, tile)] = left_all[term, local]

    @pl.when(is_home())
    def _():
        for copy in sides:
            copy.wait()

    @pl.when(jnp.logical_not(is_home()))
    def _():
        for spot, (term, local) in enumerate(picked):
            side_out[pl.ds(spot * tile, tile)] = left_all[term, local]

    for copy in others:
        copy.wait()


def keep_mask(z, distance, sizes, a, b, sectors, tile):
    lsize_ref, rsize_ref = sizes
    rows = lax.broadcasted_iota(jnp.int32, (tile, tile), 0)
    lanes = lax.broadcasted_iota(jnp.int32, (tile, tile), 1)
    height = lsize_ref[jnp.bitwise_xor(z, distance) * sectors + a]
    return (rows < height) & (lanes < rsize_ref[z * sectors + b])


def wide_psi(keep, a, blocks):
    cut = []
    for b, block in enumerate(blocks):
        cut.append(jnp.where(keep(a, b), block.astype(jnp.float32), 0.0).astype(jnp.bfloat16))
    return jnp.concatenate(cut, axis=1)


def partial_sums(sectors, keep, psi, lefts, rights, store):
    for a in range(sectors):
        wide = wide_psi(keep, a, psi(a))
        tile = wide.shape[0]
        applied = []
        for left in lefts:
            both = jnp.dot(left(a), wide, preferred_element_type=jnp.float32).astype(jnp.bfloat16)
            applied += [both[:tile], both[tile:]]
        for b in range(sectors):
            picked = [right(a, slot, b) for right in rights for slot in range(2)]
            column = [part[:, b * tile : (b + 1) * tile] for part in applied]
            total = lax.dot_general(
                jnp.concatenate(column, axis=1),
                jnp.concatenate(picked, axis=1),
                (((1,), (1,)), ((), ())),
                preferred_element_type=jnp.float32,
            )
            store(b, a, jnp.where(keep(a, b), total, 0.0))


def message(ref, right_ref):
    terms, sectors, tile = right_ref.shape[0], right_ref.shape[1], right_ref.shape[-1]
    ids = ref[pl.ds(2 * sectors * tile, ID_ROWS)].astype(jnp.float32)

    def left(a):
        return ref[pl.ds(2 * a * tile, 2 * tile)]

    def right(a, slot, b):
        spot = 2 * a + slot
        term = jnp.broadcast_to(ids[spot : spot + 1], (tile, tile))
        block = right_ref[0, b].astype(jnp.float32)
        for t in range(1, terms):
            block = jnp.where(term == t, right_ref[t, b].astype(jnp.float32), block)
        return block.astype(jnp.bfloat16)

    return left, right


def near_kernel(lsize_ref, rsize_ref, blocks_ref, *rest):
    psi_ref, left_ref, side, direct_a, direct_b, right_own, right_other = rest[:7]
    out_ref, mask_ref = rest[7:]
    z, _, _ = place()
    sectors, tile = out_ref.shape[0], out_ref.shape[-1]
    columns = range(sectors)

    def masks(distance):
        return lambda a, b: keep_mask(z, distance, (lsize_ref, rsize_ref), a, b, sectors, tile)

    far = masks(jnp.where(is_home(), 2, 3))
    for a in columns:
        for b in columns:
            mask_ref[a, b] = jnp.where(far(a, b), 1.0, 0.0).astype(mask_ref.dtype)

    def store(b, a, total):
        out_ref[b, a] = total

    @pl.when(is_home())
    def _():
        terms = [acting_terms(blocks_ref, z * sectors + a) for a in columns]
        left, right = message(side, right_other)
        partial_sums(
            sectors, masks(0),
            lambda a: [psi_ref[a, z * sectors + b] for b in columns],
            [lambda a: jnp.concatenate([left_ref[term, a] for term in terms[a]], axis=0), left],
            [lambda a, slot, b: right_own[terms[a][slot], b], right],
            store,
        )

    @pl.when(jnp.logical_not(is_home()))
    def _():
        lefts, rights = zip(message(direct_b, right_own), message(direct_a, right_other))

        def psi(a):
            return [side[pl.ds((sectors * a + b) * tile, tile)] for b in columns]

        partial_sums(sectors, masks(1), psi, lefts, rights, store)


def far_kernel(*refs):
    direct_a, direct_b, passed_a, passed_b, right_own, right_other = refs[:6]
    near_ref, mask_ref, psi_ref, sent_ref, out_ref = refs[6:]
    z, x, _ = place()
    sectors, tile = out_ref.shape[0], out_ref.shape[-1]
    far_leaves = lax.shift_right_logical(z, 1) == x

    def store_sent(b, a, total):
        sent_ref[b, a] = total.astype(sent_ref.dtype)

    def store_kept(b, a, total):
        out_ref[b, a] = total
        sent_ref[b, a] = near_ref[b, a].astype(sent_ref.dtype)

    def keep(a, b):
        return mask_ref[a, b].astype(jnp.float32) > 0

    def psi(a):
        return [psi_ref[pl.ds((sectors * a + b) * tile, tile)] for b in range(sectors)]

    for leaves, store in ((True, store_sent), (False, store_kept)):
        for at_home, first, second in (
            (True, direct_a, direct_b),
            (False, passed_a, passed_b),
        ):

            @pl.when((is_home() == at_home) & (far_leaves == leaves))
            def _(store=store, first=first, second=second):
                lefts, rights = zip(message(first, right_own), message(second, right_other))
                partial_sums(sectors, keep, psi, lefts, rights, store)


def shards(psi, left_ops, right_ops, term_blocks, left_sizes, right_sizes):
    n = 4
    sectors, tile = psi.shape[0], psi.shape[-1]
    block = functools.partial(jax.ShapeDtypeStruct, dtype=jnp.bfloat16)
    out_shape = (sectors, sectors, tile, tile)
    message_shape = (2 * sectors * tile + ID_ROWS, tile)

    def over_op(array, step):
        return lax.ppermute(array, "op", [(o, o ^ step) for o in range(n)])

    def over_z(array, home_step, other_step):
        pairs = []
        for z in range(n):
            for o in range(n):
                step = home_step if o & 1 == z & 1 else other_step
                pairs.append((z * n + o, (z ^ step) * n + (o & 2) + (z & 1)))
        return lax.ppermute(array, ("blk", "op"), pairs)

    psi_hbm, left_hbm, right_hbm, blocks_hbm = [
        pltpu.with_memory_space_constraint(array, pltpu.HBM)
        for array in (psi, left_ops, right_ops, term_blocks)
    ]
    left_sent, side_sent, far_sent, right_own = pl.pallas_call(
        pack_kernel,
        out_shape=[
            block(message_shape),
            block(message_shape),
            block((sectors * sectors * tile + FAR_PAD, tile)),
            block(right_ops.shape),
        ],
        in_specs=[ANY] * 4,
        out_specs=[VMEM] * 4,
        scratch_shapes=[
            pltpu.SMEM(term_blocks.shape, jnp.int32),
            pltpu.VMEM(left_ops.shape, jnp.bfloat16),
            pltpu.SemaphoreType.DMA((3 + 2 * sectors**2,)),
        ],
        compiler_params=PARAMS,
        name="pack",
    )(blocks_hbm, psi_hbm, left_hbm, right_hbm)
    direct_a = over_z(left_sent, 2, 1)
    direct_b = over_z(left_sent, 1, 2)
    psi_far = over_z(far_sent, 2, 3)
    side = over_z(side_sent, 1, 0)
    passed_a = over_z(direct_a, 1, 0)
    passed_b = over_z(direct_b, 1, 0)
    right_other = over_op(right_own, 1)

    def apply(kernel, name, outs, scalars, operands, cost):
        return pl.pallas_call(
            kernel,
            out_shape=outs,
            in_specs=[SMEM] * len(scalars) + [VMEM] * len(operands),
            out_specs=[VMEM] * len(outs),
            compiler_params=PARAMS,
            cost_estimate=pl.CostEstimate(
                flops=64 * cost**3, bytes_accessed=16 * cost**2, transcendentals=0
            ),
            name=name,
        )(*scalars, *operands)

    sizes = (left_sizes, right_sizes)
    rights = [right_own, right_other]
    total = jax.ShapeDtypeStruct(out_shape, jnp.float32)
    near, far_mask = apply(
        near_kernel, "near", [total, block(out_shape)], sizes + (term_blocks,),
        [psi, left_ops, side, direct_a, direct_b] + rights, 96,
    )
    sent, far = apply(
        far_kernel, "far", [block(out_shape), total], (),
        [direct_a, direct_b, passed_a, passed_b] + rights + [near, far_mask, psi_far], 2 * tile,
    )
    arrived = over_op(sent, 2)
    kept = jnp.where(lax.axis_index("blk") // 2 == lax.axis_index("op") // 2, near, far)
    kept = lax.optimization_barrier(kept)
    return (kept + arrived.astype(jnp.float32)).astype(jnp.bfloat16)


def wide_shards(psi, left_ops, right_ops, term_blocks, left_sizes, right_sizes):
    sectors_here = psi.shape[0]
    tile_size = psi.shape[2]
    left_first = lax.axis_index("blk") * sectors_here
    positions = lax.broadcasted_iota(jnp.int32, (tile_size,), 0)
    left_local = lax.dynamic_slice_in_dim(left_sizes, left_first, sectors_here)
    left_keep = positions[None, :] < left_local[:, None]
    right_keep = positions[None, :] < right_sizes[:, None]
    keep_mask = (left_keep[:, None, :, None] & right_keep[None, :, None, :]).astype(jnp.bfloat16)
    masked = psi * keep_mask
    acting_count = left_ops.shape[0] // 2
    order = jnp.argsort(1 - term_blocks, axis=0, stable=True)[:acting_count]
    ids_local = lax.dynamic_slice_in_dim(order, left_first, sectors_here, 1)
    sector_index = lax.broadcasted_iota(jnp.int32, (acting_count, sectors_here), 1)
    picked = left_ops[ids_local, sector_index]
    applied = jnp.einsum(
        "kaim,abmj->kabij", picked, masked, preferred_element_type=jnp.float32
    ).astype(jnp.bfloat16)
    arrived = lax.all_to_all(applied, "blk", split_axis=2, concat_axis=1, tiled=True)
    right_picked = right_ops[order]
    partial_value = jnp.einsum(
        "kabij,kablj->bail", arrived, right_picked, preferred_element_type=jnp.float32
    )
    summed = lax.psum_scatter(
        partial_value.astype(jnp.bfloat16), "op", scatter_dimension=1, tiled=True
    ).astype(jnp.float32)
    row_count = summed.shape[1]
    op_first = lax.axis_index("op") * row_count
    left_share = lax.dynamic_slice_in_dim(left_sizes, op_first, row_count)
    right_local = lax.dynamic_slice_in_dim(right_sizes, left_first, sectors_here)
    rows_keep = positions[None, :] < left_share[:, None]
    cols_keep = positions[None, :] < right_local[:, None]
    out_keep = (cols_keep[:, None, None, :] & rows_keep[None, :, :, None]).astype(jnp.float32)
    return (summed * out_keep).astype(jnp.bfloat16)


def solution(mesh):
    in_specs = (
        P(("parts", "blk"), None, None, None),
        P(("parts", "op"), "blk", None, None),
        P(("parts", "op"), "blk", None, None),
        P(("parts", "op"), None),
        P("parts"),
        P("parts"),
    )
    out_specs = P(("parts", "blk"), "op", None, None)
    nz, no = mesh.shape["blk"], mesh.shape["op"]
    body = shards if nz == no == 4 else wide_shards
    return jax.shard_map(body, mesh=mesh, in_specs=in_specs, out_specs=out_specs, check_vma=False)
```
